128 devices in a mesh: row: 16 (over z, x), col: 8 (over y, core).
Axes of the slice: x: 4, y: 4, z: 4, core: 2. Of those that a mesh axis runs over, the one named last changes fastest.
Arguments:
- iterate: float32 [16, 2048, 2048], P(None, 'row', 'col'), may hold values from -6 to 6
- direction: float32 [16, 2048, 2048], P(None, 'row', 'col'), may hold values from -6 to 6
- conductance: float32 [2048, 2048], P('row', 'col'), may hold values from 0.1 to 10
- ground: int32 [2048, 2048], P('row', 'col'), may hold values 0 or 1
- local_patch: int32 [2048, 2048], P('row', 'col'), may hold values from 0 to 2047, as said below
- tile_patches: int32 [16, 8, 2048], P('row', 'col'), may hold values from 0 to 65535, as said below
- sources: int32 [16], replicated, may hold values from 0 to 65535, as said below
Outputs:
- new_iterate: float32 [16, 2048, 2048], P(None, 'row', 'col')
- new_direction: float32 [16, 2048, 2048], P(None, 'row', 'col')
- migration: float32 [16, 65536], P(None, ('row', 'col'))
The draws below stay inside these ranges and needn't reach their ends.
Inputs may be any that keep to these rules, and one draw needn't show every extreme that they name: `local_patch`: each aligned 4 x 4 block of cells holds one value, and the blocks of one tile take each value once. `tile_patches`: in every tile's list, entries o * 16 to (o + 1) * 16 - 1 are ids from o * 512 to (o + 1) * 512 - 1, where o runs over the devices in row-major order of (row, col); some list holds 0 and some holds the largest id. Each source patch appears in some tile's list; 0 and the largest id are among the sources.
All inputs are finite; a program needn't handle non-finite values. No bound on the sum of `ground` on one device may be relied on, other than what follows from the above.
Results may differ from the reference program's by a relative error of at most 0.0003.
Values sent between devices are 32-bit elements; how exact they have to be, the bound alone decides.
No kernel may reach another device: no remote copies, remote signals or barrier semaphores. Data moves between devices by JAX's collectives and lax.ppermute only.
A program may use at most 128 MiB of HBM per device.

```python
import math
import jax
import jax.numpy as jnp
from jax import lax

K = 16
CR = 128
CC = 256
PB = 4
PATCH_DEV = 512
NR = 2048
NC = 2048
PATCHES = 65536
LP = 2048
N_ROW = 16
N_COL = 8


def tile_lists(key):
    owners = jnp.arange(LP, dtype=jnp.int32) // (LP // (N_ROW * N_COL))
    offsets = jax.random.randint(jax.random.fold_in(key, 11), (N_ROW, N_COL, LP), 0, PATCH_DEV, dtype=jnp.int32)
    offsets = offsets.at[0, 0, 0].set(0).at[0, 0, LP - 1].set(PATCH_DEV - 1)
    return (owners[None, None, :] * PATCH_DEV + offsets).astype(jnp.int32)


def draw_tile_patches(key, part):
    return tile_lists(key)


def draw_sources(key, part):
    listed = tile_lists(key).reshape(-1)
    picks = jax.random.randint(jax.random.fold_in(key, 12), (K,), 0, listed.shape[0], dtype=jnp.int32)
    picks = picks.at[0].set(LP - 1).at[1].set(0)
    return listed[picks].astype(jnp.int32)


def draw_local_patch(key, part):
    tiles = N_ROW * N_COL
    keys = jax.random.split(jax.random.fold_in(key, 13), tiles)
    orders = jax.vmap(lambda single: jax.random.permutation(single, LP))(keys).astype(jnp.int32)
    blocks = orders.reshape(N_ROW, N_COL, CR // PB, CC // PB)
    blocks = jnp.repeat(jnp.repeat(blocks, PB, axis=2), PB, axis=3)
    return blocks.transpose(0, 2, 1, 3).reshape(NR, NC).astype(jnp.int32)


def set_ends(array, stream_key, low, largest):
    extent = array.shape
    place = [jax.random.randint(jax.random.fold_in(stream_key, axis), (), 0, extent[axis]) for axis in range(len(extent))]
    array = array.at[tuple(place)].set(low)
    longest = extent.index(max(extent))
    place[longest] = (place[longest] + 1) % extent[longest]
    return array.at[tuple(place)].set(largest)


def shard_levels(key, dims, cuts, smallest, high):
    def one(position, parts):
        draws = jax.random.uniform(jax.random.fold_in(jax.random.fold_in(key, 6), position), (parts,), jnp.float32, smallest / len(cuts), high / len(cuts))
        return jnp.repeat(jnp.exp(draws), dims[position] // parts).reshape((-1,) + (1,) * (len(dims) - position - 1))

    factor_of = one(*cuts[0])
    for cut in cuts[1:]:
        factor_of = factor_of * one(*cut)
    return factor_of


def noise(own_key, shape, width, limit, pieces=(), kind=jnp.bfloat16):
    gain = shard_levels(own_key, shape, pieces, -0.22, 0.18) if pieces else 1.0
    array = jax.random.normal(own_key, shape, jnp.float32) * width * gain
    return jnp.minimum(jnp.maximum(array, -limit), limit).astype(kind)


def setup_inputs(seed: int = 0) -> dict:
    arg_keys = jax.random.split(jax.random.key(seed), 8)
    iterate = noise(arg_keys[0], (K, NR, NC), 1.0, 6.0, ((1, 16), (2, 8)), jnp.float32)
    direction = noise(arg_keys[1], (K, NR, NC), 1.0, 6.0, ((1, 16), (2, 8)), jnp.float32)
    conductance = jnp.clip(jnp.exp(math.log(10.0) - 4.6051702 * jax.random.uniform(arg_keys[2], (NR, NC), jnp.float32) ** shard_levels(arg_keys[2], (NR, NC), ((0, 16), (1, 8)), -0.2, 0.2)), 0.1, 10.0)
    ground = set_ends((jax.random.randint(arg_keys[3], (NR, NC), 0, 32) < 1).astype(jnp.int32), jax.random.fold_in(arg_keys[3], 1), 0, 1)
    local_patch = draw_local_patch(jax.random.fold_in(arg_keys[7], 71), 0)
    tile_patches = draw_tile_patches(jax.random.fold_in(arg_keys[7], 71), 0)
    sources = draw_sources(jax.random.fold_in(arg_keys[7], 71), 0)
    return dict(iterate=iterate, direction=direction, conductance=conductance, ground=ground, local_patch=local_patch, tile_patches=tile_patches, sources=sources)


SOURCE_AMPS = 4.0
GROUND_LEAK = 2.0
NEIGHBOURS = ((2, 1), (0, 1), (1, 2), (1, 0))

def edge_terms(field_pad, cond_pad, magnitude):
    height = field_pad.shape[1] - 2
    breadth = field_pad.shape[2] - 2
    centre = field_pad[:, 1:-1, 1:-1]
    middle = cond_pad[1:-1, 1:-1]
    summed = jnp.zeros(centre.shape, jnp.float32)
    for row_start, col_start in NEIGHBOURS:
        other = field_pad[:, row_start:row_start + height, col_start:col_start + breadth]
        cond_other = cond_pad[row_start:row_start + height, col_start:col_start + breadth]
        edges = jnp.where(cond_other > 0, 0.5 * (middle + cond_other), 0.0)
        change = centre - other
        if magnitude:
            change = jnp.abs(change)
        summed = summed + edges * change
    return summed

def operate(field_pad, cond_pad, grounded):
    centre = field_pad[:, 1:-1, 1:-1]
    return edge_terms(field_pad, cond_pad, False) + GROUND_LEAK * grounded * centre

def products(left, right):
    return jnp.einsum('kab,lab->kl', left, right, precision=lax.Precision.HIGHEST)

def combine(fields, matrix):
    return jnp.einsum('kab,kl->lab', fields, matrix, precision=lax.Precision.HIGHEST)

def pad_fields(fields):
    return jnp.pad(fields, ((0, 0), (1, 1), (1, 1)))

def reference(iterate, direction, conductance, ground, local_patch, tile_patches, sources):
    row_tile = (jnp.arange(NR, dtype=jnp.int32) // CR)[:, None]
    col_tile = (jnp.arange(NC, dtype=jnp.int32) // CC)[None, :]
    patch_of_cell = tile_patches[row_tile, col_tile, local_patch]
    source = SOURCE_AMPS * (patch_of_cell[None] == sources[:, None, None]).astype(jnp.float32)
    cond_pad = jnp.pad(conductance, 1)
    grounded = ground.astype(jnp.float32)
    residual = source - operate(pad_fields(iterate), cond_pad, grounded)
    image = operate(pad_fields(direction), cond_pad, grounded)
    curvature = products(direction, image)
    projection = products(direction, residual)
    factor = jnp.linalg.cholesky(curvature)
    alpha = jax.scipy.linalg.cho_solve((factor, True), projection)
    new_iterate = iterate + combine(direction, alpha)
    new_residual = residual - combine(image, alpha)
    cross = products(image, new_residual)
    beta = -jax.scipy.linalg.cho_solve((factor, True), cross)
    new_direction = new_residual + combine(direction, beta)
    current = 0.5 * edge_terms(pad_fields(new_iterate), cond_pad, True)
    flat = current.reshape(K, -1).T
    migration = jax.ops.segment_sum(flat, patch_of_cell.reshape(-1), num_segments=PATCHES).T
    return (new_iterate, new_direction, migration)
```

```python
import jax
import jax.numpy as jnp
from jax import lax
from jax.experimental import pallas as pl
from jax.experimental.pallas import tpu as pltpu
from jax.sharding import PartitionSpec as P

K = 16
CR = 128
CC = 256
PATCH_DEV = 512
DEVICES = 128
SLOTS = 16
SOURCE_AMPS = 4.0
GROUND_LEAK = 2.0
AXES = ("row", "col")
F32 = jnp.float32
BF16 = jnp.bfloat16
VMEM_BYTES = 30 * 1024 * 1024


def iota(shape, dim):
    return lax.broadcasted_iota(jnp.int32, shape, dim)


def dot(a, b, ca=1, cb=0, precision=None):
    return lax.dot_general(
        a, b, (((ca,), (cb,)), ((), ())), precision=precision, preferred_element_type=F32
    )


def dot_full(a, b, ca=1, cb=0):
    return dot(a, b, ca, cb, lax.Precision.HIGHEST)


def split(a):
    high = a.astype(BF16)
    return high, (a - high.astype(F32)).astype(BF16)


def one_hot(mask):
    return jnp.where(mask, 1.0, 0.0).astype(BF16)


def call(body, outs, scratch=(), specs=None, flops=0, moved=0):
    return pl.pallas_call(
        body,
        out_shape=outs,
        in_specs=specs,
        scratch_shapes=list(scratch),
        compiler_params=pltpu.CompilerParams(vmem_limit_bytes=VMEM_BYTES),
        cost_estimate=pl.CostEstimate(flops=flops, bytes_accessed=moved, transcendentals=0),
    )


def f32(*shape):
    return jax.ShapeDtypeStruct(shape, F32)


def i32(*shape):
    return jax.ShapeDtypeStruct(shape, jnp.int32)


def strips_body(x_ref, d_ref, c_ref, top_ref, bottom_ref, left_ref, right_ref):
    for row, out in ((0, top_ref), (CR - 1, bottom_ref)):
        out[0:16, :] = x_ref[:, row, :]
        out[16:32, :] = d_ref[:, row, :]
        out[32:40, :] = jnp.broadcast_to(c_ref[row : row + 1, :], (8, CC))
    lane = iota((CR, 128), 1)
    left = jnp.zeros((CR, 128), F32)
    right = jnp.zeros((CR, 128), F32)
    for f in range(33):
        ref = x_ref.at[f] if f < 16 else (d_ref.at[f - 16] if f < 32 else c_ref)
        west = ref[:, 0:128]
        east = ref[:, 128:256]
        left = jnp.where(lane == f, pltpu.roll(west, f, 1) if f else west, left)
        right = jnp.where(lane == f, pltpu.roll(east, f + 1, 1), right)
    left_ref[...] = left
    right_ref[...] = right


def patches_body(lp_ref, tp_ref, poc_ref, slot_ref, lp_s):
    lp_s[0] = lp_ref[:, 0:128]
    lp_s[1] = lp_ref[:, 128:256]
    cell = iota((CC, CC), 0)
    spot = iota((CC, CC), 1)
    acc = jnp.zeros((16, CC), F32)
    for q in range(4):
        every = pl.ds(4 * q, 8, stride=16)
        rows = jnp.concatenate([lp_s[0, every, :], lp_s[1, every, :]], axis=1)
        parts = jnp.concatenate([rows >> 4, rows & 15], axis=0).astype(F32).astype(BF16)
        pick = one_hot(((spot >> 6) == q) & (cell == 4 * (spot & 63)))
        acc = acc + dot(parts, pick)
    slots = (acc[8:16] * 128.0 + acc[0:8]).astype(jnp.int32)
    slot_ref[...] = slots
    listed = jnp.concatenate([tp_ref[e : e + 1, :] for e in range(SLOTS)], axis=1)
    table = jnp.concatenate(
        [jnp.broadcast_to(listed >> 8, (8, 2048)), jnp.broadcast_to(listed & 255, (8, 2048))], axis=0
    )
    table = table.astype(F32).astype(BF16)
    entry = iota((2048, CC), 0)
    highs = []
    lows = []
    for i in range(8):
        found = dot(table, one_hot(entry == slots[i : i + 1, :]))
        highs.append(found[0:1])
        lows.append(found[8:9])
    found = jnp.concatenate(highs + lows, axis=0).astype(BF16)
    for q in range(4):
        spread = dot(found, one_hot(spot == q * 64 + (cell >> 2)), 1, 1)
        ids = (spread[0:8] * 256.0 + spread[8:16]).astype(jnp.int32)
        for r in range(4):
            poc_ref[0, pl.ds(4 * q + r, 8, stride=16), :] = ids[:, 0:128]
            poc_ref[1, pl.ds(4 * q + r, 8, stride=16), :] = ids[:, 128:256]


def edges(c, east_ref, south_ref):
    east = 0.5 * (c + pltpu.roll(c, CC - 1, 1))
    east_ref[...] = jnp.where(iota((CR, CC), 1) == CC - 1, 0.0, east)
    south = 0.5 * (c + pltpu.roll(c, CR - 1, 0))
    south_ref[...] = jnp.where(iota((CR, CC), 0) == CR - 1, 0.0, south)


def products_body(
    src_ref, x_ref, d_ref, c_ref, gr_ref, poc_ref,
    top_ref, bottom_ref, left_ref, right_ref,
    north_ref, south_ref, west_ref, east_ref,
    gram_ref, nf_ref, sf_ref, wf_ref, ef_ref,
    q_s, r_s, ee_s, es_s, leak_s, acc_s,
):
    edges(c_ref[...], ee_s, es_s)
    leak_s[...] = GROUND_LEAK * gr_ref[...].astype(F32)
    for own, far, out in ((top_ref, north_ref, nf_ref), (bottom_ref, south_ref, sf_ref)):
        edge = jnp.where(far[32:33, :] > 0, 0.5 * (own[32:33, :] + far[32:33, :]), 0.0)
        out[...] = edge * (own[0:32, :] - far[0:32, :])
    for own, far, out in ((left_ref, west_ref, wf_ref), (right_ref, east_ref, ef_ref)):
        edge = jnp.where(far[:, 32:33] > 0, 0.5 * (own[:, 32:33] + far[:, 32:33]), 0.0)
        out[...] = edge * (own[...] - far[...])
    lane = iota((CR, 128), 1)

    def operate(v, field):
        flow = ee_s[...] * (v - pltpu.roll(v, CC - 1, 1))
        total = flow - pltpu.roll(flow, 1, 1) + leak_s[...] * v
        flow = es_s[...] * (v - pltpu.roll(v, CR - 1, 0))
        total = total + flow - pltpu.roll(flow, 1, 0)
        west = pltpu.roll(wf_ref[...], lax.rem(128 - field, 128), 1)
        east = pltpu.roll(ef_ref[...], 127 - field, 1)
        return (
            total[:, 0:128] + jnp.where(lane == 0, west, 0.0),
            total[:, 128:256] + jnp.where(lane == 127, east, 0.0),
        )

    def field_step(k, carry):
        first, second = operate(d_ref[k], k + 16)
        q_s[k, :, 0:128] = first
        q_s[k, :, 128:256] = second
        q_s[k, 0:1, :] += nf_ref[pl.ds(k + 16, 1), :]
        q_s[k, CR - 1 : CR, :] += sf_ref[pl.ds(k + 16, 1), :]
        first, second = operate(x_ref[k], k)
        patch = src_ref[k]
        r_s[k, :, 0:128] = jnp.where(poc_ref[0] == patch, SOURCE_AMPS, 0.0) - first
        r_s[k, :, 128:256] = jnp.where(poc_ref[1] == patch, SOURCE_AMPS, 0.0) - second
        r_s[k, 0:1, :] -= nf_ref[pl.ds(k, 1), :]
        r_s[k, CR - 1 : CR, :] -= sf_ref[pl.ds(k, 1), :]
        return carry

    lax.fori_loop(0, K, field_step, 0)
    acc_s[...] = jnp.zeros((256, 256), F32)

    def gram_step(b, carry):
        rows = pl.ds(pl.multiple_of(b * 8, 8), 8)
        dh, dl = split(d_ref[:, rows, :].reshape(128, CC))
        qh, ql = split(q_s[:, rows, :].reshape(128, CC))
        rh, rl = split(r_s[:, rows, :].reshape(128, CC))
        lh = jnp.concatenate([dh, qh], axis=0)
        ll = jnp.concatenate([dl, ql], axis=0)
        gh = jnp.concatenate([qh, rh], axis=0)
        gl = jnp.concatenate([ql, rl], axis=0)
        acc_s[...] += dot(lh, gh, 1, 1) + (dot(lh, gl, 1, 1) + dot(ll, gh, 1, 1))
        return carry

    lax.fori_loop(0, CR // 8, gram_step, 0)
    i = iota((256, 256), 0)
    j = iota((256, 256), 1)
    kept = jnp.where((i & 7) == (j & 7), acc_s[...], 0.0)
    fold_rows = jnp.where(iota((32, 256), 0) == (iota((32, 256), 1) >> 3), 1.0, 0.0)
    fold_lanes = jnp.where((iota((256, 128), 0) >> 3) == iota((256, 128), 1), 1.0, 0.0)
    small = dot_full(dot_full(fold_rows, kept), fold_lanes)
    packed = small[0:8]
    for q in range(1, 4):
        packed = packed + pltpu.roll(small[8 * q : 8 * q + 8], 32 * q, 1)
    gram_ref[...] = packed


def update_body(
    src_ref, gram_ref, x_ref, d_ref, c_ref, gr_ref, poc_ref, slot_ref, ids_ref,
    nf_ref, sf_ref, wf_ref, ef_ref,
    xo_ref, do_ref, msg_ref,
    db_s, cur_s, ee_s, es_s, leak_s, bs_s, wn_s, en_s, nn_s, sn_s,
):
    packed = gram_ref[...]
    small = jnp.concatenate(
        [packed] + [pltpu.roll(packed, 128 - 32 * q, 1) for q in range(1, 4)], axis=0
    )
    lane = iota((16, 128), 1)
    row = iota((16, 128), 0)
    system = jnp.where(lane < 32, small[0:16], pltpu.roll(small[16:32], 32, 1))
    system = jnp.where(lane < 64, system, 0.0)
    for j in range(K):
        pivot = system[j : j + 1, :]
        pivot = pivot / pivot[:, j : j + 1]
        system = jnp.where(row == j, pivot, system - system[:, j : j + 1] * pivot)

    def part(p):
        return jnp.where(lane < 16, pltpu.roll(system, 128 - 16 * p, 1), 0.0)

    alpha = part(1)
    blank = jnp.zeros((112, 128), F32)
    alpha_pad = jnp.concatenate([alpha, blank], axis=0)
    beta = dot_full(part(2), alpha_pad) - part(3)
    beta_pad = jnp.concatenate([beta, blank], axis=0)
    i = iota((128, 128), 0)
    j = iota((128, 128), 1)
    same = (i & 7) == (j & 7)
    repeat_rows = jnp.where((i >> 3) == j, 1.0, 0.0)
    repeat_lanes = jnp.where(i == (j >> 3), 1.0, 0.0)
    mix = []
    for coef in (alpha_pad, beta_pad):
        wide = dot_full(dot_full(repeat_rows, coef, 1, 1), repeat_lanes)
        mix.append(jnp.where(same, wide, 0.0))
    mh, ml = split(jnp.concatenate(mix, axis=0))
    carry_over = jnp.concatenate(
        [jnp.where(row == lane, 1.0, 0.0), alpha, jnp.zeros((96, 128), F32)], axis=0
    )
    wn_s[...] = dot_full(wf_ref[...], carry_over)
    en_s[...] = dot_full(ef_ref[...], carry_over)
    turned = carry_over.T[0:16, 0:32]
    nn_s[...] = dot_full(turned, nf_ref[...])
    sn_s[...] = dot_full(turned, sf_ref[...])
    edges(c_ref[...], ee_s, es_s)
    leak_s[...] = GROUND_LEAK * gr_ref[...].astype(F32)

    def combine_step(b, carry):
        rows = pl.ds(pl.multiple_of(b * 8, 8), 8)
        dh, dl = split(d_ref[:, rows, :].reshape(128, CC))
        mixed = dot(mh, dh) + (dot(mh, dl) + dot(ml, dh))
        xo_ref[:, rows, :] = x_ref[:, rows, :] + mixed[0:128].reshape(16, 8, CC)
        db_s[:, rows, :] = mixed[128:256].reshape(16, 8, CC)
        return carry

    lax.fori_loop(0, CR // 8, combine_step, 0)
    lane2 = iota((CR, 128), 1)

    def field_step(k, carry):
        v = xo_ref[k]
        flow = ee_s[...] * (v - pltpu.roll(v, CC - 1, 1))
        total = flow - pltpu.roll(flow, 1, 1) + leak_s[...] * v
        flow = jnp.abs(flow)
        current = flow + pltpu.roll(flow, 1, 1)
        flow = es_s[...] * (v - pltpu.roll(v, CR - 1, 0))
        total = total + flow - pltpu.roll(flow, 1, 0)
        flow = jnp.abs(flow)
        current = current + flow + pltpu.roll(flow, 1, 0)
        west = jnp.where(lane2 == 0, pltpu.roll(wn_s[...], lax.rem(128 - k, 128), 1), 0.0)
        east = jnp.where(lane2 == 127, pltpu.roll(en_s[...], 127 - k, 1), 0.0)
        north = nn_s[pl.ds(k, 1), :]
        south = sn_s[pl.ds(k, 1), :]
        patch = src_ref[k]
        for half, outer in ((0, west), (1, east)):
            at = slice(128 * half, 128 * half + 128)
            source = jnp.where(poc_ref[half] == patch, SOURCE_AMPS, 0.0)
            do_ref[k, :, at] = (source - (total[:, at] + outer)) + db_s[k, :, at]
            cur_s[half, k] = current[:, at] + jnp.abs(outer)
            cur_s[half, k, 0:1, :] += jnp.abs(north[:, at])
            cur_s[half, k, CR - 1 : CR, :] += jnp.abs(south[:, at])
        do_ref[k, 0:1, :] -= north
        do_ref[k, CR - 1 : CR, :] -= south
        return carry

    lax.fori_loop(0, K, field_step, 0)
    cell = iota((CC, CC), 0)
    spot = iota((CC, CC), 1)
    blocks = jnp.zeros((128, CC), F32)
    for q in range(4):
        halves = []
        for half in range(2):
            rows = [cur_s[half, :, pl.ds(4 * q + r, 8, stride=16), :] for r in range(4)]
            halves.append(((rows[0] + rows[1]) + (rows[2] + rows[3])).reshape(128, 128))
        pooled = jnp.concatenate(halves, axis=1)
        high, low = split(0.5 * pooled)
        spread = one_hot(spot == q * 64 + (cell >> 2))
        blocks = blocks + (dot(high, spread) + dot(low, spread))
    bs_s[0] = blocks[:, 0:128]
    bs_s[1] = blocks[:, 128:256]
    entry = iota((2048, CC), 0)
    sums = jnp.zeros((32, 2048), F32)
    for b in range(8):
        every = pl.ds(b, 16, stride=8)
        high, low = split(jnp.concatenate([bs_s[0, every, :], bs_s[1, every, :]], axis=1))
        place = one_hot(entry == slot_ref[b : b + 1, :])
        sums = sums + dot(jnp.concatenate([high, low], axis=0), place, 1, 1)
    sums = sums[0:16] + sums[16:32]
    stacked = jnp.concatenate([sums[:, 128 * e : 128 * e + 128] for e in range(SLOTS)], axis=0)
    msg_ref[:, 0:256] = stacked.T
    msg_ref[:, 256:384] = ids_ref[...]


def owner_body(msg_ref, out_ref):
    values = msg_ref[:, 0:256].T
    ids = msg_ref[:, 256:384].T
    patch = iota((PATCH_DEV, 256), 0).astype(F32)
    total = jnp.zeros((32, PATCH_DEV), F32)
    for e in range(0, SLOTS, 2):
        pair = jnp.concatenate(
            [values[16 * e : 16 * e + 16], values[16 * e + 16 : 16 * e + 32]], axis=1
        )
        high, low = split(pair)
        at = jnp.concatenate([ids[e : e + 1], ids[e + 1 : e + 2]], axis=1)
        total = total + dot(jnp.concatenate([high, low], axis=0), one_hot(patch == at), 1, 1)
    out_ref[...] = total[0:16] + total[16:32]


def exchange(value, axis, partner):
    return lax.ppermute(value, axis, [(i, partner(i)) for i in range(lax.axis_size(axis))])


def ring_partner(stride, step):
    table = ((1, 0, 3, 2), (3, 2, 1, 0))[step]

    def partner(i):
        at = (i // stride) % 4
        return i + (table[at] - at) * stride

    return partner


def add_up(value):
    value = value + exchange(value, "col", lambda i: i ^ 1)
    for axis, stride in (("col", 2), ("row", 1), ("row", 4)):
        for step in range(2):
            value = value + exchange(value, axis, ring_partner(stride, step))
    return value


def on_device(iterate, direction, conductance, ground, local_patch, tile_patches, sources):
    vmem = pl.BlockSpec(memory_space=pltpu.VMEM)
    smem = pl.BlockSpec(memory_space=pltpu.SMEM)
    listed = tile_patches.reshape(DEVICES, SLOTS)
    owners = jnp.arange(DEVICES, dtype=jnp.int32)[:, None]
    ids = jnp.pad((listed - owners * PATCH_DEV).astype(F32), ((0, 0), (0, 128 - SLOTS)))

    top, bottom, left, right = call(
        strips_body,
        (f32(40, CC), f32(40, CC), f32(CR, 128), f32(CR, 128)),
        specs=[vmem] * 3,
        moved=4_500_000,
    )(iterate, direction, conductance)
    rows = lax.axis_size("row")
    cols = lax.axis_size("col")
    north = lax.ppermute(bottom, "row", [(i, i + 1) for i in range(rows - 1)])
    south = lax.ppermute(top, "row", [(i + 1, i) for i in range(rows - 1)])
    west = lax.ppermute(right, "col", [(i, i + 1) for i in range(cols - 1)])
    east = lax.ppermute(left, "col", [(i + 1, i) for i in range(cols - 1)])

    patch_of_cell, slots = call(
        patches_body,
        (i32(2, CR, 128), i32(8, CC)),
        scratch=[pltpu.VMEM((2, CR, 128), jnp.int32)],
        specs=[vmem] * 2,
        moved=10_000_000,
    )(local_patch, listed.T)

    gram, nf, sf, wf, ef = call(
        products_body,
        (f32(8, 128), f32(32, CC), f32(32, CC), f32(CR, 128), f32(CR, 128)),
        scratch=[
            pltpu.VMEM((K, CR, CC), F32),
            pltpu.VMEM((K, CR, CC), F32),
            pltpu.VMEM((CR, CC), F32),
            pltpu.VMEM((CR, CC), F32),
            pltpu.VMEM((CR, CC), F32),
            pltpu.VMEM((256, 256), F32),
        ],
        specs=[smem] + [vmem] * 13,
        moved=20_000_000,
    )(
        sources, iterate, direction, conductance, ground, patch_of_cell,
        top, bottom, left, right, north, south, west, east,
    )
    gram = add_up(gram)

    new_iterate, new_direction, message = call(
        update_body,
        (f32(K, CR, CC), f32(K, CR, CC), f32(DEVICES, 384)),
        scratch=[
            pltpu.VMEM((K, CR, CC), F32),
            pltpu.VMEM((2, K, CR, 128), F32),
            pltpu.VMEM((CR, CC), F32),
            pltpu.VMEM((CR, CC), F32),
            pltpu.VMEM((CR, CC), F32),
            pltpu.VMEM((2, 128, 128), F32),
            pltpu.VMEM((CR, 128), F32),
            pltpu.VMEM((CR, 128), F32),
            pltpu.VMEM((16, CC), F32),
            pltpu.VMEM((16, CC), F32),
        ],
        specs=[smem] + [vmem] * 12,
        moved=20_000_000,
    )(
        sources, gram, iterate, direction, conductance, ground, patch_of_cell, slots, ids,
        nf, sf, wf, ef,
    )
    received = lax.all_to_all(message, AXES, 0, 0, tiled=True)
    migration = call(owner_body, f32(K, PATCH_DEV), specs=[vmem], moved=1_000_000)(received)
    return new_iterate, new_direction, migration


def solution(mesh):
    in_specs = (
        P(None, "row", "col"),
        P(None, "row", "col"),
        P("row", "col"),
        P("row", "col"),
        P("row", "col"),
        P("row", "col", None),
        P(),
    )
    out_specs = (P(None, "row", "col"), P(None, "row", "col"), P(None, ("row", "col")))
    return jax.shard_map(
        on_device, mesh=mesh, in_specs=in_specs, out_specs=out_specs, check_vma=False
    )
```

```python
import jax
import jax.numpy as jnp
from jax import lax
from jax.experimental import pallas as pl
from jax.experimental.pallas import tpu as pltpu
from jax.sharding import PartitionSpec as P

K = 16
CR = 128
CC = 256
PATCH_DEV = 512
DEVICES = 128
SLOTS = 16
SOURCE_AMPS = 4.0
GROUND_LEAK = 2.0
AXES = ("row", "col")
F32 = jnp.float32
BF16 = jnp.bfloat16
VMEM_BYTES = 20 * 1024 * 1024


def iota(shape, dim):
    return lax.broadcasted_iota(jnp.int32, shape, dim)


def dot(a, b, ca=1, cb=0, precision=None):
    return lax.dot_general(
        a, b, (((ca,), (cb,)), ((), ())), precision=precision, preferred_element_type=F32
    )


def dot_full(a, b, ca=1, cb=0):
    return dot(a, b, ca, cb, lax.Precision.HIGHEST)


def split(a):
    high = a.astype(BF16)
    return high, (a - high.astype(F32)).astype(BF16)


def one_hot(mask):
    return jnp.where(mask, 1.0, 0.0).astype(BF16)


def stack2(high, low):
    return jnp.concatenate([high, low], axis=0)


def call(body, outs, scratch=(), specs=None, places=None, vmem=VMEM_BYTES, flops=0, moved=0):
    return pl.pallas_call(
        body,
        out_shape=outs,
        in_specs=specs,
        **({} if places is None else {"out_specs": places}),
        scratch_shapes=list(scratch),
        compiler_params=pltpu.CompilerParams(vmem_limit_bytes=vmem),
        cost_estimate=pl.CostEstimate(flops=flops, bytes_accessed=moved, transcendentals=0),
    )


def f32(*shape):
    return jax.ShapeDtypeStruct(shape, F32)


def i32(*shape):
    return jax.ShapeDtypeStruct(shape, jnp.int32)


def rows_body(x_ref, d_ref, c_ref, first_ref, second_ref, x_s, d_s, c_s, sems):
    copies = []
    for at, row in ((0, 0), (1, CR - 8)):
        for n, (ref, buf) in enumerate(((x_ref, x_s), (d_ref, d_s))):
            copies.append(pltpu.make_async_copy(ref.at[:, pl.ds(row, 8), :], buf.at[at], sems.at[at, n]))
        copies.append(pltpu.make_async_copy(c_ref.at[pl.ds(row, 8), :], c_s.at[at], sems.at[at, 2]))
    for copy in copies:
        copy.start()
    for copy in copies:
        copy.wait()
    even = jnp.bitwise_and(lax.axis_index("row"), 1) == 0

    def pack(x0, d0, c0, x1, d1, c1, out):
        out[0:16, :] = jnp.where(even, x1, x0)
        out[16:32, :] = jnp.where(even, d1, d0)
        out[32:40, :] = jnp.broadcast_to(jnp.where(even, c1, c0), (8, CC))

    top = (x_s[0, :, 0, :], d_s[0, :, 0, :], c_s[0, 0:1, :])
    bottom = (x_s[1, :, 7, :], d_s[1, :, 7, :], c_s[1, 7:8, :])
    pack(*top, *bottom, first_ref)
    pack(*bottom, *top, second_ref)


def columns_body(x_ref, d_ref, c_ref, after_ref, out_ref, xv_ref, dv_ref):
    lane = iota((CR, 128), 1)
    packed = jnp.zeros((CR, 128), F32)
    for f in range(33):
        ref = x_ref.at[f] if f < 16 else (d_ref.at[f - 16] if f < 32 else c_ref)
        west = ref[:, 0:128]
        east = ref[:, 128:256]
        if f < 32:
            kept = xv_ref if f < 16 else dv_ref
            kept[f % 16, :, 0:128] = west
            kept[f % 16, :, 128:256] = east
        both = pltpu.roll(jnp.where(lane == 127, east, west), 2 * f + 1, 1)
        packed = jnp.where((lane >> 1) == f, both, packed)
    out_ref[...] = packed


def patches_body(lp_ref, tp_ref, after_ref, poc_ref, slot_ref, ids_ref, lp_s):
    lp_s[0] = lp_ref[:, 0:128]
    lp_s[1] = lp_ref[:, 128:256]
    listed = tp_ref[0]
    lane = iota((8, 128), 1)
    row = iota((8, 128), 0)
    for j in range(16):
        chunk = jnp.broadcast_to(listed[:, 128 * j : 128 * j + 128], (8, 128))
        chunk = chunk - (8 * j + row) * PATCH_DEV
        ids_ref[8 * j : 8 * j + 8, :] = jnp.where((lane >> 4) == row, chunk, 0).astype(F32)
    cell = iota((CC, CC), 0)
    spot = iota((CC, CC), 1)
    acc = jnp.zeros((16, CC), F32)
    for q in range(4):
        every = pl.ds(4 * q, 8, stride=16)
        rows = jnp.concatenate([lp_s[0, every, :], lp_s[1, every, :]], axis=1)
        parts = stack2(rows >> 4, rows & 15).astype(F32).astype(BF16)
        pick = one_hot(((spot >> 6) == q) & (cell == 4 * (spot & 63)))
        acc = acc + dot(parts, pick)
    slot_ref[...] = (acc[8:16] * 128.0 + acc[0:8]).astype(jnp.int32)
    place = (acc[0:8] * 16.0 + acc[8:16]).astype(jnp.int32)
    table = stack2(jnp.broadcast_to(listed >> 8, (8, 2048)), jnp.broadcast_to(listed & 255, (8, 2048)))
    table = table.astype(F32).astype(BF16)
    entry = iota((2048, CC), 0)
    highs = []
    lows = []
    for i in range(8):
        found = dot(table, one_hot(entry == place[i : i + 1, :]))
        highs.append(found[0:1])
        lows.append(found[8:9])
    found = jnp.concatenate(highs + lows, axis=0).astype(BF16)
    for q in range(4):
        spread = dot(found, one_hot(spot == q * 64 + (cell >> 2)), 1, 1)
        ids = (spread[0:8] * 256.0 + spread[8:16]).astype(jnp.int32)
        for r in range(4):
            poc_ref[0, pl.ds(4 * q + r, 8, stride=16), :] = ids[:, 0:128]
            poc_ref[1, pl.ds(4 * q + r, 8, stride=16), :] = ids[:, 128:256]


def edges(c, east_ref, south_ref):
    east = 0.5 * (c + pltpu.roll(c, CC - 1, 1))
    east_ref[...] = jnp.where(iota((CR, CC), 1) == CC - 1, 0.0, east)
    south = 0.5 * (c + pltpu.roll(c, CR - 1, 0))
    south_ref[...] = jnp.where(iota((CR, CC), 0) == CR - 1, 0.0, south)


def operate(v, ee_s, es_s, leak_s):
    flow = ee_s[...] * (v - pltpu.roll(v, CC - 1, 1))
    total = flow - pltpu.roll(flow, 1, 1) + leak_s[...] * v
    flow = es_s[...] * (v - pltpu.roll(v, CR - 1, 0))
    return total + flow - pltpu.roll(flow, 1, 0)


def outer_columns(flows, field, lane):
    turned = pltpu.roll(flows, lax.rem(127 - 2 * field + 128, 128), 1)
    return jnp.where(lane == 0, turned, 0.0), jnp.where(lane == 127, turned, 0.0)


def products_body(
    src_ref, x_ref, d_ref, c_ref, gr_ref, poc_ref,
    own_first_ref, own_second_ref, far_first_ref, far_second_ref,
    cols_ref, cols_first_ref, cols_second_ref,
    gram_ref, nf_ref, sf_ref, cf_ref,
    q_s, r_s, ee_s, es_s, leak_s,
):
    edges(c_ref[...], ee_s, es_s)
    leak_s[...] = GROUND_LEAK * gr_ref[...].astype(F32)
    even = jnp.bitwise_and(lax.axis_index("row"), 1) == 0
    first = (own_first_ref[...], far_first_ref[...])
    second = (own_second_ref[...], far_second_ref[...])
    for out, before, after in ((nf_ref, second, first), (sf_ref, first, second)):
        own = jnp.where(even, before[0], after[0])
        far = jnp.where(even, before[1], after[1])
        edge = jnp.where(far[32:33, :] > 0, 0.5 * (own[32:33, :] + far[32:33, :]), 0.0)
        out[...] = edge * (own[0:32, :] - far[0:32, :])
    lane = iota((CR, 128), 1)
    even = jnp.bitwise_and(lax.axis_index("col"), 1) == 0
    next_cols = jnp.where(even, cols_first_ref[...], cols_second_ref[...])
    last_cols = jnp.where(even, cols_second_ref[...], cols_first_ref[...])
    far = jnp.where((lane & 1) == 0, pltpu.roll(next_cols, 127, 1), pltpu.roll(last_cols, 1, 1))
    own = cols_ref[...]
    edge = jnp.where(far > 0, 0.5 * (own + far), 0.0)
    edge = jnp.where((lane & 1) == 0, edge[:, 64:65], edge[:, 65:66])
    cf_ref[...] = jnp.where(lane < 64, edge * (own - far), 0.0)

    def field_step(k, carry):
        total = operate(d_ref[k], ee_s, es_s, leak_s)
        west, east = outer_columns(cf_ref[...], k + 16, lane)
        q_s[k, :, 0:128] = total[:, 0:128] + west
        q_s[k, :, 128:256] = total[:, 128:256] + east
        q_s[k, 0:1, :] += nf_ref[pl.ds(k + 16, 1), :]
        q_s[k, CR - 1 : CR, :] += sf_ref[pl.ds(k + 16, 1), :]
        total = operate(x_ref[k], ee_s, es_s, leak_s)
        west, east = outer_columns(cf_ref[...], k, lane)
        patch = src_ref[k]
        r_s[k, :, 0:128] = jnp.where(poc_ref[0] == patch, SOURCE_AMPS, 0.0) - (total[:, 0:128] + west)
        r_s[k, :, 128:256] = jnp.where(poc_ref[1] == patch, SOURCE_AMPS, 0.0) - (total[:, 128:256] + east)
        r_s[k, 0:1, :] -= nf_ref[pl.ds(k, 1), :]
        r_s[k, CR - 1 : CR, :] -= sf_ref[pl.ds(k, 1), :]
        return carry

    lax.fori_loop(0, K, field_step, 0)
    acc = jnp.zeros((256, 256), F32)
    for b in range(CR // 8):
        rows = slice(8 * b, 8 * b + 8)
        dh, dl = split(d_ref[:, rows, :].reshape(128, CC))
        qh, ql = split(q_s[:, rows, :].reshape(128, CC))
        rh, rl = split(r_s[:, rows, :].reshape(128, CC))
        lh = stack2(dh, qh)
        ll = stack2(dl, ql)
        gh = stack2(qh, rh)
        gl = stack2(ql, rl)
        acc = acc + (dot(lh, gh, 1, 1) + (dot(lh, gl, 1, 1) + dot(ll, gh, 1, 1)))
    i = iota((256, 256), 0)
    j = iota((256, 256), 1)
    kept = jnp.where((i & 7) == (j & 7), acc, 0.0)
    fold_rows = jnp.where(iota((32, 256), 0) == (iota((32, 256), 1) >> 3), 1.0, 0.0)
    fold_lanes = jnp.where((iota((256, 128), 0) >> 3) == iota((256, 128), 1), 1.0, 0.0)
    small = dot_full(dot_full(fold_rows, kept), fold_lanes)
    packed = small[0:8]
    for q in range(1, 4):
        packed = packed + pltpu.roll(small[8 * q : 8 * q + 8], 32 * q, 1)
    for o in range(DEVICES):
        gram_ref[8 * o : 8 * o + 8, :] = packed


def mixer(mix):
    high, low = split(mix)
    return stack2(jnp.concatenate([high, high], axis=1), jnp.concatenate([low, jnp.zeros_like(low)], axis=1))


def mixed(mix, d):
    both = dot(mix, stack2(*split(d)))
    return both[0:128] + both[128:256]


def iterate_body(
    gram_ref, x_ref, d_ref, c_ref, slot_ref, ids_ref, nf_ref, sf_ref, cf_ref,
    out_ref, msg_ref, beta_ref, nn_ref, sn_ref, cn_ref,
    xn_ref, fe_s, cs_s, ee_s, es_s, bs_s, turn_s, sem,
):
    edges(c_ref[...], ee_s, es_s)
    packed = gram_ref[...].reshape(DEVICES, 8, 128).sum(axis=0)
    small = jnp.concatenate(
        [packed] + [pltpu.roll(packed, 128 - 32 * q, 1) for q in range(1, 4)], axis=0
    )
    lane = iota((16, 128), 1)
    row = iota((16, 128), 0)
    system = jnp.where(lane < 32, small[0:16], pltpu.roll(small[16:32], 32, 1))
    system = jnp.where(lane < 64, system, 0.0)
    for j in range(K):
        pivot = system[j : j + 1, :]
        pivot = pivot / pivot[:, j : j + 1]
        system = jnp.where(row == j, pivot, system - system[:, j : j + 1] * pivot)

    def part(p):
        return jnp.where(lane < 16, pltpu.roll(system, 128 - 16 * p, 1), 0.0)

    alpha = part(1)
    blank = jnp.zeros((112, 128), F32)
    alpha_pad = stack2(alpha, blank)
    i = iota((128, 128), 0)
    j = iota((128, 128), 1)
    same = (i & 7) == (j & 7)
    repeat_rows = jnp.where((i >> 3) == j, 1.0, 0.0)
    repeat_lanes = jnp.where(i == (j >> 3), 1.0, 0.0)

    def widen(coef):
        return jnp.where(same, dot_full(dot_full(repeat_rows, coef, 1, 1), repeat_lanes), 0.0)

    mix = mixer(widen(alpha_pad))
    for b in range(CR // 8):
        rows = slice(8 * b, 8 * b + 8)
        step = mixed(mix, d_ref[:, rows, :].reshape(128, CC))
        xn_ref[:, rows, :] = x_ref[:, rows, :] + step.reshape(16, 8, CC)
    leave = pltpu.make_async_copy(xn_ref, out_ref, sem)
    leave.start()
    beta = dot_full(part(2), alpha_pad) - part(3)
    beta_ref[...] = widen(stack2(beta, blank))
    base = jnp.concatenate(
        [jnp.where(row == lane, 1.0, 0.0), alpha, jnp.zeros((96, 128), F32)], axis=0
    )
    pair_rows = jnp.where((i >> 1) == j, 1.0, 0.0)
    pair_lanes = jnp.where(i == (j >> 1), 1.0, 0.0)
    pairs = dot_full(dot_full(pair_rows, base), pair_lanes)
    cn = dot_full(cf_ref[...], jnp.where((i & 1) == (j & 1), pairs, 0.0))
    cn_ref[...] = cn
    turn_s[...] = jnp.abs(cn).T
    turned = base.T[0:16, 0:32]
    nn_ref[...] = dot_full(turned, nf_ref[...])
    sn_ref[...] = dot_full(turned, sf_ref[...])

    def field_step(k, carry):
        v = xn_ref[k]
        flow = jnp.abs(ee_s[...] * (v - pltpu.roll(v, CC - 1, 1)))
        fe_s[0, k] = flow[:, 0:128]
        fe_s[1, k] = flow[:, 128:256]
        flow = jnp.abs(es_s[...] * (v - pltpu.roll(v, CR - 1, 0)))
        flow = flow + pltpu.roll(flow, 1, 0)
        north = jnp.abs(nn_ref[pl.ds(k, 1), :])
        south = jnp.abs(sn_ref[pl.ds(k, 1), :])
        for half in range(2):
            at = slice(128 * half, 128 * half + 128)
            cs_s[half, k] = flow[:, at]
            cs_s[half, k, 0:1, :] += north[:, at]
            cs_s[half, k, CR - 1 : CR, :] += south[:, at]
        return carry

    lax.fori_loop(0, K, field_step, 0)
    cell = iota((CC, CC), 0)
    spot = iota((CC, CC), 1)
    blocks = jnp.zeros((128, CC), F32)
    for q in range(4):

        def pool(ref):
            halves = []
            for half in range(2):
                rows = [ref[half, :, pl.ds(4 * q + r, 8, stride=16), :] for r in range(4)]
                halves.append(((rows[0] + rows[1]) + (rows[2] + rows[3])).reshape(128, 128))
            return split(jnp.concatenate(halves, axis=1))

        here = jnp.where(spot == q * 64 + (cell >> 2), 1.0, 0.0)
        ahead = jnp.where(spot == q * 64 + ((cell + 1) >> 2), 1.0, 0.0)
        ahead = jnp.where((cell & 3) == 3, jnp.where(((cell + 1) >> 2) < 64, ahead, 0.0), ahead)
        along = (here + ahead).astype(BF16)
        here = here.astype(BF16)
        high, low = pool(fe_s)
        blocks = blocks + (dot(high, along) + dot(low, along))
        high, low = pool(cs_s)
        blocks = blocks + (dot(high, here) + dot(low, here))
    bs_s[0] = blocks[:, 0:128]
    bs_s[1] = blocks[:, 128:256]
    outer = jnp.concatenate(
        [turn_s[pl.ds(1, 16, stride=2), :], turn_s[pl.ds(0, 16, stride=2), :]], axis=1
    )
    outer = stack2(*split(outer))
    target = ((cell >> 2) & 3) * 64 + jnp.where(cell < 128, 0, 63)
    band = (cell & 127) >> 4
    entry = iota((2048, CC), 0)
    sums = jnp.zeros((32, 2048), F32)
    for b in range(8):
        every = pl.ds(b, 16, stride=8)
        rim = dot(outer, one_hot((spot == target) & (band == b)))
        rim = rim[0:16] + rim[16:32]
        inner = jnp.concatenate([bs_s[0, every, :], bs_s[1, every, :]], axis=1)
        place = one_hot(entry == slot_ref[b : b + 1, :])
        sums = sums + dot(stack2(*split(0.5 * (inner + rim))), place, 1, 1)
    sums = sums[0:16] + sums[16:32]
    stacked = jnp.concatenate([sums[:, 128 * e : 128 * e + 128] for e in range(SLOTS)], axis=0)
    msg_ref[pl.ds(0, DEVICES, stride=3), :] = stacked[0:128].T
    msg_ref[pl.ds(1, DEVICES, stride=3), :] = stacked[128:256].T
    msg_ref[pl.ds(2, DEVICES, stride=3), :] = ids_ref[...]
    leave.wait()


def direction_body(
    src_ref, xn_ref, d_ref, c_ref, gr_ref, poc_ref, beta_ref, nn_ref, sn_ref, cn_ref,
    do_ref, db_s, ee_s, es_s, leak_s,
):
    edges(c_ref[...], ee_s, es_s)
    leak_s[...] = GROUND_LEAK * gr_ref[...].astype(F32)
    mix = mixer(beta_ref[...])
    for b in range(CR // 8):
        rows = slice(8 * b, 8 * b + 8)
        step = mixed(mix, d_ref[:, rows, :].reshape(128, CC))
        db_s[:, rows, :] = step.reshape(16, 8, CC)
    lane = iota((CR, 128), 1)

    def field_step(k, carry):
        v = xn_ref[k]
        total = operate(v, ee_s, es_s, leak_s)
        outer = outer_columns(cn_ref[...], k, lane)
        patch = src_ref[k]
        for half in range(2):
            at = slice(128 * half, 128 * half + 128)
            source = jnp.where(poc_ref[half] == patch, SOURCE_AMPS, 0.0)
            do_ref[k, :, at] = (source - (total[:, at] + outer[half])) + db_s[k, :, at]
        do_ref[k, 0:1, :] -= nn_ref[pl.ds(k, 1), :]
        do_ref[k, CR - 1 : CR, :] -= sn_ref[pl.ds(k, 1), :]
        return carry

    lax.fori_loop(0, K, field_step, 0)


def owner_body(msg_ref, out_ref, ids_s):
    me = lax.axis_index("row") * lax.axis_size("col") + lax.axis_index("col")
    values = stack2(
        msg_ref[pl.ds(0, DEVICES, stride=3), :].T, msg_ref[pl.ds(1, DEVICES, stride=3), :].T
    )
    ids_s[...] = msg_ref[pl.ds(2, DEVICES, stride=3), :].T
    ids = ids_s[pl.ds(pl.multiple_of(jnp.bitwise_and(me, 7) * 16, 16), 16), :]
    patch = iota((PATCH_DEV, 256), 0).astype(F32)
    total = jnp.zeros((32, PATCH_DEV), F32)
    for e in range(0, SLOTS, 2):
        pair = jnp.concatenate(
            [values[16 * e : 16 * e + 16], values[16 * e + 16 : 16 * e + 32]], axis=1
        )
        at = jnp.concatenate([ids[e : e + 1], ids[e + 1 : e + 2]], axis=1)
        total = total + dot(stack2(*split(pair)), one_hot(patch == at), 1, 1)
    out_ref[...] = total[0:16] + total[16:32]


def neighbours(value, axis, which):
    count = lax.axis_size(axis)
    starts = range(which, count - 1, 2)
    return lax.ppermute(value, axis, [(i, i + 1) for i in starts] + [(i + 1, i) for i in starts])


def on_device(iterate, direction, conductance, ground, local_patch, tile_patches, sources):
    vmem = pl.BlockSpec(memory_space=pltpu.VMEM)
    smem = pl.BlockSpec(memory_space=pltpu.SMEM)
    hbm = pl.BlockSpec(memory_space=pltpu.HBM)
    order = pl.BlockSpec(memory_space=pl.ANY)
    field = pltpu.VMEM((K, CR, CC), F32)
    halves = pltpu.VMEM((2, K, CR, 128), F32)
    plane = pltpu.VMEM((CR, CC), F32)

    first, second = call(
        rows_body,
        (f32(40, CC), f32(40, CC)),
        scratch=[
            pltpu.VMEM((2, K, 8, CC), F32),
            pltpu.VMEM((2, K, 8, CC), F32),
            pltpu.VMEM((2, 8, CC), F32),
            pltpu.SemaphoreType.DMA((2, 3)),
        ],
        specs=[hbm] * 3,
        vmem=60 * 1024 * 1024,
        moved=600_000,
    )(iterate, direction, conductance)
    far_first = neighbours(first, "row", 0)
    far_second = neighbours(second, "row", 1)
    patch_of_cell, slots, ids = call(
        patches_body,
        (i32(2, CR, 128), i32(8, CC), f32(DEVICES, 128)),
        scratch=[pltpu.VMEM((2, CR, 128), jnp.int32)],
        specs=[vmem] * 2 + [order],
        moved=10_000_000,
    )(local_patch, tile_patches, first)

    columns, x_held, d_held = call(
        columns_body,
        (f32(CR, 128), f32(K, CR, CC), f32(K, CR, CC)),
        specs=[vmem] * 3 + [order],
        moved=8_000_000,
    )(iterate, direction, conductance, slots)
    cols_first = neighbours(columns, "col", 0)
    cols_second = neighbours(columns, "col", 1)

    gram, nf, sf, cf = call(
        products_body,
        (f32(8 * DEVICES, 128), f32(32, CC), f32(32, CC), f32(CR, 128)),
        scratch=[field, field, plane, plane, plane],
        specs=[smem] + [vmem] * 12,
        moved=20_000_000,
    )(
        sources, x_held, d_held, conductance, ground, patch_of_cell,
        first, second, far_first, far_second, columns, cols_first, cols_second,
    )
    gram = lax.all_to_all(gram, AXES, 0, 0, tiled=True)

    new_iterate, message, beta, nn, sn, cn = call(
        iterate_body,
        (f32(K, CR, CC), f32(DEVICES * 3, 128), f32(128, 128), f32(16, CC), f32(16, CC), f32(CR, 128)),
        scratch=[
            field,
            halves,
            halves,
            plane,
            plane,
            pltpu.VMEM((2, 128, 128), F32),
            pltpu.VMEM((128, 128), F32),
            pltpu.SemaphoreType.DMA(()),
        ],
        specs=[vmem] * 9,
        places=(hbm,) + (vmem,) * 5,
        moved=20_000_000,
    )(gram, x_held, d_held, conductance, slots, ids, nf, sf, cf)
    received = lax.all_to_all(message.reshape(DEVICES, 1, 384), AXES, 0, 0, tiled=True)
    new_direction = call(
        direction_body,
        f32(K, CR, CC),
        scratch=[field, plane, plane, plane],
        specs=[smem] + [vmem] * 9,
        moved=20_000_000,
    )(sources, new_iterate, direction, conductance, ground, patch_of_cell, beta, nn, sn, cn)
    migration = call(
        owner_body,
        f32(K, PATCH_DEV),
        scratch=[pltpu.VMEM((128, 128), F32)],
        specs=[vmem],
        moved=1_000_000,
    )(received.reshape(DEVICES * 3, 128))
    return new_iterate, new_direction, migration


def solution(mesh):
    in_specs = (
        P(None, "row", "col"),
        P(None, "row", "col"),
        P("row", "col"),
        P("row", "col"),
        P("row", "col"),
        P("row", "col", None),
        P(),
    )
    out_specs = (P(None, "row", "col"), P(None, "row", "col"), P(None, ("row", "col")))
    return jax.shard_map(
        on_device, mesh=mesh, in_specs=in_specs, out_specs=out_specs, check_vma=False
    )
```

```python
import jax
import jax.numpy as jnp
from jax import lax
from jax.experimental import pallas as pl
from jax.experimental.pallas import tpu as pltpu
from jax.sharding import PartitionSpec as P

K = 16
CR = 128
CC = 256
PATCH_DEV = 512
DEVICES = 128
SLOTS = 16
SOURCE_AMPS = 4.0
GROUND_LEAK = 2.0
AXES = ("row", "col")
F32 = jnp.float32
BF16 = jnp.bfloat16
VMEM_BYTES = 20 * 1024 * 1024


def iota(shape, dim):
    return lax.broadcasted_iota(jnp.int32, shape, dim)


def dot(a, b, ca=1, cb=0, precision=None):
    return lax.dot_general(
        a, b, (((ca,), (cb,)), ((), ())), precision=precision, preferred_element_type=F32
    )


def dot_full(a, b, ca=1, cb=0):
    return dot(a, b, ca, cb, lax.Precision.HIGHEST)


def split(a):
    high = a.astype(BF16)
    return high, (a - high.astype(F32)).astype(BF16)


def one_hot(mask):
    return jnp.where(mask, 1.0, 0.0).astype(BF16)


def stack2(high, low):
    return jnp.concatenate([high, low], axis=0)


def call(body, outs, scratch=(), specs=None, places=None, vmem=VMEM_BYTES, flops=0, moved=0):
    return pl.pallas_call(
        body,
        out_shape=outs,
        in_specs=specs,
        **({} if places is None else {"out_specs": places}),
        scratch_shapes=list(scratch),
        compiler_params=pltpu.CompilerParams(vmem_limit_bytes=vmem),
        cost_estimate=pl.CostEstimate(flops=flops, bytes_accessed=moved, transcendentals=0),
    )


def f32(*shape):
    return jax.ShapeDtypeStruct(shape, F32)


def i32(*shape):
    return jax.ShapeDtypeStruct(shape, jnp.int32)


def front_body(x_ref, d_ref, c_ref, first_ref, second_ref, cols_ref, xv_ref, dv_ref, c_s, sems):
    pairs = [(x_ref.at[k], xv_ref.at[k]) for k in range(K)]
    pairs += [(d_ref.at[k], dv_ref.at[k]) for k in range(K)]
    pairs += [(c_ref, c_s)]
    copies = [pltpu.make_async_copy(*pair, sems.at[f]) for f, pair in enumerate(pairs)]
    for copy in copies:
        copy.start()
    even = jnp.bitwise_and(lax.axis_index("row"), 1) == 0
    lane = iota((CR, 128), 1)
    packed = jnp.zeros((CR, 128), F32)
    for f, copy in enumerate(copies):
        copy.wait()
        ref = pairs[f][1]
        top = ref[0:1, :]
        bottom = ref[CR - 1 : CR, :]
        first_ref[f : f + 1, :] = jnp.where(even, bottom, top)
        second_ref[f : f + 1, :] = jnp.where(even, top, bottom)
        both = pltpu.roll(jnp.where(lane == 127, ref[:, 128:256], ref[:, 0:128]), 2 * f + 1, 1)
        packed = jnp.where((lane >> 1) == f, both, packed)
    for ref in (first_ref, second_ref):
        ref[33:40, :] = jnp.zeros((7, CC), F32)
    cols_ref[...] = packed


def patches_body(lp_ref, tp_ref, after_ref, poc_ref, slot_ref, ids_ref, lp_s):
    lp_s[0] = lp_ref[:, 0:128]
    lp_s[1] = lp_ref[:, 128:256]
    listed = tp_ref[0]
    lane = iota((8, 128), 1)
    row = iota((8, 128), 0)
    for j in range(16):
        chunk = jnp.broadcast_to(listed[:, 128 * j : 128 * j + 128], (8, 128))
        chunk = chunk - (8 * j + row) * PATCH_DEV
        ids_ref[8 * j : 8 * j + 8, :] = jnp.where((lane >> 4) == row, chunk, 0).astype(F32)
    cell = iota((CC, CC), 0)
    spot = iota((CC, CC), 1)
    acc = jnp.zeros((16, CC), F32)
    for q in range(4):
        every = pl.ds(4 * q, 8, stride=16)
        rows = jnp.concatenate([lp_s[0, every, :], lp_s[1, every, :]], axis=1)
        parts = stack2(rows >> 4, rows & 15).astype(F32).astype(BF16)
        pick = one_hot(((spot >> 6) == q) & (cell == 4 * (spot & 63)))
        acc = acc + dot(parts, pick)
    slot_ref[...] = (acc[8:16] * 128.0 + acc[0:8]).astype(jnp.int32)
    place = (acc[0:8] * 16.0 + acc[8:16]).astype(jnp.int32)
    table = stack2(jnp.broadcast_to(listed >> 8, (8, 2048)), jnp.broadcast_to(listed & 255, (8, 2048)))
    table = table.astype(F32).astype(BF16)
    entry = iota((2048, CC), 0)
    highs = []
    lows = []
    for i in range(8):
        found = dot(table, one_hot(entry == place[i : i + 1, :]))
        highs.append(found[0:1])
        lows.append(found[8:9])
    found = jnp.concatenate(highs + lows, axis=0).astype(BF16)
    for q in range(4):
        spread = dot(found, one_hot(spot == q * 64 + (cell >> 2)), 1, 1)
        ids = (spread[0:8] * 256.0 + spread[8:16]).astype(jnp.int32)
        for r in range(4):
            poc_ref[0, pl.ds(4 * q + r, 8, stride=16), :] = ids[:, 0:128]
            poc_ref[1, pl.ds(4 * q + r, 8, stride=16), :] = ids[:, 128:256]


def edges(c, east_ref, south_ref):
    east = 0.5 * (c + pltpu.roll(c, CC - 1, 1))
    east_ref[...] = jnp.where(iota((CR, CC), 1) == CC - 1, 0.0, east)
    south = 0.5 * (c + pltpu.roll(c, CR - 1, 0))
    south_ref[...] = jnp.where(iota((CR, CC), 0) == CR - 1, 0.0, south)


def turn_columns(flows, field):
    return pltpu.roll(flows, lax.rem(127 - 2 * field + 128, 128), 1)


def operate(v, outer, ee_s, es_s, leak_s):
    lane = iota((CR, 128), 1)
    a = v[:, 0:128]
    b = v[:, 128:256]
    after = pltpu.roll(b, 127, 1)
    flow_a = ee_s[:, 0:128] * (a - jnp.where(lane == 127, after, pltpu.roll(a, 127, 1)))
    flow_b = jnp.where(lane == 127, outer, ee_s[:, 128:256] * (b - after))
    before = pltpu.roll(flow_a, 1, 1)
    total_a = flow_a - jnp.where(lane == 0, -outer, before)
    total_b = flow_b - jnp.where(lane == 0, before, pltpu.roll(flow_b, 1, 1))
    flow = es_s[...] * (v - pltpu.roll(v, CR - 1, 0))
    down = (flow - pltpu.roll(flow, 1, 0)) + leak_s[...] * v
    return total_a + down[:, 0:128], total_b + down[:, 128:256]


def products_body(
    src_ref, x_ref, d_ref, c_ref, gr_ref, poc_ref,
    own_first_ref, own_second_ref, far_first_ref, far_second_ref,
    cols_ref, cols_first_ref, cols_second_ref,
    gram_ref, nf_ref, sf_ref, cf_ref,
    q_s, r_s, ee_s, es_s, leak_s,
):
    edges(c_ref[...], ee_s, es_s)
    leak_s[...] = GROUND_LEAK * gr_ref[...].astype(F32)
    even = jnp.bitwise_and(lax.axis_index("row"), 1) == 0
    first = (own_first_ref[...], far_first_ref[...])
    second = (own_second_ref[...], far_second_ref[...])
    for out, before, after in ((nf_ref, second, first), (sf_ref, first, second)):
        own = jnp.where(even, before[0], after[0])
        far = jnp.where(even, before[1], after[1])
        edge = jnp.where(far[32:33, :] > 0, 0.5 * (own[32:33, :] + far[32:33, :]), 0.0)
        out[...] = edge * (own[0:32, :] - far[0:32, :])
    lane = iota((CR, 128), 1)
    even = jnp.bitwise_and(lax.axis_index("col"), 1) == 0
    next_cols = jnp.where(even, cols_first_ref[...], cols_second_ref[...])
    last_cols = jnp.where(even, cols_second_ref[...], cols_first_ref[...])
    far = jnp.where((lane & 1) == 0, pltpu.roll(next_cols, 127, 1), pltpu.roll(last_cols, 1, 1))
    own = cols_ref[...]
    edge = jnp.where(far > 0, 0.5 * (own + far), 0.0)
    edge = jnp.where((lane & 1) == 0, edge[:, 64:65], edge[:, 65:66])
    cf_ref[...] = jnp.where(lane < 64, edge * (own - far), 0.0)

    def field_step(k, carry):
        image = operate(d_ref[k], turn_columns(cf_ref[...], k + 16), ee_s, es_s, leak_s)
        part = operate(x_ref[k], turn_columns(cf_ref[...], k), ee_s, es_s, leak_s)
        patch = src_ref[k]
        for half in range(2):
            at = slice(128 * half, 128 * half + 128)
            q_s[k, :, at] = image[half]
            r_s[k, :, at] = jnp.where(poc_ref[half] == patch, SOURCE_AMPS, 0.0) - part[half]
        q_s[k, 0:1, :] += nf_ref[pl.ds(k + 16, 1), :]
        q_s[k, CR - 1 : CR, :] += sf_ref[pl.ds(k + 16, 1), :]
        r_s[k, 0:1, :] -= nf_ref[pl.ds(k, 1), :]
        r_s[k, CR - 1 : CR, :] -= sf_ref[pl.ds(k, 1), :]
        return carry

    lax.fori_loop(0, K, field_step, 0)
    acc = jnp.zeros((256, 256), F32)
    for b in range(CR // 8):
        rows = slice(8 * b, 8 * b + 8)
        dh, dl = split(d_ref[:, rows, :].reshape(128, CC))
        qh, ql = split(q_s[:, rows, :].reshape(128, CC))
        rh, rl = split(r_s[:, rows, :].reshape(128, CC))
        lh = stack2(dh, qh)
        ll = stack2(dl, ql)
        gh = stack2(qh, rh)
        gl = stack2(ql, rl)
        acc = acc + (dot(lh, gh, 1, 1) + (dot(lh, gl, 1, 1) + dot(ll, gh, 1, 1)))
    i = iota((256, 256), 0)
    j = iota((256, 256), 1)
    kept = jnp.where((i & 7) == (j & 7), acc, 0.0)
    fold_rows = jnp.where(iota((32, 256), 0) == (iota((32, 256), 1) >> 3), 1.0, 0.0)
    fold_lanes = jnp.where((iota((256, 128), 0) >> 3) == iota((256, 128), 1), 1.0, 0.0)
    small = dot_full(dot_full(fold_rows, kept), fold_lanes)
    packed = small[0:8]
    for q in range(1, 4):
        packed = packed + pltpu.roll(small[8 * q : 8 * q + 8], 32 * q, 1)
    for o in range(DEVICES):
        gram_ref[8 * o : 8 * o + 8, :] = packed


def mixer(mix):
    high, low = split(mix)
    return stack2(jnp.concatenate([high, high], axis=1), jnp.concatenate([low, jnp.zeros_like(low)], axis=1))


def mixed(mix, d):
    both = dot(mix, stack2(*split(d)))
    return both[0:128] + both[128:256]


def iterate_body(
    gram_ref, x_ref, d_ref, c_ref, slot_ref, ids_ref, nf_ref, sf_ref, cf_ref,
    out_ref, msg_ref, beta_ref, nn_ref, sn_ref, cn_ref,
    xn_ref, cur_s, ee_s, es_s, turn_s, sem,
):
    edges(c_ref[...], ee_s, es_s)
    packed = gram_ref[...].reshape(DEVICES, 8, 128).sum(axis=0)
    small = jnp.concatenate(
        [packed] + [pltpu.roll(packed, 128 - 32 * q, 1) for q in range(1, 4)], axis=0
    )
    lane = iota((16, 128), 1)
    row = iota((16, 128), 0)
    system = jnp.where(lane < 32, small[0:16], pltpu.roll(small[16:32], 32, 1))
    system = jnp.where(lane < 64, system, 0.0)
    for j in range(K):
        pivot = system[j : j + 1, :]
        pivot = pivot / pivot[:, j : j + 1]
        system = jnp.where(row == j, pivot, system - system[:, j : j + 1] * pivot)

    def part(p):
        return jnp.where(lane < 16, pltpu.roll(system, 128 - 16 * p, 1), 0.0)

    alpha = part(1)
    blank = jnp.zeros((112, 128), F32)
    alpha_pad = stack2(alpha, blank)
    i = iota((128, 128), 0)
    j = iota((128, 128), 1)
    same = (i & 7) == (j & 7)
    repeat_rows = jnp.where((i >> 3) == j, 1.0, 0.0)
    repeat_lanes = jnp.where(i == (j >> 3), 1.0, 0.0)

    def widen(coef):
        return jnp.where(same, dot_full(dot_full(repeat_rows, coef, 1, 1), repeat_lanes), 0.0)

    mix = mixer(widen(alpha_pad))
    for b in range(CR // 8):
        rows = slice(8 * b, 8 * b + 8)
        step = mixed(mix, d_ref[:, rows, :].reshape(128, CC))
        xn_ref[:, rows, :] = x_ref[:, rows, :] + step.reshape(16, 8, CC)
    leave = pltpu.make_async_copy(xn_ref, out_ref, sem)
    leave.start()
    beta = dot_full(part(2), alpha_pad) - part(3)
    beta_ref[...] = widen(stack2(beta, blank))
    base = jnp.concatenate(
        [jnp.where(row == lane, 1.0, 0.0), alpha, jnp.zeros((96, 128), F32)], axis=0
    )
    pair_rows = jnp.where((i >> 1) == j, 1.0, 0.0)
    pair_lanes = jnp.where(i == (j >> 1), 1.0, 0.0)
    pairs = dot_full(dot_full(pair_rows, base), pair_lanes)
    cn = dot_full(cf_ref[...], jnp.where((i & 1) == (j & 1), pairs, 0.0))
    cn_ref[...] = cn
    turn_s[...] = jnp.abs(cn).T
    turned = base.T[0:16, 0:32]
    nn_ref[...] = dot_full(turned, nf_ref[...])
    sn_ref[...] = dot_full(turned, sf_ref[...])

    def field_step(k, carry):
        v = xn_ref[k]
        flow = jnp.abs(ee_s[...] * (v - pltpu.roll(v, CC - 1, 1)))
        total = flow + pltpu.roll(flow, 1, 1)
        flow = jnp.abs(es_s[...] * (v - pltpu.roll(v, CR - 1, 0)))
        cur_s[k] = total + (flow + pltpu.roll(flow, 1, 0))
        cur_s[k, 0:1, :] += jnp.abs(nn_ref[pl.ds(k, 1), :])
        cur_s[k, CR - 1 : CR, :] += jnp.abs(sn_ref[pl.ds(k, 1), :])
        return carry

    lax.fori_loop(0, K, field_step, 0)
    take = iota((32, 256), 0)
    given = iota((32, 256), 1) & 127
    rows_of = one_hot(((given >> 3) == (take & 15)) & (((given >> 2) & 1) == (take >> 4)))
    strips = []
    for b in range(CR // 8):
        high, low = split(cur_s[:, 8 * b : 8 * b + 8, :].reshape(128, CC))
        both = dot(rows_of, stack2(high, low))
        strips += [both[0:16], both[16:32]]
    cell = iota((CC, CC), 0)
    spot = iota((CC, CC), 1)
    blocks = jnp.zeros((128, CC), F32)
    for q in range(4):
        high, low = split(jnp.concatenate([strips[4 * i + q] for i in range(8)], axis=0))
        spread = one_hot(spot == q * 64 + (cell >> 2))
        blocks = blocks + (dot(high, spread) + dot(low, spread))
    outer = jnp.concatenate(
        [turn_s[pl.ds(1, 16, stride=2), :], turn_s[pl.ds(0, 16, stride=2), :]], axis=1
    )
    outer = stack2(*split(outer))
    target = ((cell >> 2) & 3) * 64 + jnp.where(cell < 128, 0, 63)
    band = (cell & 127) >> 4
    owner = iota((128, CC), 0)
    stacked = jnp.zeros((256, 128), F32)
    for b in range(8):
        rim = dot(outer, one_hot((spot == target) & (band == b)))
        inner = 0.5 * (blocks[16 * b : 16 * b + 16] + (rim[0:16] + rim[16:32]))
        slot = slot_ref[b : b + 1, :]
        entry = jnp.broadcast_to(slot >> 7, (16, CC))
        spread = jnp.concatenate([jnp.where(entry == e, inner, 0.0) for e in range(SLOTS)], axis=0)
        high, low = split(spread)
        place = one_hot(owner == (slot & 127))
        stacked = stacked + (dot(high, place, 1, 1) + dot(low, place, 1, 1))
    msg_ref[pl.ds(0, DEVICES, stride=3), :] = stacked[0:128].T
    msg_ref[pl.ds(1, DEVICES, stride=3), :] = stacked[128:256].T
    msg_ref[pl.ds(2, DEVICES, stride=3), :] = ids_ref[...]
    leave.wait()


def direction_body(
    src_ref, xn_ref, d_ref, c_ref, gr_ref, poc_ref, beta_ref, nn_ref, sn_ref, cn_ref,
    do_ref, db_s, ee_s, es_s, leak_s,
):
    edges(c_ref[...], ee_s, es_s)
    leak_s[...] = GROUND_LEAK * gr_ref[...].astype(F32)
    mix = mixer(beta_ref[...])
    for b in range(CR // 8):
        rows = slice(8 * b, 8 * b + 8)
        step = mixed(mix, d_ref[:, rows, :].reshape(128, CC))
        db_s[:, rows, :] = step.reshape(16, 8, CC)

    def field_step(k, carry):
        total = operate(xn_ref[k], turn_columns(cn_ref[...], k), ee_s, es_s, leak_s)
        patch = src_ref[k]
        for half in range(2):
            at = slice(128 * half, 128 * half + 128)
            source = jnp.where(poc_ref[half] == patch, SOURCE_AMPS, 0.0)
            do_ref[k, :, at] = (source - total[half]) + db_s[k, :, at]
        do_ref[k, 0:1, :] -= nn_ref[pl.ds(k, 1), :]
        do_ref[k, CR - 1 : CR, :] -= sn_ref[pl.ds(k, 1), :]
        return carry

    lax.fori_loop(0, K, field_step, 0)


def owner_body(msg_ref, out_ref, ids_s):
    me = lax.axis_index("row") * lax.axis_size("col") + lax.axis_index("col")
    values = stack2(
        msg_ref[pl.ds(0, DEVICES, stride=3), :].T, msg_ref[pl.ds(1, DEVICES, stride=3), :].T
    )
    ids_s[...] = msg_ref[pl.ds(2, DEVICES, stride=3), :].T
    ids = ids_s[pl.ds(pl.multiple_of(jnp.bitwise_and(me, 7) * 16, 16), 16), :]
    patch = iota((128, 256), 0)
    total = jnp.zeros((64, 128), F32)
    for e in range(0, SLOTS, 2):
        pair = jnp.concatenate(
            [values[16 * e : 16 * e + 16], values[16 * e + 16 : 16 * e + 32]], axis=1
        )
        at = jnp.concatenate([ids[e : e + 1], ids[e + 1 : e + 2]], axis=1).astype(jnp.int32)
        group = jnp.broadcast_to(at >> 7, (16, 256))
        spread = jnp.concatenate([jnp.where(group == g, pair, 0.0) for g in range(4)], axis=0)
        high, low = split(spread)
        place = one_hot(patch == (at & 127))
        total = total + (dot(high, place, 1, 1) + dot(low, place, 1, 1))
    for g in range(4):
        out_ref[:, 128 * g : 128 * g + 128] = total[16 * g : 16 * g + 16]


def neighbours(value, axis, which):
    count = lax.axis_size(axis)
    starts = range(which, count - 1, 2)
    return lax.ppermute(value, axis, [(i, i + 1) for i in starts] + [(i + 1, i) for i in starts])


def on_device(iterate, direction, conductance, ground, local_patch, tile_patches, sources):
    vmem = pl.BlockSpec(memory_space=pltpu.VMEM)
    smem = pl.BlockSpec(memory_space=pltpu.SMEM)
    hbm = pl.BlockSpec(memory_space=pltpu.HBM)
    order = pl.BlockSpec(memory_space=pl.ANY)
    field = pltpu.VMEM((K, CR, CC), F32)
    plane = pltpu.VMEM((CR, CC), F32)

    first, second, columns, x_held, d_held = call(
        front_body,
        (
            pltpu.VMEM((40, CC), F32),
            pltpu.VMEM((40, CC), F32),
            pltpu.VMEM((CR, 128), F32),
            field,
            field,
        ),
        scratch=[plane, pltpu.SemaphoreType.DMA((33,))],
        specs=[hbm] * 3,
        places=(vmem,) * 5,
        moved=8_000_000,
    )(*[pltpu.with_memory_space_constraint(a, pltpu.HBM) for a in (iterate, direction, conductance)])
    far_second = neighbours(second, "row", 1)
    cols_second = neighbours(columns, "col", 1)
    far_first = neighbours(first, "row", 0)
    cols_first = neighbours(columns, "col", 0)

    patch_of_cell, slots, ids = call(
        patches_body,
        (i32(2, CR, 128), i32(8, CC), f32(DEVICES, 128)),
        scratch=[pltpu.VMEM((2, CR, 128), jnp.int32)],
        specs=[vmem] * 2 + [order],
        moved=10_000_000,
    )(local_patch, tile_patches, columns)

    gram, nf, sf, cf = call(
        products_body,
        (f32(8 * DEVICES, 128), f32(32, CC), f32(32, CC), f32(CR, 128)),
        scratch=[field, field, plane, plane, plane],
        specs=[smem] + [vmem] * 12,
        moved=20_000_000,
    )(
        sources, x_held, d_held, conductance, ground, patch_of_cell,
        first, second, far_first, far_second, columns, cols_first, cols_second,
    )
    gram = lax.all_to_all(gram, AXES, 0, 0, tiled=True)

    new_iterate, message, beta, nn, sn, cn = call(
        iterate_body,
        (f32(K, CR, CC), f32(DEVICES * 3, 128), f32(128, 128), f32(16, CC), f32(16, CC), f32(CR, 128)),
        scratch=[
            field,
            field,
            plane,
            plane,
            pltpu.VMEM((128, 128), F32),
            pltpu.SemaphoreType.DMA(()),
        ],
        specs=[vmem] * 9,
        places=(hbm,) + (vmem,) * 5,
        moved=20_000_000,
    )(gram, x_held, d_held, conductance, slots, ids, nf, sf, cf)
    received = lax.all_to_all(message.reshape(DEVICES, 1, 384), AXES, 0, 0, tiled=True)
    new_direction = call(
        direction_body,
        f32(K, CR, CC),
        scratch=[field, plane, plane, plane],
        specs=[smem] + [vmem] * 9,
        moved=20_000_000,
    )(sources, new_iterate, direction, conductance, ground, patch_of_cell, beta, nn, sn, cn)
    migration = call(
        owner_body,
        f32(K, PATCH_DEV),
        scratch=[pltpu.VMEM((128, 128), F32)],
        specs=[vmem],
        moved=1_000_000,
    )(received.reshape(DEVICES * 3, 128))
    return new_iterate, new_direction, migration


def solution(mesh):
    in_specs = (
        P(None, "row", "col"),
        P(None, "row", "col"),
        P("row", "col"),
        P("row", "col"),
        P("row", "col"),
        P("row", "col", None),
        P(),
    )
    out_specs = (P(None, "row", "col"), P(None, "row", "col"), P(None, ("row", "col")))
    return jax.shard_map(
        on_device, mesh=mesh, in_specs=in_specs, out_specs=out_specs, check_vma=False
    )
```

```python
import jax
import jax.numpy as jnp
from jax import lax
from jax.experimental import pallas as pl
from jax.experimental.pallas import tpu as pltpu
from jax.sharding import PartitionSpec as P

K = 16
CR = 128
CC = 256
PATCH_DEV = 512
DEVICES = 128
SLOTS = 16
SOURCE_AMPS = 4.0
GROUND_LEAK = 2.0
AXES = ("row", "col")
F32 = jnp.float32
BF16 = jnp.bfloat16
VMEM_BYTES = 20 * 1024 * 1024


def iota(shape, dim):
    return lax.broadcasted_iota(jnp.int32, shape, dim)


def dot(a, b, ca=1, cb=0, precision=None):
    return lax.dot_general(
        a, b, (((ca,), (cb,)), ((), ())), precision=precision, preferred_element_type=F32
    )


def dot_full(a, b, ca=1, cb=0):
    return dot(a, b, ca, cb, lax.Precision.HIGHEST)


def split(a):
    high = a.astype(BF16)
    return high, (a - high.astype(F32)).astype(BF16)


def one_hot(mask):
    return jnp.where(mask, 1.0, 0.0).astype(BF16)


def stack2(high, low):
    return jnp.concatenate([high, low], axis=0)


def call(body, outs, scratch=(), specs=None, places=None, vmem=VMEM_BYTES, flops=0, moved=0):
    return pl.pallas_call(
        body,
        out_shape=outs,
        in_specs=specs,
        **({} if places is None else {"out_specs": places}),
        scratch_shapes=list(scratch),
        compiler_params=pltpu.CompilerParams(vmem_limit_bytes=vmem),
        cost_estimate=pl.CostEstimate(flops=flops, bytes_accessed=moved, transcendentals=0),
    )


def f32(*shape):
    return jax.ShapeDtypeStruct(shape, F32)


def i32(*shape):
    return jax.ShapeDtypeStruct(shape, jnp.int32)


def front_body(x_ref, d_ref, c_ref, first_ref, second_ref, cols_ref, xv_ref, dv_ref, c_s, sems):
    pairs = [(x_ref.at[k], xv_ref.at[k]) for k in range(K)]
    pairs += [(d_ref.at[k], dv_ref.at[k]) for k in range(K)]
    pairs += [(c_ref, c_s)]
    copies = [pltpu.make_async_copy(*pair, sems.at[f]) for f, pair in enumerate(pairs)]
    for copy in copies:
        copy.start()
    even = jnp.bitwise_and(lax.axis_index("row"), 1) == 0
    lane = iota((CR, 128), 1)
    packed = jnp.zeros((CR, 128), F32)
    for group in (range(0, 8), range(8, 16), range(16, 24), range(24, 33)):
        for f in group:
            copies[f].wait()
        for f in group:
            ref = pairs[f][1]
            top = ref[0:1, :]
            bottom = ref[CR - 1 : CR, :]
            first_ref[f : f + 1, :] = jnp.where(even, bottom, top)
            second_ref[f : f + 1, :] = jnp.where(even, top, bottom)
            both = pltpu.roll(jnp.where(lane == 127, ref[:, 128:256], ref[:, 0:128]), (2 * f + 1) % 128, 1)
            packed = jnp.where((lane >> 1) == f, both, packed)
    for ref in (first_ref, second_ref):
        ref[33:40, :] = jnp.zeros((7, CC), F32)
    cols_ref[...] = packed


def prepare_body(
    lp_ref, tp_ref, c_ref, gr_ref, after_ref, poc_ref, slot_ref, ids_ref, ee_ref, es_ref, leak_ref, lp_s
):
    edges(c_ref[...], ee_ref, es_ref)
    leak_ref[...] = GROUND_LEAK * gr_ref[...].astype(F32)
    lp_s[0] = lp_ref[:, 0:128]
    lp_s[1] = lp_ref[:, 128:256]
    listed = tp_ref[0]
    lane = iota((8, 128), 1)
    row = iota((8, 128), 0)
    for j in range(16):
        chunk = jnp.broadcast_to(listed[:, 128 * j : 128 * j + 128], (8, 128))
        chunk = chunk - (8 * j + row) * PATCH_DEV
        ids_ref[8 * j : 8 * j + 8, :] = jnp.where((lane >> 4) == row, chunk, 0).astype(F32)
    cell = iota((CC, CC), 0)
    spot = iota((CC, CC), 1)
    acc = jnp.zeros((16, CC), F32)
    for q in range(4):
        every = pl.ds(4 * q, 8, stride=16)
        rows = jnp.concatenate([lp_s[0, every, :], lp_s[1, every, :]], axis=1)
        parts = stack2(rows >> 4, rows & 15).astype(F32).astype(BF16)
        pick = one_hot(((spot >> 6) == q) & (cell == 4 * (spot & 63)))
        acc = acc + dot(parts, pick)
    slot_ref[...] = (acc[8:16] * 128.0 + acc[0:8]).astype(jnp.int32)
    place = (acc[0:8] * 16.0 + acc[8:16]).astype(jnp.int32)
    table = stack2(jnp.broadcast_to(listed >> 8, (8, 2048)), jnp.broadcast_to(listed & 255, (8, 2048)))
    table = table.astype(F32).astype(BF16)
    entry = iota((2048, CC), 0)
    highs = []
    lows = []
    for i in range(8):
        found = dot(table, one_hot(entry == place[i : i + 1, :]))
        highs.append(found[0:1])
        lows.append(found[8:9])
    found = jnp.concatenate(highs + lows, axis=0).astype(BF16)
    for q in range(4):
        spread = dot(found, one_hot(spot == q * 64 + (cell >> 2)), 1, 1)
        ids = (spread[0:8] * 256.0 + spread[8:16]).astype(jnp.int32)
        for r in range(4):
            poc_ref[0, pl.ds(4 * q + r, 8, stride=16), :] = ids[:, 0:128]
            poc_ref[1, pl.ds(4 * q + r, 8, stride=16), :] = ids[:, 128:256]


def edges(c, east_ref, south_ref):
    east = 0.5 * (c + pltpu.roll(c, CC - 1, 1))
    east_ref[...] = jnp.where(iota((CR, CC), 1) == CC - 1, 0.0, east)
    south = 0.5 * (c + pltpu.roll(c, CR - 1, 0))
    south_ref[...] = jnp.where(iota((CR, CC), 0) == CR - 1, 0.0, south)


def turn_columns(flows, field):
    return pltpu.roll(flows, 127 - 2 * field, 1)


def operate(v, outer, ee_s, es_s, leak_s):
    lane = iota((CR, 128), 1)
    a = v[:, 0:128]
    b = v[:, 128:256]
    after = pltpu.roll(b, 127, 1)
    flow_a = ee_s[:, 0:128] * (a - jnp.where(lane == 127, after, pltpu.roll(a, 127, 1)))
    flow_b = jnp.where(lane == 127, outer, ee_s[:, 128:256] * (b - after))
    before = pltpu.roll(flow_a, 1, 1)
    total_a = flow_a - jnp.where(lane == 0, -outer, before)
    total_b = flow_b - jnp.where(lane == 0, before, pltpu.roll(flow_b, 1, 1))
    flow = es_s[...] * (v - pltpu.roll(v, CR - 1, 0))
    down = (flow - pltpu.roll(flow, 1, 0)) + leak_s[...] * v
    return total_a + down[:, 0:128], total_b + down[:, 128:256]


def products_body(
    src_ref, x_ref, d_ref, ee_s, es_s, leak_s, poc_ref,
    own_first_ref, own_second_ref, far_first_ref, far_second_ref,
    cols_ref, cols_first_ref, cols_second_ref,
    gram_ref, nf_ref, sf_ref, cf_ref,
    q_s, r_s,
):
    even = jnp.bitwise_and(lax.axis_index("row"), 1) == 0
    first = (own_first_ref[...], far_first_ref[...])
    second = (own_second_ref[...], far_second_ref[...])
    for out, before, after in ((nf_ref, second, first), (sf_ref, first, second)):
        own = jnp.where(even, before[0], after[0])
        far = jnp.where(even, before[1], after[1])
        edge = jnp.where(far[32:33, :] > 0, 0.5 * (own[32:33, :] + far[32:33, :]), 0.0)
        out[...] = edge * (own[0:32, :] - far[0:32, :])
    lane = iota((CR, 128), 1)
    even = jnp.bitwise_and(lax.axis_index("col"), 1) == 0
    next_cols = jnp.where(even, cols_first_ref[...], cols_second_ref[...])
    last_cols = jnp.where(even, cols_second_ref[...], cols_first_ref[...])
    far = jnp.where((lane & 1) == 0, pltpu.roll(next_cols, 127, 1), pltpu.roll(last_cols, 1, 1))
    own = cols_ref[...]
    edge = jnp.where(far > 0, 0.5 * (own + far), 0.0)
    edge = jnp.where((lane & 1) == 0, edge[:, 64:65], edge[:, 65:66])
    cf_ref[...] = jnp.where(lane < 64, edge * (own - far), 0.0)

    def field_step(k):
        image = operate(d_ref[k], turn_columns(cf_ref[...], k + 16), ee_s, es_s, leak_s)
        part = operate(x_ref[k], turn_columns(cf_ref[...], k), ee_s, es_s, leak_s)
        patch = src_ref[k]
        for half in range(2):
            at = slice(128 * half, 128 * half + 128)
            q_s[k, :, at] = image[half]
            r_s[k, :, at] = jnp.where(poc_ref[half] == patch, SOURCE_AMPS, 0.0) - part[half]
        q_s[k, 0:1, :] += nf_ref[k + 16 : k + 17, :]
        q_s[k, CR - 1 : CR, :] += sf_ref[k + 16 : k + 17, :]
        r_s[k, 0:1, :] -= nf_ref[k : k + 1, :]
        r_s[k, CR - 1 : CR, :] -= sf_ref[k : k + 1, :]

    for k in range(K):
        field_step(k)
    acc = jnp.zeros((256, 256), F32)
    for b in range(CR // 8):
        rows = slice(8 * b, 8 * b + 8)
        dh, dl = split(d_ref[:, rows, :].reshape(128, CC))
        qh, ql = split(q_s[:, rows, :].reshape(128, CC))
        rh, rl = split(r_s[:, rows, :].reshape(128, CC))
        lh = stack2(dh, qh)
        ll = stack2(dl, ql)
        gh = stack2(qh, rh)
        gl = stack2(ql, rl)
        acc = acc + (dot(lh, gh, 1, 1) + (dot(lh, gl, 1, 1) + dot(ll, gh, 1, 1)))
    i = iota((256, 256), 0)
    j = iota((256, 256), 1)
    kept = jnp.where((i & 7) == (j & 7), acc, 0.0)
    fold_lanes = jnp.where((iota((256, 128), 0) >> 3) == iota((256, 128), 1), 1.0, 0.0)
    small = dot_full(kept.reshape(32, 8, 256).sum(axis=1), fold_lanes)
    packed = small[0:8]
    for q in range(1, 4):
        packed = packed + pltpu.roll(small[8 * q : 8 * q + 8], 32 * q, 1)
    for o in range(DEVICES):
        gram_ref[8 * o : 8 * o + 8, :] = packed


def mixer(mix):
    high, low = split(mix)
    return stack2(jnp.concatenate([high, high], axis=1), jnp.concatenate([low, jnp.zeros_like(low)], axis=1))


def mixed(mix, d):
    both = dot(mix, stack2(*split(d)))
    return both[0:128] + both[128:256]


def iterate_body(
    gram_ref, x_ref, d_ref, ee_s, es_s, slot_ref, ids_ref, nf_ref, sf_ref, cf_ref,
    out_ref, msg_ref, beta_ref, nn_ref, sn_ref, cn_ref,
    xn_ref, cur_s, turn_s, sem,
):
    packed = gram_ref[...].reshape(DEVICES, 8, 128).sum(axis=0)
    small = jnp.concatenate(
        [packed] + [pltpu.roll(packed, 128 - 32 * q, 1) for q in range(1, 4)], axis=0
    )
    lane = iota((16, 128), 1)
    row = iota((16, 128), 0)
    system = jnp.where(lane < 32, small[0:16], pltpu.roll(small[16:32], 32, 1))
    system = jnp.where(lane < 64, system, 0.0)
    for j in range(K):
        pivot = system[j : j + 1, :]
        pivot = pivot / pivot[:, j : j + 1]
        system = jnp.where(row == j, pivot, system - system[:, j : j + 1] * pivot)

    def part(p):
        return jnp.where(lane < 16, pltpu.roll(system, 128 - 16 * p, 1), 0.0)

    alpha = part(1)
    blank = jnp.zeros((112, 128), F32)
    alpha_pad = stack2(alpha, blank)
    i = iota((128, 128), 0)
    j = iota((128, 128), 1)
    same = (i & 7) == (j & 7)
    repeat_rows = jnp.where((i >> 3) == j, 1.0, 0.0)
    repeat_lanes = jnp.where(i == (j >> 3), 1.0, 0.0)

    def widen(coef):
        return jnp.where(same, dot_full(dot_full(repeat_rows, coef, 1, 1), repeat_lanes), 0.0)

    mix = mixer(widen(alpha_pad))
    for b in range(CR // 8):
        rows = slice(8 * b, 8 * b + 8)
        step = mixed(mix, d_ref[:, rows, :].reshape(128, CC))
        xn_ref[:, rows, :] = x_ref[:, rows, :] + step.reshape(16, 8, CC)
    leave = pltpu.make_async_copy(xn_ref, out_ref, sem)
    leave.start()
    beta = dot_full(part(2), alpha_pad) - part(3)
    beta_ref[...] = widen(stack2(beta, blank))
    base = jnp.concatenate(
        [jnp.where(row == lane, 1.0, 0.0), alpha, jnp.zeros((96, 128), F32)], axis=0
    )
    pair_rows = jnp.where((i >> 1) == j, 1.0, 0.0)
    pair_lanes = jnp.where(i == (j >> 1), 1.0, 0.0)
    pairs = dot_full(dot_full(pair_rows, base), pair_lanes)
    cn = dot_full(cf_ref[...], jnp.where((i & 1) == (j & 1), pairs, 0.0))
    cn_ref[...] = cn
    turn_s[...] = jnp.abs(cn).T
    turned = base.T[0:16, 0:32]
    nn_ref[...] = dot_full(turned, nf_ref[...])
    sn_ref[...] = dot_full(turned, sf_ref[...])

    def field_step(k):
        v = xn_ref[k]
        flow = jnp.abs(ee_s[...] * (v - pltpu.roll(v, CC - 1, 1)))
        total = flow + pltpu.roll(flow, 1, 1)
        flow = jnp.abs(es_s[...] * (v - pltpu.roll(v, CR - 1, 0)))
        cur_s[k] = total + (flow + pltpu.roll(flow, 1, 0))
        cur_s[k, 0:1, :] += jnp.abs(nn_ref[k : k + 1, :])
        cur_s[k, CR - 1 : CR, :] += jnp.abs(sn_ref[k : k + 1, :])

    for k in range(K):
        field_step(k)
    take = iota((32, 256), 0)
    given = iota((32, 256), 1) & 127
    rows_of = one_hot(((given >> 3) == (take & 15)) & (((given >> 2) & 1) == (take >> 4)))
    strips = []
    for b in range(CR // 8):
        high, low = split(cur_s[:, 8 * b : 8 * b + 8, :].reshape(128, CC))
        both = dot(rows_of, stack2(high, low))
        strips += [both[0:16], both[16:32]]
    cell = iota((CC, CC), 0)
    spot = iota((CC, CC), 1)
    blocks = jnp.zeros((128, CC), F32)
    for q in range(4):
        high, low = split(jnp.concatenate([strips[4 * i + q] for i in range(8)], axis=0))
        spread = one_hot(spot == q * 64 + (cell >> 2))
        blocks = blocks + (dot(high, spread) + dot(low, spread))
    outer = jnp.concatenate(
        [turn_s[pl.ds(1, 16, stride=2), :], turn_s[pl.ds(0, 16, stride=2), :]], axis=1
    )
    outer = stack2(*split(outer))
    target = ((cell >> 2) & 3) * 64 + jnp.where(cell < 128, 0, 63)
    band = (cell & 127) >> 4
    owner = iota((128, CC), 0)
    stacked = jnp.zeros((256, 128), F32)
    for b in range(8):
        rim = dot(outer, one_hot((spot == target) & (band == b)))
        inner = 0.5 * (blocks[16 * b : 16 * b + 16] + (rim[0:16] + rim[16:32]))
        slot = slot_ref[b : b + 1, :]
        entry = jnp.broadcast_to(slot >> 7, (16, CC))
        spread = jnp.concatenate([jnp.where(entry == e, inner, 0.0) for e in range(SLOTS)], axis=0)
        high, low = split(spread)
        place = one_hot(owner == (slot & 127))
        stacked = stacked + (dot(high, place, 1, 1) + dot(low, place, 1, 1))
    msg_ref[pl.ds(0, DEVICES, stride=3), :] = stacked[0:128].T
    msg_ref[pl.ds(1, DEVICES, stride=3), :] = stacked[128:256].T
    msg_ref[pl.ds(2, DEVICES, stride=3), :] = ids_ref[...]
    leave.wait()


def direction_body(
    src_ref, xn_ref, d_ref, ee_s, es_s, leak_s, poc_ref, beta_ref, nn_ref, sn_ref, cn_ref,
    do_ref, db_s,
):
    mix = mixer(beta_ref[...])
    for b in range(CR // 8):
        rows = slice(8 * b, 8 * b + 8)
        step = mixed(mix, d_ref[:, rows, :].reshape(128, CC))
        db_s[:, rows, :] = step.reshape(16, 8, CC)

    def field_step(k):
        total = operate(xn_ref[k], turn_columns(cn_ref[...], k), ee_s, es_s, leak_s)
        patch = src_ref[k]
        for half in range(2):
            at = slice(128 * half, 128 * half + 128)
            source = jnp.where(poc_ref[half] == patch, SOURCE_AMPS, 0.0)
            do_ref[k, :, at] = (source - total[half]) + db_s[k, :, at]
        do_ref[k, 0:1, :] -= nn_ref[k : k + 1, :]
        do_ref[k, CR - 1 : CR, :] -= sn_ref[k : k + 1, :]

    for k in range(K):
        field_step(k)


def owner_body(msg_ref, out_ref, ids_s):
    me = lax.axis_index("row") * lax.axis_size("col") + lax.axis_index("col")
    values = stack2(
        msg_ref[pl.ds(0, DEVICES, stride=3), :].T, msg_ref[pl.ds(1, DEVICES, stride=3), :].T
    )
    ids_s[...] = msg_ref[pl.ds(2, DEVICES, stride=3), :].T
    ids = ids_s[pl.ds(pl.multiple_of(jnp.bitwise_and(me, 7) * 16, 16), 16), :]
    patch = iota((128, 256), 0)
    total = jnp.zeros((64, 128), F32)
    for e in range(0, SLOTS, 2):
        pair = jnp.concatenate(
            [values[16 * e : 16 * e + 16], values[16 * e + 16 : 16 * e + 32]], axis=1
        )
        at = jnp.concatenate([ids[e : e + 1], ids[e + 1 : e + 2]], axis=1).astype(jnp.int32)
        group = jnp.broadcast_to(at >> 7, (16, 256))
        spread = jnp.concatenate([jnp.where(group == g, pair, 0.0) for g in range(4)], axis=0)
        high, low = split(spread)
        place = one_hot(patch == (at & 127))
        total = total + (dot(high, place, 1, 1) + dot(low, place, 1, 1))
    for g in range(4):
        out_ref[:, 128 * g : 128 * g + 128] = total[16 * g : 16 * g + 16]


def neighbours(value, axis, which):
    count = lax.axis_size(axis)
    starts = range(which, count - 1, 2)
    return lax.ppermute(value, axis, [(i, i + 1) for i in starts] + [(i + 1, i) for i in starts])


def on_device(iterate, direction, conductance, ground, local_patch, tile_patches, sources):
    vmem = pl.BlockSpec(memory_space=pltpu.VMEM)
    smem = pl.BlockSpec(memory_space=pltpu.SMEM)
    hbm = pl.BlockSpec(memory_space=pltpu.HBM)
    order = pl.BlockSpec(memory_space=pl.ANY)
    field = pltpu.VMEM((K, CR, CC), F32)
    plane = pltpu.VMEM((CR, CC), F32)

    first, second, columns, x_held, d_held = call(
        front_body,
        (
            pltpu.VMEM((40, CC), F32),
            pltpu.VMEM((40, CC), F32),
            pltpu.VMEM((CR, 128), F32),
            field,
            field,
        ),
        scratch=[plane, pltpu.SemaphoreType.DMA((33,))],
        specs=[hbm] * 3,
        places=(vmem,) * 5,
        moved=8_000_000,
    )(*[pltpu.with_memory_space_constraint(a, pltpu.HBM) for a in (iterate, direction, conductance)])
    far_second = neighbours(second, "row", 1)
    cols_second = neighbours(columns, "col", 1)
    far_first = neighbours(first, "row", 0)
    cols_first = neighbours(columns, "col", 0)

    patch_of_cell, slots, ids, ee, es, leak = call(
        prepare_body,
        (i32(2, CR, 128), i32(8, CC), f32(DEVICES, 128), f32(CR, CC), f32(CR, CC), f32(CR, CC)),
        scratch=[pltpu.VMEM((2, CR, 128), jnp.int32)],
        specs=[vmem] * 4 + [order],
        moved=10_000_000,
    )(local_patch, tile_patches, conductance, ground, columns)

    gram, nf, sf, cf = call(
        products_body,
        (f32(8 * DEVICES, 128), f32(32, CC), f32(32, CC), f32(CR, 128)),
        scratch=[field, field],
        specs=[smem] + [vmem] * 13,
        moved=20_000_000,
    )(
        sources, x_held, d_held, ee, es, leak, patch_of_cell,
        first, second, far_first, far_second, columns, cols_first, cols_second,
    )
    gram = lax.all_to_all(gram, AXES, 0, 0, tiled=True)

    new_iterate, message, beta, nn, sn, cn = call(
        iterate_body,
        (f32(K, CR, CC), f32(DEVICES * 3, 128), f32(128, 128), f32(16, CC), f32(16, CC), f32(CR, 128)),
        scratch=[
            field,
            field,
            pltpu.VMEM((128, 128), F32),
            pltpu.SemaphoreType.DMA(()),
        ],
        specs=[vmem] * 10,
        places=(hbm,) + (vmem,) * 5,
        moved=20_000_000,
    )(gram, x_held, d_held, ee, es, slots, ids, nf, sf, cf)
    received = lax.all_to_all(message.reshape(DEVICES, 1, 384), AXES, 0, 0, tiled=True)
    new_direction = call(
        direction_body,
        f32(K, CR, CC),
        scratch=[field],
        specs=[smem] + [vmem] * 10,
        moved=20_000_000,
    )(sources, new_iterate, direction, ee, es, leak, patch_of_cell, beta, nn, sn, cn)
    migration = call(
        owner_body,
        f32(K, PATCH_DEV),
        scratch=[pltpu.VMEM((128, 128), F32)],
        specs=[vmem],
        moved=1_000_000,
    )(received.reshape(DEVICES * 3, 128))
    return new_iterate, new_direction, migration


def solution(mesh):
    in_specs = (
        P(None, "row", "col"),
        P(None, "row", "col"),
        P("row", "col"),
        P("row", "col"),
        P("row", "col"),
        P("row", "col", None),
        P(),
    )
    out_specs = (P(None, "row", "col"), P(None, "row", "col"), P(None, ("row", "col")))
    return jax.shard_map(
        on_device, mesh=mesh, in_specs=in_specs, out_specs=out_specs, check_vma=False
    )
```

```python
import jax
import jax.numpy as jnp
from jax import lax
from jax.experimental import pallas as pl
from jax.experimental.pallas import tpu as pltpu
from jax.sharding import PartitionSpec as P

K = 16
CR = 128
CC = 256
PATCH_DEV = 512
DEVICES = 128
SLOTS = 16
SOURCE_AMPS = 4.0
GROUND_LEAK = 2.0
AXES = ("row", "col")
F32 = jnp.float32
BF16 = jnp.bfloat16
VMEM_BYTES = 20 * 1024 * 1024


def iota(shape, dim):
    return lax.broadcasted_iota(jnp.int32, shape, dim)


def dot(a, b, ca=1, cb=0, precision=None):
    return lax.dot_general(
        a, b, (((ca,), (cb,)), ((), ())), precision=precision, preferred_element_type=F32
    )


def dot_full(a, b, ca=1, cb=0):
    return dot(a, b, ca, cb, lax.Precision.HIGHEST)


def split(a):
    high = a.astype(BF16)
    return high, (a - high.astype(F32)).astype(BF16)


def one_hot(mask):
    return jnp.where(mask, 1.0, 0.0).astype(BF16)


def stack2(high, low):
    return jnp.concatenate([high, low], axis=0)


def call(body, outs, scratch=(), specs=None, places=None, vmem=VMEM_BYTES, flops=0, moved=0):
    return pl.pallas_call(
        body,
        out_shape=outs,
        in_specs=specs,
        **({} if places is None else {"out_specs": places}),
        scratch_shapes=list(scratch),
        compiler_params=pltpu.CompilerParams(vmem_limit_bytes=vmem),
        cost_estimate=pl.CostEstimate(flops=flops, bytes_accessed=moved, transcendentals=0),
    )


def f32(*shape):
    return jax.ShapeDtypeStruct(shape, F32)


def i32(*shape):
    return jax.ShapeDtypeStruct(shape, jnp.int32)


def front_body(
    x_ref, d_ref, c_ref, gr_ref, lp_ref, tp_ref,
    first_ref, second_ref, cols_ref, xv_ref, dv_ref,
    poc_ref, slot_ref, ids_ref, ee_ref, es_ref, leak_ref,
    c_s, gr_s, whole_s, tp_s, lp_s, sems,
):
    pairs = [(x_ref.at[k], xv_ref.at[k]) for k in range(K)]
    pairs += [(d_ref.at[k], dv_ref.at[k]) for k in range(K)]
    pairs += [(c_ref, c_s), (gr_ref, gr_s), (lp_ref, whole_s), (tp_ref, tp_s)]
    copies = [pltpu.make_async_copy(*pair, sems.at[f]) for f, pair in enumerate(pairs)]
    for copy in copies[32:] + copies[:32]:
        copy.start()
    for copy in copies[32:]:
        copy.wait()
    prepare(whole_s, tp_s, c_s, gr_s, poc_ref, slot_ref, ids_ref, ee_ref, es_ref, leak_ref, lp_s)
    even = jnp.bitwise_and(lax.axis_index("row"), 1) == 0
    lane = iota((CR, 128), 1)
    packed = jnp.zeros((CR, 128), F32)
    for group in (range(0, 8), range(8, 16), range(16, 24), range(24, 33)):
        for f in group:
            if f < 32:
                copies[f].wait()
        for f in group:
            ref = pairs[f][1]
            top = ref[0:1, :]
            bottom = ref[CR - 1 : CR, :]
            first_ref[f : f + 1, :] = jnp.where(even, bottom, top)
            second_ref[f : f + 1, :] = jnp.where(even, top, bottom)
            both = pltpu.roll(jnp.where(lane == 127, ref[:, 128:256], ref[:, 0:128]), (2 * f + 1) % 128, 1)
            packed = jnp.where((lane >> 1) == f, both, packed)
    for ref in (first_ref, second_ref):
        ref[33:40, :] = jnp.zeros((7, CC), F32)
    cols_ref[...] = packed


def prepare(lp_ref, tp_ref, c_ref, gr_ref, poc_ref, slot_ref, ids_ref, ee_ref, es_ref, leak_ref, lp_s):
    edges(c_ref[...], ee_ref, es_ref)
    leak_ref[...] = GROUND_LEAK * gr_ref[...].astype(F32)
    lp_s[0] = lp_ref[:, 0:128]
    lp_s[1] = lp_ref[:, 128:256]
    listed = tp_ref[0]
    lane = iota((8, 128), 1)
    row = iota((8, 128), 0)
    for j in range(16):
        chunk = jnp.broadcast_to(listed[:, 128 * j : 128 * j + 128], (8, 128))
        chunk = chunk - (8 * j + row) * PATCH_DEV
        ids_ref[8 * j : 8 * j + 8, :] = jnp.where((lane >> 4) == row, chunk, 0).astype(F32)
    cell = iota((CC, CC), 0)
    spot = iota((CC, CC), 1)
    acc = jnp.zeros((16, CC), F32)
    for q in range(4):
        every = pl.ds(4 * q, 8, stride=16)
        rows = jnp.concatenate([lp_s[0, every, :], lp_s[1, every, :]], axis=1)
        parts = stack2(rows >> 4, rows & 15).astype(F32).astype(BF16)
        pick = one_hot(((spot >> 6) == q) & (cell == 4 * (spot & 63)))
        acc = acc + dot(parts, pick)
    slot_ref[...] = (acc[8:16] * 128.0 + acc[0:8]).astype(jnp.int32)
    place = (acc[0:8] * 16.0 + acc[8:16]).astype(jnp.int32)
    table = jnp.concatenate([listed[:, 128 * j : 128 * j + 128] for j in range(16)], axis=0)
    table = stack2(table >> 8, table & 255).astype(F32).astype(BF16)
    low = iota((128, CC), 0)
    high = iota((16, CC), 0)
    highs = []
    lows = []
    for i in range(8):
        at = place[i : i + 1, :]
        options = dot(table, one_hot(low == (at & 127)))
        here = high == (at >> 7)
        highs.append(jnp.where(here, options[0:16], 0.0).sum(axis=0, keepdims=True))
        lows.append(jnp.where(here, options[16:32], 0.0).sum(axis=0, keepdims=True))
    found = jnp.concatenate(highs + lows, axis=0).astype(BF16)
    for q in range(4):
        spread = dot(found, one_hot(spot == q * 64 + (cell >> 2)), 1, 1)
        ids = (spread[0:8] * 256.0 + spread[8:16]).astype(jnp.int32)
        for r in range(4):
            poc_ref[0, pl.ds(4 * q + r, 8, stride=16), :] = ids[:, 0:128]
            poc_ref[1, pl.ds(4 * q + r, 8, stride=16), :] = ids[:, 128:256]


def edges(c, east_ref, south_ref):
    east = 0.5 * (c + pltpu.roll(c, CC - 1, 1))
    east_ref[...] = jnp.where(iota((CR, CC), 1) == CC - 1, 0.0, east)
    south = 0.5 * (c + pltpu.roll(c, CR - 1, 0))
    south_ref[...] = jnp.where(iota((CR, CC), 0) == CR - 1, 0.0, south)


def turn_columns(flows, field):
    return pltpu.roll(flows, 127 - 2 * field, 1)


def operate(v, outer, ee_s, es_s, leak_s):
    lane = iota((CR, 128), 1)
    a = v[:, 0:128]
    b = v[:, 128:256]
    after = pltpu.roll(b, 127, 1)
    flow_a = ee_s[:, 0:128] * (a - jnp.where(lane == 127, after, pltpu.roll(a, 127, 1)))
    flow_b = ee_s[:, 128:256] * (b - after)
    before = pltpu.roll(flow_a, 1, 1)
    if outer is None:
        total_a = flow_a - jnp.where(lane == 0, 0.0, before)
    else:
        flow_b = jnp.where(lane == 127, outer, flow_b)
        total_a = flow_a - jnp.where(lane == 0, -outer, before)
    total_b = flow_b - jnp.where(lane == 0, before, pltpu.roll(flow_b, 1, 1))
    flow = es_s[...] * (v - pltpu.roll(v, CR - 1, 0))
    down = (flow - pltpu.roll(flow, 1, 0)) + leak_s[...] * v
    return total_a + down[:, 0:128], total_b + down[:, 128:256]


def fields_body(src_ref, x_ref, d_ref, ee_s, es_s, leak_s, poc_ref, q_ref, r_ref):
    for k in range(K):
        image = operate(d_ref[k], None, ee_s, es_s, leak_s)
        part = operate(x_ref[k], None, ee_s, es_s, leak_s)
        patch = src_ref[k]
        for half in range(2):
            at = slice(128 * half, 128 * half + 128)
            q_ref[k, :, at] = image[half]
            r_ref[k, :, at] = jnp.where(poc_ref[half] == patch, SOURCE_AMPS, 0.0) - part[half]


def products_body(
    d_ref, q_ref, r_ref,
    own_first_ref, own_second_ref, far_first_ref, far_second_ref,
    cols_ref, cols_first_ref, cols_second_ref,
    gram_ref, nf_ref, sf_ref, cf_ref,
    q_s, r_s,
):
    even = jnp.bitwise_and(lax.axis_index("row"), 1) == 0
    first = (own_first_ref[...], far_first_ref[...])
    second = (own_second_ref[...], far_second_ref[...])
    for out, before, after in ((nf_ref, second, first), (sf_ref, first, second)):
        own = jnp.where(even, before[0], after[0])
        far = jnp.where(even, before[1], after[1])
        edge = jnp.where(far[32:33, :] > 0, 0.5 * (own[32:33, :] + far[32:33, :]), 0.0)
        out[...] = edge * (own[0:32, :] - far[0:32, :])
    lane = iota((CR, 128), 1)
    even = jnp.bitwise_and(lax.axis_index("col"), 1) == 0
    next_cols = jnp.where(even, cols_first_ref[...], cols_second_ref[...])
    last_cols = jnp.where(even, cols_second_ref[...], cols_first_ref[...])
    far = jnp.where((lane & 1) == 0, pltpu.roll(next_cols, 127, 1), pltpu.roll(last_cols, 1, 1))
    own = cols_ref[...]
    edge = jnp.where(far > 0, 0.5 * (own + far), 0.0)
    edge = jnp.where((lane & 1) == 0, edge[:, 64:65], edge[:, 65:66])
    cf_ref[...] = jnp.where(lane < 64, edge * (own - far), 0.0)

    for n, at, row, flows in ((0, 0, 0, nf_ref), (1, CR - 8, 7, sf_ref)):
        q_s[n] = q_ref[:, at : at + 8, :]
        r_s[n] = r_ref[:, at : at + 8, :]
        for k in range(K):
            q_s[n, k, row : row + 1, :] += flows[k + 16 : k + 17, :]
            r_s[n, k, row : row + 1, :] -= flows[k : k + 1, :]
    side = iota((K, 8, 128), 2)

    def complete(inner, flows, base):
        turned = jnp.concatenate(
            [turn_columns(flows, base + k).reshape(1, 8, 128) for k in range(K)], axis=0
        )
        if base == 0:
            turned = -turned
        return jnp.concatenate(
            [
                inner[:, :, 0:128] + jnp.where(side == 0, turned, 0.0),
                inner[:, :, 128:256] + jnp.where(side == 127, turned, 0.0),
            ],
            axis=2,
        ).reshape(128, CC)

    acc = jnp.zeros((256, 256), F32)
    for b in range(CR // 8):
        rows = slice(8 * b, 8 * b + 8)
        dh, dl = split(d_ref[:, rows, :].reshape(128, CC))
        image = q_s[0] if b == 0 else (q_s[1] if b == CR // 8 - 1 else q_ref[:, rows, :])
        part = r_s[0] if b == 0 else (r_s[1] if b == CR // 8 - 1 else r_ref[:, rows, :])
        flows = cf_ref[rows, :]
        qh, ql = split(complete(image, flows, 16))
        rh, rl = split(complete(part, flows, 0))
        lh = stack2(dh, qh)
        ll = stack2(dl, ql)
        gh = stack2(qh, rh)
        gl = stack2(ql, rl)
        acc = acc + (dot(lh, gh, 1, 1) + (dot(lh, gl, 1, 1) + dot(ll, gh, 1, 1)))
    i = iota((256, 256), 0)
    j = iota((256, 256), 1)
    kept = jnp.where((i & 7) == (j & 7), acc, 0.0)
    fold_lanes = jnp.where((iota((256, 128), 0) >> 3) == iota((256, 128), 1), 1.0, 0.0)
    small = dot_full(kept.reshape(32, 8, 256).sum(axis=1), fold_lanes)
    packed = small[0:8]
    for q in range(1, 4):
        packed = packed + pltpu.roll(small[8 * q : 8 * q + 8], 32 * q, 1)
    for o in range(DEVICES):
        gram_ref[8 * o : 8 * o + 8, :] = packed


def mixer(mix):
    high, low = split(mix)
    return stack2(jnp.concatenate([high, high], axis=1), jnp.concatenate([low, jnp.zeros_like(low)], axis=1))


def mixed(mix, d):
    both = dot(mix, stack2(*split(d)))
    return both[0:128] + both[128:256]


def iterate_body(
    gram_ref, x_ref, d_ref, ee_s, es_s, slot_ref, ids_ref, nf_ref, sf_ref, cf_ref,
    out_ref, msg_ref, beta_ref, nn_ref, sn_ref, cn_ref,
    xn_ref, cur_s, turn_s, sem,
):
    packed = gram_ref[...].reshape(DEVICES, 8, 128).sum(axis=0)
    small = jnp.concatenate(
        [packed] + [pltpu.roll(packed, 128 - 32 * q, 1) for q in range(1, 4)], axis=0
    )
    lane = iota((16, 128), 1)
    row = iota((16, 128), 0)
    system = jnp.where(lane < 32, small[0:16], pltpu.roll(small[16:32], 32, 1))
    system = jnp.where(lane < 64, system, 0.0)
    for j in range(K):
        pivot = system[j : j + 1, :]
        pivot = pivot / pivot[:, j : j + 1]
        system = jnp.where(row == j, pivot, system - system[:, j : j + 1] * pivot)

    def part(p):
        return jnp.where(lane < 16, pltpu.roll(system, 128 - 16 * p, 1), 0.0)

    alpha = part(1)
    blank = jnp.zeros((112, 128), F32)
    alpha_pad = stack2(alpha, blank)
    i = iota((128, 128), 0)
    j = iota((128, 128), 1)
    same = (i & 7) == (j & 7)
    repeat_rows = jnp.where((i >> 3) == j, 1.0, 0.0)
    repeat_lanes = jnp.where(i == (j >> 3), 1.0, 0.0)

    def widen(coef):
        return jnp.where(same, dot_full(dot_full(repeat_rows, coef, 1, 1), repeat_lanes), 0.0)

    mix = mixer(widen(alpha_pad))
    for b in range(CR // 8):
        rows = slice(8 * b, 8 * b + 8)
        step = mixed(mix, d_ref[:, rows, :].reshape(128, CC))
        xn_ref[:, rows, :] = x_ref[:, rows, :] + step.reshape(16, 8, CC)
    leave = pltpu.make_async_copy(xn_ref, out_ref, sem)
    leave.start()
    beta = dot_full(part(2), alpha_pad) - part(3)
    beta_ref[...] = widen(stack2(beta, blank))
    base = jnp.concatenate(
        [jnp.where(row == lane, 1.0, 0.0), alpha, jnp.zeros((96, 128), F32)], axis=0
    )
    pair_rows = jnp.where((i >> 1) == j, 1.0, 0.0)
    pair_lanes = jnp.where(i == (j >> 1), 1.0, 0.0)
    pairs = dot_full(dot_full(pair_rows, base), pair_lanes)
    cn = dot_full(cf_ref[...], jnp.where((i & 1) == (j & 1), pairs, 0.0))
    cn_ref[...] = cn
    turn_s[...] = jnp.abs(cn).T
    turned = base.T[0:16, 0:32]
    nn_ref[...] = dot_full(turned, nf_ref[...])
    sn_ref[...] = dot_full(turned, sf_ref[...])

    def field_step(k):
        v = xn_ref[k]
        flow = jnp.abs(ee_s[...] * (v - pltpu.roll(v, CC - 1, 1)))
        total = flow + pltpu.roll(flow, 1, 1)
        flow = jnp.abs(es_s[...] * (v - pltpu.roll(v, CR - 1, 0)))
        cur_s[k] = total + (flow + pltpu.roll(flow, 1, 0))
        cur_s[k, 0:1, :] += jnp.abs(nn_ref[k : k + 1, :])
        cur_s[k, CR - 1 : CR, :] += jnp.abs(sn_ref[k : k + 1, :])

    for k in range(K):
        field_step(k)
    take = iota((32, 256), 0)
    given = iota((32, 256), 1) & 127
    rows_of = one_hot(((given >> 3) == (take & 15)) & (((given >> 2) & 1) == (take >> 4)))
    strips = []
    for b in range(CR // 8):
        high, low = split(cur_s[:, 8 * b : 8 * b + 8, :].reshape(128, CC))
        both = dot(rows_of, stack2(high, low))
        strips += [both[0:16], both[16:32]]
    cell = iota((CC, CC), 0)
    spot = iota((CC, CC), 1)
    blocks = jnp.zeros((128, CC), F32)
    for q in range(4):
        high, low = split(jnp.concatenate([strips[4 * i + q] for i in range(8)], axis=0))
        spread = one_hot(spot == q * 64 + (cell >> 2))
        blocks = blocks + (dot(high, spread) + dot(low, spread))
    outer = jnp.concatenate(
        [turn_s[pl.ds(1, 16, stride=2), :], turn_s[pl.ds(0, 16, stride=2), :]], axis=1
    )
    outer = stack2(*split(outer))
    target = ((cell >> 2) & 3) * 64 + jnp.where(cell < 128, 0, 63)
    band = (cell & 127) >> 4
    owner = iota((128, CC), 0)
    stacked = jnp.zeros((256, 128), F32)
    for b in range(8):
        rim = dot(outer, one_hot((spot == target) & (band == b)))
        inner = 0.5 * (blocks[16 * b : 16 * b + 16] + (rim[0:16] + rim[16:32]))
        slot = slot_ref[b : b + 1, :]
        entry = jnp.broadcast_to(slot >> 7, (16, CC))
        spread = jnp.concatenate([jnp.where(entry == e, inner, 0.0) for e in range(SLOTS)], axis=0)
        high, low = split(spread)
        place = one_hot(owner == (slot & 127))
        stacked = stacked + (dot(high, place, 1, 1) + dot(low, place, 1, 1))
    msg_ref[pl.ds(0, DEVICES, stride=3), :] = stacked[0:128].T
    msg_ref[pl.ds(1, DEVICES, stride=3), :] = stacked[128:256].T
    msg_ref[pl.ds(2, DEVICES, stride=3), :] = ids_ref[...]
    leave.wait()


def direction_body(
    src_ref, xn_ref, d_ref, ee_s, es_s, leak_s, poc_ref, beta_ref, nn_ref, sn_ref, cn_ref,
    do_ref, db_s,
):
    mix = mixer(beta_ref[...])
    for b in range(CR // 8):
        rows = slice(8 * b, 8 * b + 8)
        step = mixed(mix, d_ref[:, rows, :].reshape(128, CC))
        db_s[:, rows, :] = step.reshape(16, 8, CC)

    def field_step(k):
        total = operate(xn_ref[k], turn_columns(cn_ref[...], k), ee_s, es_s, leak_s)
        patch = src_ref[k]
        for half in range(2):
            at = slice(128 * half, 128 * half + 128)
            source = jnp.where(poc_ref[half] == patch, SOURCE_AMPS, 0.0)
            do_ref[k, :, at] = (source - total[half]) + db_s[k, :, at]
        do_ref[k, 0:1, :] -= nn_ref[k : k + 1, :]
        do_ref[k, CR - 1 : CR, :] -= sn_ref[k : k + 1, :]

    for k in range(K):
        field_step(k)


def owner_body(msg_ref, out_ref, ids_s):
    me = lax.axis_index("row") * lax.axis_size("col") + lax.axis_index("col")
    values = stack2(
        msg_ref[pl.ds(0, DEVICES, stride=3), :].T, msg_ref[pl.ds(1, DEVICES, stride=3), :].T
    )
    ids_s[...] = msg_ref[pl.ds(2, DEVICES, stride=3), :].T
    ids = ids_s[pl.ds(pl.multiple_of(jnp.bitwise_and(me, 7) * 16, 16), 16), :]
    patch = iota((128, 256), 0)
    total = jnp.zeros((64, 128), F32)
    for e in range(0, SLOTS, 2):
        pair = jnp.concatenate(
            [values[16 * e : 16 * e + 16], values[16 * e + 16 : 16 * e + 32]], axis=1
        )
        at = jnp.concatenate([ids[e : e + 1], ids[e + 1 : e + 2]], axis=1).astype(jnp.int32)
        group = jnp.broadcast_to(at >> 7, (16, 256))
        spread = jnp.concatenate([jnp.where(group == g, pair, 0.0) for g in range(4)], axis=0)
        high, low = split(spread)
        place = one_hot(patch == (at & 127))
        total = total + (dot(high, place, 1, 1) + dot(low, place, 1, 1))
    for g in range(4):
        out_ref[:, 128 * g : 128 * g + 128] = total[16 * g : 16 * g + 16]


def neighbours(value, axis, which):
    count = lax.axis_size(axis)
    starts = range(which, count - 1, 2)
    return lax.ppermute(value, axis, [(i, i + 1) for i in starts] + [(i + 1, i) for i in starts])


def on_device(iterate, direction, conductance, ground, local_patch, tile_patches, sources):
    vmem = pl.BlockSpec(memory_space=pltpu.VMEM)
    smem = pl.BlockSpec(memory_space=pltpu.SMEM)
    hbm = pl.BlockSpec(memory_space=pltpu.HBM)
    field = pltpu.VMEM((K, CR, CC), F32)
    plane = pltpu.VMEM((CR, CC), F32)

    first, second, columns, x_held, d_held, patch_of_cell, slots, ids, ee, es, leak = call(
        front_body,
        (
            pltpu.VMEM((40, CC), F32),
            pltpu.VMEM((40, CC), F32),
            pltpu.VMEM((CR, 128), F32),
            field,
            field,
            pltpu.VMEM((2, CR, 128), jnp.int32),
            pltpu.VMEM((8, CC), jnp.int32),
            pltpu.VMEM((DEVICES, 128), F32),
            plane,
            plane,
            plane,
        ),
        scratch=[
            plane,
            pltpu.VMEM((CR, CC), jnp.int32),
            pltpu.VMEM((CR, CC), jnp.int32),
            pltpu.VMEM((1, 1, 2048), jnp.int32),
            pltpu.VMEM((2, CR, 128), jnp.int32),
            pltpu.SemaphoreType.DMA((36,)),
        ],
        specs=[hbm] * 6,
        places=(vmem,) * 11,
        moved=8_000_000,
    )(*[pltpu.with_memory_space_constraint(a, pltpu.HBM) for a in (iterate, direction, conductance, ground, local_patch, tile_patches)])
    far_second = neighbours(second, "row", 1)
    cols_second = neighbours(columns, "col", 1)
    far_first = neighbours(first, "row", 0)
    cols_first = neighbours(columns, "col", 0)

    image, part = call(
        fields_body,
        (pltpu.VMEM((K, CR, CC), F32), pltpu.VMEM((K, CR, CC), F32)),
        specs=[smem] + [vmem] * 6,
        places=(vmem, vmem),
        moved=12_000_000,
    )(sources, x_held, d_held, ee, es, leak, patch_of_cell)

    gram, nf, sf, cf = call(
        products_body,
        (f32(8 * DEVICES, 128), f32(32, CC), f32(32, CC), f32(CR, 128)),
        scratch=[pltpu.VMEM((2, K, 8, CC), F32), pltpu.VMEM((2, K, 8, CC), F32)],
        specs=[vmem] * 10,
        moved=20_000_000,
    )(
        d_held, image, part,
        first, second, far_first, far_second, columns, cols_first, cols_second,
    )
    gram = lax.all_to_all(gram, AXES, 0, 0, tiled=True)

    new_iterate, message, beta, nn, sn, cn = call(
        iterate_body,
        (f32(K, CR, CC), f32(DEVICES * 3, 128), f32(128, 128), f32(16, CC), f32(16, CC), f32(CR, 128)),
        scratch=[
            field,
            field,
            pltpu.VMEM((128, 128), F32),
            pltpu.SemaphoreType.DMA(()),
        ],
        specs=[vmem] * 10,
        places=(hbm,) + (vmem,) * 5,
        moved=20_000_000,
    )(gram, x_held, d_held, ee, es, slots, ids, nf, sf, cf)
    received = lax.all_to_all(message.reshape(DEVICES, 1, 384), AXES, 0, 0, tiled=True)
    new_direction = call(
        direction_body,
        f32(K, CR, CC),
        scratch=[field],
        specs=[smem] + [vmem] * 10,
        moved=20_000_000,
    )(sources, new_iterate, direction, ee, es, leak, patch_of_cell, beta, nn, sn, cn)
    migration = call(
        owner_body,
        f32(K, PATCH_DEV),
        scratch=[pltpu.VMEM((128, 128), F32)],
        specs=[vmem],
        moved=1_000_000,
    )(received.reshape(DEVICES * 3, 128))
    return new_iterate, new_direction, migration


def solution(mesh):
    in_specs = (
        P(None, "row", "col"),
        P(None, "row", "col"),
        P("row", "col"),
        P("row", "col"),
        P("row", "col"),
        P("row", "col", None),
        P(),
    )
    out_specs = (P(None, "row", "col"), P(None, "row", "col"), P(None, ("row", "col")))
    return jax.shard_map(
        on_device, mesh=mesh, in_specs=in_specs, out_specs=out_specs, check_vma=False
    )
```

```python
import jax
import jax.numpy as jnp
from jax import lax
from jax.experimental import pallas as pl
from jax.experimental.pallas import tpu as pltpu
from jax.sharding import PartitionSpec as P

K = 16
CR = 128
CC = 256
PATCH_DEV = 512
DEVICES = 128
SLOTS = 16
SOURCE_AMPS = 4.0
GROUND_LEAK = 2.0
AXES = ("row", "col")
F32 = jnp.float32
BF16 = jnp.bfloat16
VMEM_BYTES = 20 * 1024 * 1024


def iota(shape, dim):
    return lax.broadcasted_iota(jnp.int32, shape, dim)


def dot(a, b, ca=1, cb=0, precision=None):
    return lax.dot_general(
        a, b, (((ca,), (cb,)), ((), ())), precision=precision, preferred_element_type=F32
    )


def dot_full(a, b, ca=1, cb=0):
    return dot(a, b, ca, cb, lax.Precision.HIGHEST)


def split(a):
    high = a.astype(BF16)
    return high, (a - high.astype(F32)).astype(BF16)


def one_hot(mask):
    return jnp.where(mask, 1.0, 0.0).astype(BF16)


def stack2(high, low):
    return jnp.concatenate([high, low], axis=0)


def call(body, outs, scratch=(), specs=None, places=None, vmem=VMEM_BYTES, flops=0, moved=0):
    return pl.pallas_call(
        body,
        out_shape=outs,
        in_specs=specs,
        **({} if places is None else {"out_specs": places}),
        scratch_shapes=list(scratch),
        compiler_params=pltpu.CompilerParams(vmem_limit_bytes=vmem),
        cost_estimate=pl.CostEstimate(flops=flops, bytes_accessed=moved, transcendentals=0),
    )


def f32(*shape):
    return jax.ShapeDtypeStruct(shape, F32)


def i32(*shape):
    return jax.ShapeDtypeStruct(shape, jnp.int32)


def front_body(
    x_ref, d_ref, c_ref, gr_ref, lp_ref, tp_ref,
    first_ref, second_ref, cols_ref, xv_ref, dv_ref,
    poc_ref, slot_ref, ids_ref, ee_ref, es_ref, leak_ref,
    c_s, gr_s, whole_s, tp_s, lp_s, sems,
):
    pairs = [(x_ref.at[k], xv_ref.at[k]) for k in range(K)]
    pairs += [(d_ref.at[k], dv_ref.at[k]) for k in range(K)]
    pairs += [(c_ref, c_s), (gr_ref, gr_s), (lp_ref, whole_s), (tp_ref, tp_s)]
    copies = [pltpu.make_async_copy(*pair, sems.at[f]) for f, pair in enumerate(pairs)]
    for copy in copies[32:] + copies[:32]:
        copy.start()
    for copy in copies[32:]:
        copy.wait()
    prepare(whole_s, tp_s, c_s, gr_s, poc_ref, slot_ref, ids_ref, ee_ref, es_ref, leak_ref, lp_s)
    even = jnp.bitwise_and(lax.axis_index("row"), 1) == 0
    lane = iota((CR, 128), 1)
    packed = jnp.zeros((CR, 128), F32)
    for group in (range(0, 8), range(8, 16), range(16, 24), range(24, 33)):
        for f in group:
            if f < 32:
                copies[f].wait()
        for f in group:
            ref = pairs[f][1]
            top = ref[0:1, :]
            bottom = ref[CR - 1 : CR, :]
            first_ref[f : f + 1, :] = jnp.where(even, bottom, top)
            second_ref[f : f + 1, :] = jnp.where(even, top, bottom)
            both = pltpu.roll(jnp.where(lane == 127, ref[:, 128:256], ref[:, 0:128]), (2 * f + 1) % 128, 1)
            packed = jnp.where((lane >> 1) == f, both, packed)
    for ref in (first_ref, second_ref):
        ref[33:40, :] = jnp.zeros((7, CC), F32)
    cols_ref[...] = packed


def prepare(lp_ref, tp_ref, c_ref, gr_ref, poc_ref, slot_ref, ids_ref, ee_ref, es_ref, leak_ref, lp_s):
    edges(c_ref[...], ee_ref, es_ref)
    leak_ref[...] = GROUND_LEAK * gr_ref[...].astype(F32)
    lp_s[0] = lp_ref[:, 0:128]
    lp_s[1] = lp_ref[:, 128:256]
    listed = tp_ref[0]
    lane = iota((8, 128), 1)
    row = iota((8, 128), 0)
    for j in range(16):
        chunk = jnp.broadcast_to(listed[:, 128 * j : 128 * j + 128], (8, 128))
        chunk = chunk - (8 * j + row) * PATCH_DEV
        ids_ref[8 * j : 8 * j + 8, :] = jnp.where((lane >> 4) == row, chunk, 0).astype(F32)
    cell = iota((CC, CC), 0)
    spot = iota((CC, CC), 1)
    acc = jnp.zeros((16, CC), F32)
    for q in range(4):
        every = pl.ds(4 * q, 8, stride=16)
        rows = jnp.concatenate([lp_s[0, every, :], lp_s[1, every, :]], axis=1)
        parts = stack2(rows >> 4, rows & 15).astype(F32).astype(BF16)
        pick = one_hot(((spot >> 6) == q) & (cell == 4 * (spot & 63)))
        acc = acc + dot(parts, pick)
    slot_ref[...] = (acc[8:16] * 128.0 + acc[0:8]).astype(jnp.int32)
    place = (acc[0:8] * 16.0 + acc[8:16]).astype(jnp.int32)
    table = jnp.concatenate([listed[:, 128 * j : 128 * j + 128] for j in range(16)], axis=0)
    table = stack2(table >> 8, table & 255).astype(F32).astype(BF16)
    low = iota((128, CC), 0)
    high = iota((16, CC), 0)
    highs = []
    lows = []
    for i in range(8):
        at = place[i : i + 1, :]
        options = dot(table, one_hot(low == (at & 127)))
        here = high == (at >> 7)
        highs.append(jnp.where(here, options[0:16], 0.0).sum(axis=0, keepdims=True))
        lows.append(jnp.where(here, options[16:32], 0.0).sum(axis=0, keepdims=True))
    found = jnp.concatenate(highs + lows, axis=0).astype(BF16)
    for q in range(4):
        spread = dot(found, one_hot(spot == q * 64 + (cell >> 2)), 1, 1)
        ids = (spread[0:8] * 256.0 + spread[8:16]).astype(jnp.int32)
        for r in range(4):
            poc_ref[0, pl.ds(4 * q + r, 8, stride=16), :] = ids[:, 0:128]
            poc_ref[1, pl.ds(4 * q + r, 8, stride=16), :] = ids[:, 128:256]


def edges(c, east_ref, south_ref):
    east = 0.5 * (c + pltpu.roll(c, CC - 1, 1))
    east_ref[...] = jnp.where(iota((CR, CC), 1) == CC - 1, 0.0, east)
    south = 0.5 * (c + pltpu.roll(c, CR - 1, 0))
    south_ref[...] = jnp.where(iota((CR, CC), 0) == CR - 1, 0.0, south)


def turn_columns(flows, field):
    return pltpu.roll(flows, 127 - 2 * field, 1)


def operate(v, outer, ee_s, es_s, leak_s):
    lane = iota((CR, 128), 1)
    a = v[:, 0:128]
    b = v[:, 128:256]
    after = pltpu.roll(b, 127, 1)
    flow_a = ee_s[:, 0:128] * (a - jnp.where(lane == 127, after, pltpu.roll(a, 127, 1)))
    flow_b = ee_s[:, 128:256] * (b - after)
    before = pltpu.roll(flow_a, 1, 1)
    if outer is None:
        total_a = flow_a - jnp.where(lane == 0, 0.0, before)
    else:
        flow_b = jnp.where(lane == 127, outer, flow_b)
        total_a = flow_a - jnp.where(lane == 0, -outer, before)
    total_b = flow_b - jnp.where(lane == 0, before, pltpu.roll(flow_b, 1, 1))
    flow = es_s[...] * (v - pltpu.roll(v, CR - 1, 0))
    down = (flow - pltpu.roll(flow, 1, 0)) + leak_s[...] * v
    return total_a + down[:, 0:128], total_b + down[:, 128:256]


def fields_body(src_ref, x_ref, d_ref, ee_s, es_s, leak_s, poc_ref, q_ref, r_ref):
    for k in range(K):
        image = operate(d_ref[k], None, ee_s, es_s, leak_s)
        part = operate(x_ref[k], None, ee_s, es_s, leak_s)
        patch = src_ref[k]
        for half in range(2):
            at = slice(128 * half, 128 * half + 128)
            q_ref[k, :, at] = image[half]
            r_ref[k, :, at] = jnp.where(poc_ref[half] == patch, SOURCE_AMPS, 0.0) - part[half]


def products_body(
    d_ref, q_ref, r_ref,
    own_first_ref, own_second_ref, cols_ref, far_second_ref, cols_second_ref, far_first_ref, cols_first_ref,
    gram_ref, nf_ref, sf_ref, cf_ref,
    q_s, r_s,
):
    even = jnp.bitwise_and(lax.axis_index("row"), 1) == 0
    first = (own_first_ref[...], far_first_ref[...])
    second = (own_second_ref[...], far_second_ref[...])
    for out, before, after in ((nf_ref, second, first), (sf_ref, first, second)):
        own = jnp.where(even, before[0], after[0])
        far = jnp.where(even, before[1], after[1])
        edge = jnp.where(far[32:33, :] > 0, 0.5 * (own[32:33, :] + far[32:33, :]), 0.0)
        out[...] = edge * (own[0:32, :] - far[0:32, :])
    lane = iota((CR, 128), 1)
    even = jnp.bitwise_and(lax.axis_index("col"), 1) == 0
    next_cols = jnp.where(even, cols_first_ref[...], cols_second_ref[...])
    last_cols = jnp.where(even, cols_second_ref[...], cols_first_ref[...])
    far = jnp.where((lane & 1) == 0, pltpu.roll(next_cols, 127, 1), pltpu.roll(last_cols, 1, 1))
    own = cols_ref[...]
    edge = jnp.where(far > 0, 0.5 * (own + far), 0.0)
    edge = jnp.where((lane & 1) == 0, edge[:, 64:65], edge[:, 65:66])
    cf_ref[...] = jnp.where(lane < 64, edge * (own - far), 0.0)

    for n, at, row, flows in ((0, 0, 0, nf_ref), (1, CR - 8, 7, sf_ref)):
        q_s[n] = q_ref[:, at : at + 8, :]
        r_s[n] = r_ref[:, at : at + 8, :]
        for k in range(K):
            q_s[n, k, row : row + 1, :] += flows[k + 16 : k + 17, :]
            r_s[n, k, row : row + 1, :] -= flows[k : k + 1, :]
    side = iota((K, 8, 128), 2)

    def complete(inner, flows, base):
        turned = jnp.concatenate(
            [turn_columns(flows, base + k).reshape(1, 8, 128) for k in range(K)], axis=0
        )
        if base == 0:
            turned = -turned
        return jnp.concatenate(
            [
                inner[:, :, 0:128] + jnp.where(side == 0, turned, 0.0),
                inner[:, :, 128:256] + jnp.where(side == 127, turned, 0.0),
            ],
            axis=2,
        ).reshape(128, CC)

    acc = jnp.zeros((256, 256), F32)
    for b in range(CR // 8):
        rows = slice(8 * b, 8 * b + 8)
        dh, dl = split(d_ref[:, rows, :].reshape(128, CC))
        image = q_s[0] if b == 0 else (q_s[1] if b == CR // 8 - 1 else q_ref[:, rows, :])
        part = r_s[0] if b == 0 else (r_s[1] if b == CR // 8 - 1 else r_ref[:, rows, :])
        flows = cf_ref[rows, :]
        qh, ql = split(complete(image, flows, 16))
        rh, rl = split(complete(part, flows, 0))
        lh = stack2(dh, qh)
        ll = stack2(dl, ql)
        gh = stack2(qh, rh)
        gl = stack2(ql, rl)
        acc = acc + (dot(lh, gh, 1, 1) + (dot(lh, gl, 1, 1) + dot(ll, gh, 1, 1)))
    i = iota((256, 256), 0)
    j = iota((256, 256), 1)
    kept = jnp.where((i & 7) == (j & 7), acc, 0.0)
    fold_lanes = jnp.where((iota((256, 128), 0) >> 3) == iota((256, 128), 1), 1.0, 0.0)
    small = dot_full(kept.reshape(32, 8, 256).sum(axis=1), fold_lanes)
    packed = small[0:8]
    for q in range(1, 4):
        packed = packed + pltpu.roll(small[8 * q : 8 * q + 8], 32 * q, 1)
    for o in range(DEVICES):
        gram_ref[8 * o : 8 * o + 8, :] = packed


def mixer(mix):
    high, low = split(mix)
    return stack2(jnp.concatenate([high, high], axis=1), jnp.concatenate([low, jnp.zeros_like(low)], axis=1))


def mixed(mix, d):
    both = dot(mix, stack2(*split(d)))
    return both[0:128] + both[128:256]


def part(system, p):
    lane = iota((16, 128), 1)
    return jnp.where(lane < 16, pltpu.roll(system, 128 - 16 * p, 1), 0.0)


def padded(coef):
    return stack2(coef, jnp.zeros((112, 128), F32))


def widen(coef):
    i = iota((128, 128), 0)
    j = iota((128, 128), 1)
    repeat_rows = jnp.where((i >> 3) == j, 1.0, 0.0)
    repeat_lanes = jnp.where(i == (j >> 3), 1.0, 0.0)
    wide = dot_full(dot_full(repeat_rows, padded(coef), 1, 1), repeat_lanes)
    return jnp.where((i & 7) == (j & 7), wide, 0.0)


def iterate_body(
    gram_ref, x_ref, d_ref, ee_s, es_s, slot_ref, ids_ref, nf_ref, sf_ref, cf_ref,
    out_ref, msg_ref, system_ref, nn_ref, sn_ref, cn_ref,
    xn_ref, cur_s, turn_s, sem,
):
    packed = gram_ref[...].reshape(DEVICES, 8, 128).sum(axis=0)
    small = jnp.concatenate(
        [packed] + [pltpu.roll(packed, 128 - 32 * q, 1) for q in range(1, 4)], axis=0
    )
    lane = iota((16, 128), 1)
    row = iota((16, 128), 0)
    system = jnp.where(lane < 32, small[0:16], pltpu.roll(small[16:32], 32, 1))
    system = jnp.where(lane < 64, system, 0.0)
    for j in range(K):
        pivot = system[j : j + 1, :]
        pivot = pivot / pivot[:, j : j + 1]
        system = jnp.where(row == j, pivot, system - system[:, j : j + 1] * pivot)

    system_ref[...] = system
    alpha = part(system, 1)
    i = iota((128, 128), 0)
    j = iota((128, 128), 1)
    mix = mixer(widen(alpha))
    for b in range(CR // 8):
        rows = slice(8 * b, 8 * b + 8)
        step = mixed(mix, d_ref[:, rows, :].reshape(128, CC))
        xn_ref[:, rows, :] = x_ref[:, rows, :] + step.reshape(16, 8, CC)
    leave = pltpu.make_async_copy(xn_ref, out_ref, sem)
    leave.start()
    base = jnp.concatenate(
        [jnp.where(row == lane, 1.0, 0.0), alpha, jnp.zeros((96, 128), F32)], axis=0
    )
    pair_rows = jnp.where((i >> 1) == j, 1.0, 0.0)
    pair_lanes = jnp.where(i == (j >> 1), 1.0, 0.0)
    pairs = dot_full(dot_full(pair_rows, base), pair_lanes)
    cn = dot_full(cf_ref[...], jnp.where((i & 1) == (j & 1), pairs, 0.0))
    cn_ref[...] = cn
    turn_s[...] = jnp.abs(cn).T
    turned = base.T[0:16, 0:32]
    nn_ref[...] = dot_full(turned, nf_ref[...])
    sn_ref[...] = dot_full(turned, sf_ref[...])

    def field_step(k):
        v = xn_ref[k]
        flow = jnp.abs(ee_s[...] * (v - pltpu.roll(v, CC - 1, 1)))
        total = flow + pltpu.roll(flow, 1, 1)
        flow = jnp.abs(es_s[...] * (v - pltpu.roll(v, CR - 1, 0)))
        cur_s[k] = total + (flow + pltpu.roll(flow, 1, 0))
        cur_s[k, 0:1, :] += jnp.abs(nn_ref[k : k + 1, :])
        cur_s[k, CR - 1 : CR, :] += jnp.abs(sn_ref[k : k + 1, :])

    for k in range(K):
        field_step(k)
    take = iota((32, 256), 0)
    given = iota((32, 256), 1) & 127
    rows_of = one_hot(((given >> 3) == (take & 15)) & (((given >> 2) & 1) == (take >> 4)))
    strips = []
    for b in range(CR // 8):
        high, low = split(cur_s[:, 8 * b : 8 * b + 8, :].reshape(128, CC))
        both = dot(rows_of, stack2(high, low))
        strips += [both[0:16], both[16:32]]
    cell = iota((CC, CC), 0)
    spot = iota((CC, CC), 1)
    blocks = jnp.zeros((128, CC), F32)
    for q in range(4):
        high, low = split(jnp.concatenate([strips[4 * i + q] for i in range(8)], axis=0))
        spread = one_hot(spot == q * 64 + (cell >> 2))
        blocks = blocks + (dot(high, spread) + dot(low, spread))
    outer = jnp.concatenate(
        [turn_s[pl.ds(1, 16, stride=2), :], turn_s[pl.ds(0, 16, stride=2), :]], axis=1
    )
    band = (iota((K, CC), 1) & 127) >> 4
    outer = jnp.concatenate([jnp.where(band == i, outer, 0.0) for i in range(8)], axis=0)
    target = ((cell >> 2) & 3) * 64 + jnp.where(cell < 128, 0, 63)
    rim = dot(stack2(*split(outer)), one_hot(spot == target))
    blocks = 0.5 * (blocks + (rim[0:128] + rim[128:256]))
    owner = iota((128, CC), 0)
    stacked = jnp.zeros((256, 128), F32)
    for b in range(8):
        inner = blocks[16 * b : 16 * b + 16]
        slot = slot_ref[b : b + 1, :]
        entry = jnp.broadcast_to(slot >> 7, (16, CC))
        spread = jnp.concatenate([jnp.where(entry == e, inner, 0.0) for e in range(SLOTS)], axis=0)
        high, low = split(spread)
        place = one_hot(owner == (slot & 127))
        stacked = stacked + (dot(high, place, 1, 1) + dot(low, place, 1, 1))
    msg_ref[pl.ds(0, DEVICES, stride=3), :] = stacked[0:128].T
    msg_ref[pl.ds(1, DEVICES, stride=3), :] = stacked[128:256].T
    msg_ref[pl.ds(2, DEVICES, stride=3), :] = ids_ref[...]
    leave.wait()


def direction_body(
    src_ref, xn_ref, d_ref, ee_s, es_s, leak_s, poc_ref, system_ref, nn_ref, sn_ref, cn_ref,
    do_ref, db_s,
):
    system = system_ref[...]
    beta = dot_full(part(system, 2), padded(part(system, 1))) - part(system, 3)
    mix = mixer(widen(beta))
    for b in range(CR // 8):
        rows = slice(8 * b, 8 * b + 8)
        step = mixed(mix, d_ref[:, rows, :].reshape(128, CC))
        db_s[:, rows, :] = step.reshape(16, 8, CC)

    def field_step(k):
        total = operate(xn_ref[k], turn_columns(cn_ref[...], k), ee_s, es_s, leak_s)
        patch = src_ref[k]
        for half in range(2):
            at = slice(128 * half, 128 * half + 128)
            source = jnp.where(poc_ref[half] == patch, SOURCE_AMPS, 0.0)
            do_ref[k, :, at] = (source - total[half]) + db_s[k, :, at]
        do_ref[k, 0:1, :] -= nn_ref[k : k + 1, :]
        do_ref[k, CR - 1 : CR, :] -= sn_ref[k : k + 1, :]

    for k in range(K):
        field_step(k)


def owner_body(msg_ref, out_ref, ids_s):
    me = lax.axis_index("row") * lax.axis_size("col") + lax.axis_index("col")
    values = stack2(
        msg_ref[pl.ds(0, DEVICES, stride=3), :].T, msg_ref[pl.ds(1, DEVICES, stride=3), :].T
    )
    ids_s[...] = msg_ref[pl.ds(2, DEVICES, stride=3), :].T
    ids = ids_s[pl.ds(pl.multiple_of(jnp.bitwise_and(me, 7) * 16, 16), 16), :]
    patch = iota((128, 256), 0)
    total = jnp.zeros((64, 128), F32)
    for e in range(0, SLOTS, 2):
        pair = jnp.concatenate(
            [values[16 * e : 16 * e + 16], values[16 * e + 16 : 16 * e + 32]], axis=1
        )
        at = jnp.concatenate([ids[e : e + 1], ids[e + 1 : e + 2]], axis=1).astype(jnp.int32)
        group = jnp.broadcast_to(at >> 7, (16, 256))
        spread = jnp.concatenate([jnp.where(group == g, pair, 0.0) for g in range(4)], axis=0)
        high, low = split(spread)
        place = one_hot(patch == (at & 127))
        total = total + (dot(high, place, 1, 1) + dot(low, place, 1, 1))
    for g in range(4):
        out_ref[:, 128 * g : 128 * g + 128] = total[16 * g : 16 * g + 16]


def neighbours(value, axis, which):
    count = lax.axis_size(axis)
    starts = range(which, count - 1, 2)
    return lax.ppermute(value, axis, [(i, i + 1) for i in starts] + [(i + 1, i) for i in starts])


def on_device(iterate, direction, conductance, ground, local_patch, tile_patches, sources):
    vmem = pl.BlockSpec(memory_space=pltpu.VMEM)
    smem = pl.BlockSpec(memory_space=pltpu.SMEM)
    hbm = pl.BlockSpec(memory_space=pltpu.HBM)
    field = pltpu.VMEM((K, CR, CC), F32)
    plane = pltpu.VMEM((CR, CC), F32)

    first, second, columns, x_held, d_held, patch_of_cell, slots, ids, ee, es, leak = call(
        front_body,
        (
            pltpu.VMEM((40, CC), F32),
            pltpu.VMEM((40, CC), F32),
            pltpu.VMEM((CR, 128), F32),
            field,
            field,
            pltpu.VMEM((2, CR, 128), jnp.int32),
            pltpu.VMEM((8, CC), jnp.int32),
            pltpu.VMEM((DEVICES, 128), F32),
            plane,
            plane,
            plane,
        ),
        scratch=[
            plane,
            pltpu.VMEM((CR, CC), jnp.int32),
            pltpu.VMEM((CR, CC), jnp.int32),
            pltpu.VMEM((1, 1, 2048), jnp.int32),
            pltpu.VMEM((2, CR, 128), jnp.int32),
            pltpu.SemaphoreType.DMA((36,)),
        ],
        specs=[hbm] * 6,
        places=(vmem,) * 11,
        moved=8_000_000,
    )(*[pltpu.with_memory_space_constraint(a, pltpu.HBM) for a in (iterate, direction, conductance, ground, local_patch, tile_patches)])
    far_second = neighbours(second, "row", 1)
    cols_second = neighbours(columns, "col", 1)
    far_first = neighbours(first, "row", 0)
    cols_first = neighbours(columns, "col", 0)

    image, part = call(
        fields_body,
        (pltpu.VMEM((K, CR, CC), F32), pltpu.VMEM((K, CR, CC), F32)),
        specs=[smem] + [vmem] * 6,
        places=(vmem, vmem),
        moved=12_000_000,
    )(sources, x_held, d_held, ee, es, leak, patch_of_cell)

    gram, nf, sf, cf = call(
        products_body,
        (f32(8 * DEVICES, 128), f32(32, CC), f32(32, CC), f32(CR, 128)),
        scratch=[pltpu.VMEM((2, K, 8, CC), F32), pltpu.VMEM((2, K, 8, CC), F32)],
        specs=[vmem] * 10,
        moved=20_000_000,
    )(
        d_held, image, part,
        first, second, columns, far_second, cols_second, far_first, cols_first,
    )
    gram = lax.all_to_all(gram, AXES, 0, 0, tiled=True)

    new_iterate, message, system, nn, sn, cn = call(
        iterate_body,
        (f32(K, CR, CC), f32(DEVICES * 3, 128), f32(16, 128), f32(16, CC), f32(16, CC), f32(CR, 128)),
        scratch=[
            field,
            field,
            pltpu.VMEM((128, 128), F32),
            pltpu.SemaphoreType.DMA(()),
        ],
        specs=[vmem] * 10,
        places=(hbm,) + (vmem,) * 5,
        moved=20_000_000,
    )(gram, x_held, d_held, ee, es, slots, ids, nf, sf, cf)
    received = lax.all_to_all(message.reshape(DEVICES, 1, 384), AXES, 0, 0, tiled=True)
    new_direction = call(
        direction_body,
        f32(K, CR, CC),
        scratch=[field],
        specs=[smem] + [vmem] * 10,
        moved=20_000_000,
    )(sources, new_iterate, direction, ee, es, leak, patch_of_cell, system, nn, sn, cn)
    migration = call(
        owner_body,
        f32(K, PATCH_DEV),
        scratch=[pltpu.VMEM((128, 128), F32)],
        specs=[vmem],
        moved=1_000_000,
    )(received.reshape(DEVICES * 3, 128))
    return new_iterate, new_direction, migration


def solution(mesh):
    in_specs = (
        P(None, "row", "col"),
        P(None, "row", "col"),
        P("row", "col"),
        P("row", "col"),
        P("row", "col"),
        P("row", "col", None),
        P(),
    )
    out_specs = (P(None, "row", "col"), P(None, "row", "col"), P(None, ("row", "col")))
    return jax.shard_map(
        on_device, mesh=mesh, in_specs=in_specs, out_specs=out_specs, check_vma=False
    )
```

```python
import jax
import jax.numpy as jnp
from jax import lax
from jax.experimental import pallas as pl
from jax.experimental.pallas import tpu as pltpu
from jax.sharding import PartitionSpec as P

K = 16
CR = 128
CC = 256
PATCH_DEV = 512
DEVICES = 128
SLOTS = 16
SOURCE_AMPS = 4.0
GROUND_LEAK = 2.0
AXES = ("row", "col")
F32 = jnp.float32
BF16 = jnp.bfloat16
VMEM_BYTES = 20 * 1024 * 1024


def iota(shape, dim):
    return lax.broadcasted_iota(jnp.int32, shape, dim)


def dot(a, b, ca=1, cb=0, precision=None):
    return lax.dot_general(
        a, b, (((ca,), (cb,)), ((), ())), precision=precision, preferred_element_type=F32
    )


def dot_full(a, b, ca=1, cb=0):
    return dot(a, b, ca, cb, lax.Precision.HIGHEST)


def split(a):
    high = a.astype(BF16)
    return high, (a - high.astype(F32)).astype(BF16)


def one_hot(mask):
    return jnp.where(mask, 1.0, 0.0).astype(BF16)


def stack2(high, low):
    return jnp.concatenate([high, low], axis=0)


def call(body, outs, scratch=(), specs=None, places=None, vmem=VMEM_BYTES, flops=0, moved=0):
    return pl.pallas_call(
        body,
        out_shape=outs,
        in_specs=specs,
        **({} if places is None else {"out_specs": places}),
        scratch_shapes=list(scratch),
        compiler_params=pltpu.CompilerParams(vmem_limit_bytes=vmem),
        cost_estimate=pl.CostEstimate(flops=flops, bytes_accessed=moved, transcendentals=0),
    )


def f32(*shape):
    return jax.ShapeDtypeStruct(shape, F32)


def i32(*shape):
    return jax.ShapeDtypeStruct(shape, jnp.int32)


def front_body(
    x_ref, d_ref, c_ref, gr_ref, lp_ref, tp_ref,
    first_ref, second_ref, cols_ref, xv_ref, dv_ref,
    poc_ref, slot_ref, ids_ref, ee_ref, es_ref, leak_ref,
    c_s, gr_s, whole_s, tp_s, lp_s, sems,
):
    fields = [xv_ref.at[k] for k in range(K)] + [dv_ref.at[k] for k in range(K)] + [c_s]
    quads = [pl.ds(4 * g, 4) for g in range(4)]
    pairs = [(x_ref.at[quad], xv_ref.at[quad]) for quad in quads]
    pairs += [(d_ref.at[quad], dv_ref.at[quad]) for quad in quads]
    pairs += [(c_ref, c_s), (gr_ref, gr_s), (lp_ref, whole_s), (tp_ref, tp_s)]
    copies = [pltpu.make_async_copy(*pair, sems.at[f]) for f, pair in enumerate(pairs)]
    for copy in copies[8:] + copies[:8]:
        copy.start()
    for copy in copies[8:]:
        copy.wait()
    prepare(whole_s, tp_s, c_s, gr_s, poc_ref, slot_ref, ids_ref, ee_ref, es_ref, leak_ref, lp_s)
    even = jnp.bitwise_and(lax.axis_index("row"), 1) == 0
    lane = iota((CR, 128), 1)
    packed = jnp.zeros((CR, 128), F32)
    for group in (range(0, 8), range(8, 16), range(16, 24), range(24, 33)):
        for g in range(group[0] // 4, group[0] // 4 + 2):
            copies[g].wait()
        for f in group:
            ref = fields[f]
            top = ref[0:1, :]
            bottom = ref[CR - 1 : CR, :]
            first_ref[f : f + 1, :] = jnp.where(even, bottom, top)
            second_ref[f : f + 1, :] = jnp.where(even, top, bottom)
            both = pltpu.roll(jnp.where(lane == 127, ref[:, 128:256], ref[:, 0:128]), (2 * f + 1) % 128, 1)
            packed = jnp.where((lane >> 1) == f, both, packed)
    for ref in (first_ref, second_ref):
        ref[33:40, :] = jnp.zeros((7, CC), F32)
    cols_ref[...] = packed


def prepare(lp_ref, tp_ref, c_ref, gr_ref, poc_ref, slot_ref, ids_ref, ee_ref, es_ref, leak_ref, lp_s):
    edges(c_ref[...], ee_ref, es_ref)
    leak_ref[...] = GROUND_LEAK * gr_ref[...].astype(F32)
    lp_s[0] = lp_ref[:, 0:128]
    lp_s[1] = lp_ref[:, 128:256]
    listed = tp_ref[0]
    lane = iota((8, 128), 1)
    row = iota((8, 128), 0)
    for j in range(16):
        chunk = jnp.broadcast_to(listed[:, 128 * j : 128 * j + 128], (8, 128))
        chunk = chunk - (8 * j + row) * PATCH_DEV
        ids_ref[8 * j : 8 * j + 8, :] = jnp.where((lane >> 4) == row, chunk, 0).astype(F32)
    cell = iota((CC, CC), 0)
    spot = iota((CC, CC), 1)
    acc = jnp.zeros((16, CC), F32)
    for q in range(4):
        every = pl.ds(4 * q, 8, stride=16)
        rows = jnp.concatenate([lp_s[0, every, :], lp_s[1, every, :]], axis=1)
        parts = stack2(rows >> 4, rows & 15).astype(F32).astype(BF16)
        pick = one_hot(((spot >> 6) == q) & (cell == 4 * (spot & 63)))
        acc = acc + dot(parts, pick)
    slot_ref[...] = (acc[8:16] * 128.0 + acc[0:8]).astype(jnp.int32)
    place = (acc[0:8] * 16.0 + acc[8:16]).astype(jnp.int32)
    table = jnp.concatenate([listed[:, 128 * j : 128 * j + 128] for j in range(16)], axis=0)
    table = stack2(table >> 8, table & 255).astype(F32).astype(BF16)
    low = iota((128, CC), 0)
    high = iota((16, CC), 0)
    highs = []
    lows = []
    for i in range(8):
        at = place[i : i + 1, :]
        options = dot(table, one_hot(low == (at & 127)))
        here = high == (at >> 7)
        highs.append(jnp.where(here, options[0:16], 0.0).sum(axis=0, keepdims=True))
        lows.append(jnp.where(here, options[16:32], 0.0).sum(axis=0, keepdims=True))
    found = jnp.concatenate(highs + lows, axis=0).astype(BF16)
    for q in range(4):
        spread = dot(found, one_hot(spot == q * 64 + (cell >> 2)), 1, 1)
        ids = (spread[0:8] * 256.0 + spread[8:16]).astype(jnp.int32)
        for r in range(4):
            poc_ref[0, pl.ds(4 * q + r, 8, stride=16), :] = ids[:, 0:128]
            poc_ref[1, pl.ds(4 * q + r, 8, stride=16), :] = ids[:, 128:256]


def edges(c, east_ref, south_ref):
    east = 0.5 * (c + pltpu.roll(c, CC - 1, 1))
    east_ref[...] = jnp.where(iota((CR, CC), 1) == CC - 1, 0.0, east)
    south = 0.5 * (c + pltpu.roll(c, CR - 1, 0))
    south_ref[...] = jnp.where(iota((CR, CC), 0) == CR - 1, 0.0, south)


def turn_columns(flows, field):
    return pltpu.roll(flows, 127 - 2 * field, 1)


def operate(v, outer, ee_s, es_s, leak_s):
    lane = iota((CR, 128), 1)
    a = v[:, 0:128]
    b = v[:, 128:256]
    after = pltpu.roll(b, 127, 1)
    flow_a = ee_s[:, 0:128] * (a - jnp.where(lane == 127, after, pltpu.roll(a, 127, 1)))
    flow_b = ee_s[:, 128:256] * (b - after)
    before = pltpu.roll(flow_a, 1, 1)
    if outer is None:
        total_a = flow_a - jnp.where(lane == 0, 0.0, before)
    else:
        flow_b = jnp.where(lane == 127, outer, flow_b)
        total_a = flow_a - jnp.where(lane == 0, -outer, before)
    total_b = flow_b - jnp.where(lane == 0, before, pltpu.roll(flow_b, 1, 1))
    flow = es_s[...] * (v - pltpu.roll(v, CR - 1, 0))
    down = (flow - pltpu.roll(flow, 1, 0)) + leak_s[...] * v
    return total_a + down[:, 0:128], total_b + down[:, 128:256]


def fields_body(src_ref, x_ref, d_ref, ee_s, es_s, leak_s, poc_ref, q_ref, r_ref):
    for k in range(K):
        image = operate(d_ref[k], None, ee_s, es_s, leak_s)
        part = operate(x_ref[k], None, ee_s, es_s, leak_s)
        patch = src_ref[k]
        for half in range(2):
            at = slice(128 * half, 128 * half + 128)
            q_ref[k, :, at] = image[half]
            r_ref[k, :, at] = jnp.where(poc_ref[half] == patch, SOURCE_AMPS, 0.0) - part[half]


def products_body(
    d_ref, q_ref, r_ref,
    own_first_ref, own_second_ref, cols_ref, far_second_ref, cols_second_ref, far_first_ref, cols_first_ref,
    gram_ref, nf_ref, sf_ref, cf_ref,
    q_s, r_s,
):
    even = jnp.bitwise_and(lax.axis_index("row"), 1) == 0
    first = (own_first_ref[...], far_first_ref[...])
    second = (own_second_ref[...], far_second_ref[...])
    for out, before, after in ((nf_ref, second, first), (sf_ref, first, second)):
        own = jnp.where(even, before[0], after[0])
        far = jnp.where(even, before[1], after[1])
        edge = jnp.where(far[32:33, :] > 0, 0.5 * (own[32:33, :] + far[32:33, :]), 0.0)
        out[...] = edge * (own[0:32, :] - far[0:32, :])
    lane = iota((CR, 128), 1)
    even = jnp.bitwise_and(lax.axis_index("col"), 1) == 0
    next_cols = jnp.where(even, cols_first_ref[...], cols_second_ref[...])
    last_cols = jnp.where(even, cols_second_ref[...], cols_first_ref[...])
    far = jnp.where((lane & 1) == 0, pltpu.roll(next_cols, 127, 1), pltpu.roll(last_cols, 1, 1))
    own = cols_ref[...]
    edge = jnp.where(far > 0, 0.5 * (own + far), 0.0)
    edge = jnp.where((lane & 1) == 0, edge[:, 64:65], edge[:, 65:66])
    cf_ref[...] = jnp.where(lane < 64, edge * (own - far), 0.0)

    for n, at, row, flows in ((0, 0, 0, nf_ref), (1, CR - 8, 7, sf_ref)):
        q_s[n] = q_ref[:, at : at + 8, :]
        r_s[n] = r_ref[:, at : at + 8, :]
        for k in range(K):
            q_s[n, k, row : row + 1, :] += flows[k + 16 : k + 17, :]
            r_s[n, k, row : row + 1, :] -= flows[k : k + 1, :]
    side = iota((K, 8, 128), 2)

    def complete(inner, flows, base):
        turned = jnp.concatenate(
            [turn_columns(flows, base + k).reshape(1, 8, 128) for k in range(K)], axis=0
        )
        if base == 0:
            turned = -turned
        return jnp.concatenate(
            [
                inner[:, :, 0:128] + jnp.where(side == 0, turned, 0.0),
                inner[:, :, 128:256] + jnp.where(side == 127, turned, 0.0),
            ],
            axis=2,
        ).reshape(128, CC)

    acc = jnp.zeros((256, 256), F32)
    for b in range(CR // 8):
        rows = slice(8 * b, 8 * b + 8)
        dh, dl = split(d_ref[:, rows, :].reshape(128, CC))
        image = q_s[0] if b == 0 else (q_s[1] if b == CR // 8 - 1 else q_ref[:, rows, :])
        part = r_s[0] if b == 0 else (r_s[1] if b == CR // 8 - 1 else r_ref[:, rows, :])
        flows = cf_ref[rows, :]
        qh, ql = split(complete(image, flows, 16))
        rh, rl = split(complete(part, flows, 0))
        lh = stack2(dh, qh)
        ll = stack2(dl, ql)
        gh = stack2(qh, rh)
        gl = stack2(ql, rl)
        acc = acc + (dot(lh, gh, 1, 1) + (dot(lh, gl, 1, 1) + dot(ll, gh, 1, 1)))
    i = iota((256, 256), 0)
    j = iota((256, 256), 1)
    kept = jnp.where((i & 7) == (j & 7), acc, 0.0)
    fold_lanes = jnp.where((iota((256, 128), 0) >> 3) == iota((256, 128), 1), 1.0, 0.0)
    small = dot_full(kept.reshape(32, 8, 256).sum(axis=1), fold_lanes)
    packed = small[0:8]
    for q in range(1, 4):
        packed = packed + pltpu.roll(small[8 * q : 8 * q + 8], 32 * q, 1)
    for o in range(DEVICES):
        gram_ref[8 * o : 8 * o + 8, :] = packed


def mixer(mix):
    high, low = split(mix)
    return stack2(jnp.concatenate([high, high], axis=1), jnp.concatenate([low, jnp.zeros_like(low)], axis=1))


def mixed(mix, d):
    both = dot(mix, stack2(*split(d)))
    return both[0:128] + both[128:256]


def part(system, p):
    lane = iota((16, 128), 1)
    return jnp.where(lane < 16, pltpu.roll(system, 128 - 16 * p, 1), 0.0)


def padded(coef):
    return stack2(coef, jnp.zeros((112, 128), F32))


def widen(coef):
    i = iota((128, 128), 0)
    j = iota((128, 128), 1)
    repeat_rows = jnp.where((i >> 3) == j, 1.0, 0.0)
    repeat_lanes = jnp.where(i == (j >> 3), 1.0, 0.0)
    wide = dot_full(dot_full(repeat_rows, padded(coef), 1, 1), repeat_lanes)
    return jnp.where((i & 7) == (j & 7), wide, 0.0)


def iterate_body(
    gram_ref, x_ref, d_ref, ee_s, es_s, slot_ref, ids_ref, nf_ref, sf_ref, cf_ref,
    out_ref, msg_ref, system_ref, nn_ref, sn_ref, cn_ref,
    xn_ref, cur_s, turn_s, sem,
):
    packed = gram_ref[...].reshape(DEVICES, 8, 128).sum(axis=0)
    small = jnp.concatenate(
        [packed] + [pltpu.roll(packed, 128 - 32 * q, 1) for q in range(1, 4)], axis=0
    )
    lane = iota((16, 128), 1)
    row = iota((16, 128), 0)
    system = jnp.where(lane < 32, small[0:16], pltpu.roll(small[16:32], 32, 1))
    system = jnp.where(lane < 64, system, 0.0)
    for j in range(K):
        column = jnp.broadcast_to(system[:, j : j + 1], (16, 128))
        pivot = system[j : j + 1, :] / column[j : j + 1, :]
        system = jnp.where(row == j, pivot, system - column * pivot)

    system_ref[...] = system
    alpha = part(system, 1)
    i = iota((128, 128), 0)
    j = iota((128, 128), 1)
    mix = mixer(widen(alpha))
    for b in range(CR // 8):
        rows = slice(8 * b, 8 * b + 8)
        step = mixed(mix, d_ref[:, rows, :].reshape(128, CC))
        xn_ref[:, rows, :] = x_ref[:, rows, :] + step.reshape(16, 8, CC)
    leave = pltpu.make_async_copy(xn_ref, out_ref, sem)
    leave.start()
    base = jnp.concatenate(
        [jnp.where(row == lane, 1.0, 0.0), alpha, jnp.zeros((96, 128), F32)], axis=0
    )
    pair_rows = jnp.where((i >> 1) == j, 1.0, 0.0)
    pair_lanes = jnp.where(i == (j >> 1), 1.0, 0.0)
    pairs = dot_full(dot_full(pair_rows, base), pair_lanes)
    cn = dot_full(cf_ref[...], jnp.where((i & 1) == (j & 1), pairs, 0.0))
    cn_ref[...] = cn
    turn_s[...] = jnp.abs(cn).T
    turned = base.T[0:16, 0:32]
    nn_ref[...] = dot_full(turned, nf_ref[...])
    sn_ref[...] = dot_full(turned, sf_ref[...])

    def field_step(k):
        v = xn_ref[k]
        flow = jnp.abs(ee_s[...] * (v - pltpu.roll(v, CC - 1, 1)))
        total = flow + pltpu.roll(flow, 1, 1)
        flow = jnp.abs(es_s[...] * (v - pltpu.roll(v, CR - 1, 0)))
        cur_s[k] = total + (flow + pltpu.roll(flow, 1, 0))
        cur_s[k, 0:1, :] += jnp.abs(nn_ref[k : k + 1, :])
        cur_s[k, CR - 1 : CR, :] += jnp.abs(sn_ref[k : k + 1, :])

    for k in range(K):
        field_step(k)
    take = iota((32, 256), 0)
    given = iota((32, 256), 1) & 127
    rows_of = one_hot(((given >> 3) == (take & 15)) & (((given >> 2) & 1) == (take >> 4)))
    strips = []
    for b in range(CR // 8):
        high, low = split(cur_s[:, 8 * b : 8 * b + 8, :].reshape(128, CC))
        both = dot(rows_of, stack2(high, low))
        strips += [both[0:16], both[16:32]]
    cell = iota((CC, CC), 0)
    spot = iota((CC, CC), 1)
    blocks = jnp.zeros((128, CC), F32)
    for q in range(4):
        high, low = split(jnp.concatenate([strips[4 * i + q] for i in range(8)], axis=0))
        spread = one_hot(spot == q * 64 + (cell >> 2))
        blocks = blocks + (dot(high, spread) + dot(low, spread))
    outer = jnp.concatenate(
        [turn_s[pl.ds(1, 16, stride=2), :], turn_s[pl.ds(0, 16, stride=2), :]], axis=1
    )
    band = (iota((K, CC), 1) & 127) >> 4
    outer = jnp.concatenate([jnp.where(band == i, outer, 0.0) for i in range(8)], axis=0)
    target = ((cell >> 2) & 3) * 64 + jnp.where(cell < 128, 0, 63)
    rim = dot(stack2(*split(outer)), one_hot(spot == target))
    blocks = 0.5 * (blocks + (rim[0:128] + rim[128:256]))
    owner = iota((128, CC), 0)
    stacked = jnp.zeros((256, 128), F32)
    for b in range(8):
        inner = blocks[16 * b : 16 * b + 16]
        slot = slot_ref[b : b + 1, :]
        entry = jnp.broadcast_to(slot >> 7, (16, CC))
        spread = jnp.concatenate([jnp.where(entry == e, inner, 0.0) for e in range(SLOTS)], axis=0)
        high, low = split(spread)
        place = one_hot(owner == (slot & 127))
        stacked = stacked + (dot(high, place, 1, 1) + dot(low, place, 1, 1))
    msg_ref[pl.ds(0, DEVICES, stride=3), :] = stacked[0:128].T
    msg_ref[pl.ds(1, DEVICES, stride=3), :] = stacked[128:256].T
    msg_ref[pl.ds(2, DEVICES, stride=3), :] = ids_ref[...]
    leave.wait()


def direction_body(
    src_ref, xn_ref, d_ref, ee_s, es_s, leak_s, poc_ref, system_ref, nn_ref, sn_ref, cn_ref,
    do_ref, db_s,
):
    system = system_ref[...]
    beta = dot_full(part(system, 2), padded(part(system, 1))) - part(system, 3)
    mix = mixer(widen(beta))
    for b in range(CR // 8):
        rows = slice(8 * b, 8 * b + 8)
        step = mixed(mix, d_ref[:, rows, :].reshape(128, CC))
        db_s[:, rows, :] = step.reshape(16, 8, CC)

    def field_step(k):
        total = operate(xn_ref[k], turn_columns(cn_ref[...], k), ee_s, es_s, leak_s)
        patch = src_ref[k]
        for half in range(2):
            at = slice(128 * half, 128 * half + 128)
            source = jnp.where(poc_ref[half] == patch, SOURCE_AMPS, 0.0)
            do_ref[k, :, at] = (source - total[half]) + db_s[k, :, at]
        do_ref[k, 0:1, :] -= nn_ref[k : k + 1, :]
        do_ref[k, CR - 1 : CR, :] -= sn_ref[k : k + 1, :]

    for k in range(K):
        field_step(k)


def owner_body(msg_ref, out_ref, ids_s):
    me = lax.axis_index("row") * lax.axis_size("col") + lax.axis_index("col")
    values = stack2(
        msg_ref[pl.ds(0, DEVICES, stride=3), :].T, msg_ref[pl.ds(1, DEVICES, stride=3), :].T
    )
    ids_s[...] = msg_ref[pl.ds(2, DEVICES, stride=3), :].T
    ids = ids_s[pl.ds(pl.multiple_of(jnp.bitwise_and(me, 7) * 16, 16), 16), :]
    patch = iota((128, 256), 0)
    total = jnp.zeros((64, 128), F32)
    for e in range(0, SLOTS, 2):
        pair = jnp.concatenate(
            [values[16 * e : 16 * e + 16], values[16 * e + 16 : 16 * e + 32]], axis=1
        )
        at = jnp.concatenate([ids[e : e + 1], ids[e + 1 : e + 2]], axis=1).astype(jnp.int32)
        group = jnp.broadcast_to(at >> 7, (16, 256))
        spread = jnp.concatenate([jnp.where(group == g, pair, 0.0) for g in range(4)], axis=0)
        high, low = split(spread)
        place = one_hot(patch == (at & 127))
        total = total + (dot(high, place, 1, 1) + dot(low, place, 1, 1))
    for g in range(4):
        out_ref[:, 128 * g : 128 * g + 128] = total[16 * g : 16 * g + 16]


def neighbours(value, axis, which):
    count = lax.axis_size(axis)
    starts = range(which, count - 1, 2)
    return lax.ppermute(value, axis, [(i, i + 1) for i in starts] + [(i + 1, i) for i in starts])


def on_device(iterate, direction, conductance, ground, local_patch, tile_patches, sources):
    vmem = pl.BlockSpec(memory_space=pltpu.VMEM)
    smem = pl.BlockSpec(memory_space=pltpu.SMEM)
    hbm = pl.BlockSpec(memory_space=pltpu.HBM)
    field = pltpu.VMEM((K, CR, CC), F32)
    plane = pltpu.VMEM((CR, CC), F32)

    first, second, columns, x_held, d_held, patch_of_cell, slots, ids, ee, es, leak = call(
        front_body,
        (
            pltpu.VMEM((40, CC), F32),
            pltpu.VMEM((40, CC), F32),
            pltpu.VMEM((CR, 128), F32),
            field,
            field,
            pltpu.VMEM((2, CR, 128), jnp.int32),
            pltpu.VMEM((8, CC), jnp.int32),
            pltpu.VMEM((DEVICES, 128), F32),
            plane,
            plane,
            plane,
        ),
        scratch=[
            plane,
            pltpu.VMEM((CR, CC), jnp.int32),
            pltpu.VMEM((CR, CC), jnp.int32),
            pltpu.VMEM((1, 1, 2048), jnp.int32),
            pltpu.VMEM((2, CR, 128), jnp.int32),
            pltpu.SemaphoreType.DMA((12,)),
        ],
        specs=[hbm] * 6,
        places=(vmem,) * 11,
        moved=8_000_000,
    )(*[pltpu.with_memory_space_constraint(a, pltpu.HBM) for a in (iterate, direction, conductance, ground, local_patch, tile_patches)])
    far_second = neighbours(second, "row", 1)
    cols_second = neighbours(columns, "col", 1)
    far_first = neighbours(first, "row", 0)
    cols_first = neighbours(columns, "col", 0)

    image, part = call(
        fields_body,
        (pltpu.VMEM((K, CR, CC), F32), pltpu.VMEM((K, CR, CC), F32)),
        specs=[smem] + [vmem] * 6,
        places=(vmem, vmem),
        moved=12_000_000,
    )(sources, x_held, d_held, ee, es, leak, patch_of_cell)

    gram, nf, sf, cf = call(
        products_body,
        (f32(8 * DEVICES, 128), f32(32, CC), f32(32, CC), f32(CR, 128)),
        scratch=[pltpu.VMEM((2, K, 8, CC), F32), pltpu.VMEM((2, K, 8, CC), F32)],
        specs=[vmem] * 10,
        moved=20_000_000,
    )(
        d_held, image, part,
        first, second, columns, far_second, cols_second, far_first, cols_first,
    )
    gram = lax.all_to_all(gram, AXES, 0, 0, tiled=True)

    new_iterate, message, system, nn, sn, cn = call(
        iterate_body,
        (f32(K, CR, CC), f32(DEVICES * 3, 128), f32(16, 128), f32(16, CC), f32(16, CC), f32(CR, 128)),
        scratch=[
            field,
            field,
            pltpu.VMEM((128, 128), F32),
            pltpu.SemaphoreType.DMA(()),
        ],
        specs=[vmem] * 10,
        places=(hbm,) + (vmem,) * 5,
        moved=20_000_000,
    )(gram, x_held, d_held, ee, es, slots, ids, nf, sf, cf)
    received = lax.all_to_all(message.reshape(DEVICES, 1, 384), AXES, 0, 0, tiled=True)
    new_direction = call(
        direction_body,
        f32(K, CR, CC),
        scratch=[field],
        specs=[smem] + [vmem] * 10,
        moved=20_000_000,
    )(sources, new_iterate, direction, ee, es, leak, patch_of_cell, system, nn, sn, cn)
    migration = call(
        owner_body,
        f32(K, PATCH_DEV),
        scratch=[pltpu.VMEM((128, 128), F32)],
        specs=[vmem],
        moved=1_000_000,
    )(received.reshape(DEVICES * 3, 128))
    return new_iterate, new_direction, migration


def solution(mesh):
    in_specs = (
        P(None, "row", "col"),
        P(None, "row", "col"),
        P("row", "col"),
        P("row", "col"),
        P("row", "col"),
        P("row", "col", None),
        P(),
    )
    out_specs = (P(None, "row", "col"), P(None, "row", "col"), P(None, ("row", "col")))
    return jax.shard_map(
        on_device, mesh=mesh, in_specs=in_specs, out_specs=out_specs, check_vma=False
    )
```

```python
import jax
import jax.numpy as jnp
from jax import lax
from jax.experimental import pallas as pl
from jax.experimental.pallas import tpu as pltpu
from jax.sharding import PartitionSpec as P

K = 16
CR = 128
CC = 256
PATCH_DEV = 512
DEVICES = 128
SLOTS = 16
SOURCE_AMPS = 4.0
GROUND_LEAK = 2.0
AXES = ("row", "col")
F32 = jnp.float32
BF16 = jnp.bfloat16
VMEM_BYTES = 20 * 1024 * 1024


def iota(shape, dim):
    return lax.broadcasted_iota(jnp.int32, shape, dim)


def dot(a, b, ca=1, cb=0, precision=None):
    return lax.dot_general(
        a, b, (((ca,), (cb,)), ((), ())), precision=precision, preferred_element_type=F32
    )


def dot_full(a, b, ca=1, cb=0):
    return dot(a, b, ca, cb, lax.Precision.HIGHEST)


def split(a):
    high = a.astype(BF16)
    return high, (a - high.astype(F32)).astype(BF16)


def one_hot(mask):
    return jnp.where(mask, 1.0, 0.0).astype(BF16)


def stack2(high, low):
    return jnp.concatenate([high, low], axis=0)


def call(body, outs, scratch=(), specs=None, places=None, vmem=VMEM_BYTES, flops=0, moved=0):
    return pl.pallas_call(
        body,
        out_shape=outs,
        in_specs=specs,
        **({} if places is None else {"out_specs": places}),
        scratch_shapes=list(scratch),
        compiler_params=pltpu.CompilerParams(vmem_limit_bytes=vmem),
        cost_estimate=pl.CostEstimate(flops=flops, bytes_accessed=moved, transcendentals=0),
    )


def f32(*shape):
    return jax.ShapeDtypeStruct(shape, F32)


def i32(*shape):
    return jax.ShapeDtypeStruct(shape, jnp.int32)


def front_body(
    x_ref, d_ref, c_ref, gr_ref, lp_ref, tp_ref,
    first_ref, second_ref, cols_ref, xv_ref, dv_ref,
    poc_ref, slot_ref, ids_ref, ee_ref, es_ref, leak_ref,
    c_s, gr_s, whole_s, tp_s, lp_s, sems,
):
    fields = [xv_ref.at[k] for k in range(K)] + [dv_ref.at[k] for k in range(K)] + [c_s]
    quads = [pl.ds(4 * g, 4) for g in range(4)]
    pairs = [(x_ref.at[quad], xv_ref.at[quad]) for quad in quads]
    pairs += [(d_ref.at[quad], dv_ref.at[quad]) for quad in quads]
    pairs += [(c_ref, c_s), (gr_ref, gr_s), (lp_ref, whole_s), (tp_ref, tp_s)]
    copies = [pltpu.make_async_copy(*pair, sems.at[f]) for f, pair in enumerate(pairs)]
    for copy in copies[8:] + copies[:8]:
        copy.start()
    for copy in copies[8:]:
        copy.wait()
    prepare(whole_s, tp_s, c_s, gr_s, poc_ref, slot_ref, ids_ref, ee_ref, es_ref, leak_ref, lp_s)
    even = jnp.bitwise_and(lax.axis_index("row"), 1) == 0
    lane = iota((CR, 128), 1)
    packed = jnp.zeros((CR, 128), F32)
    for group in (range(0, 8), range(8, 16), range(16, 24), range(24, 33)):
        for g in range(group[0] // 4, group[0] // 4 + 2):
            copies[g].wait()
        for f in group:
            ref = fields[f]
            top = ref[0:1, :]
            bottom = ref[CR - 1 : CR, :]
            first_ref[f : f + 1, :] = jnp.where(even, bottom, top)
            second_ref[f : f + 1, :] = jnp.where(even, top, bottom)
            both = pltpu.roll(jnp.where(lane == 127, ref[:, 128:256], ref[:, 0:128]), (2 * f + 1) % 128, 1)
            packed = jnp.where((lane >> 1) == f, both, packed)
    for ref in (first_ref, second_ref):
        ref[33:40, :] = jnp.zeros((7, CC), F32)
    cols_ref[...] = packed


def prepare(lp_ref, tp_ref, c_ref, gr_ref, poc_ref, slot_ref, ids_ref, ee_ref, es_ref, leak_ref, lp_s):
    edges(c_ref[...], ee_ref, es_ref)
    leak_ref[...] = GROUND_LEAK * gr_ref[...].astype(F32)
    lp_s[0] = lp_ref[:, 0:128]
    lp_s[1] = lp_ref[:, 128:256]
    listed = tp_ref[0]
    lane = iota((8, 128), 1)
    row = iota((8, 128), 0)
    for j in range(16):
        chunk = jnp.broadcast_to(listed[:, 128 * j : 128 * j + 128], (8, 128))
        chunk = chunk - (8 * j + row) * PATCH_DEV
        ids_ref[8 * j : 8 * j + 8, :] = jnp.where((lane >> 4) == row, chunk, 0).astype(F32)
    cell = iota((CC, CC), 0)
    spot = iota((CC, CC), 1)
    acc = jnp.zeros((16, CC), F32)
    for q in range(4):
        every = pl.ds(4 * q, 8, stride=16)
        rows = jnp.concatenate([lp_s[0, every, :], lp_s[1, every, :]], axis=1)
        parts = stack2(rows >> 4, rows & 15).astype(F32).astype(BF16)
        pick = one_hot(((spot >> 6) == q) & (cell == 4 * (spot & 63)))
        acc = acc + dot(parts, pick)
    slot_ref[...] = (acc[8:16] * 128.0 + acc[0:8]).astype(jnp.int32)
    place = (acc[0:8] * 16.0 + acc[8:16]).astype(jnp.int32)
    table = jnp.concatenate([listed[:, 128 * j : 128 * j + 128] for j in range(16)], axis=0)
    table = stack2(table >> 8, table & 255).astype(F32).astype(BF16)
    low = iota((128, CC), 0)
    high = iota((16, CC), 0)
    highs = []
    lows = []
    for i in range(8):
        at = place[i : i + 1, :]
        options = dot(table, one_hot(low == (at & 127)))
        here = high == (at >> 7)
        highs.append(jnp.where(here, options[0:16], 0.0).sum(axis=0, keepdims=True))
        lows.append(jnp.where(here, options[16:32], 0.0).sum(axis=0, keepdims=True))
    found = jnp.concatenate(highs + lows, axis=0).astype(BF16)
    for q in range(4):
        spread = dot(found, one_hot(spot == q * 64 + (cell >> 2)), 1, 1)
        ids = (spread[0:8] * 256.0 + spread[8:16]).astype(jnp.int32)
        for r in range(4):
            poc_ref[0, pl.ds(4 * q + r, 8, stride=16), :] = ids[:, 0:128]
            poc_ref[1, pl.ds(4 * q + r, 8, stride=16), :] = ids[:, 128:256]


def edges(c, east_ref, south_ref):
    east = 0.5 * (c + pltpu.roll(c, CC - 1, 1))
    east_ref[...] = jnp.where(iota((CR, CC), 1) == CC - 1, 0.0, east)
    south = 0.5 * (c + pltpu.roll(c, CR - 1, 0))
    south_ref[...] = jnp.where(iota((CR, CC), 0) == CR - 1, 0.0, south)


def turn_columns(flows, field):
    return pltpu.roll(flows, 127 - 2 * field, 1)


def operate(v, outer, ee_s, es_s, leak_s):
    lane = iota((CR, 128), 1)
    a = v[:, 0:128]
    b = v[:, 128:256]
    after = pltpu.roll(b, 127, 1)
    flow_a = ee_s[:, 0:128] * (a - jnp.where(lane == 127, after, pltpu.roll(a, 127, 1)))
    flow_b = ee_s[:, 128:256] * (b - after)
    before = pltpu.roll(flow_a, 1, 1)
    if outer is None:
        total_a = flow_a - jnp.where(lane == 0, 0.0, before)
    else:
        flow_b = jnp.where(lane == 127, outer, flow_b)
        total_a = flow_a - jnp.where(lane == 0, -outer, before)
    total_b = flow_b - jnp.where(lane == 0, before, pltpu.roll(flow_b, 1, 1))
    flow = es_s[...] * (v - pltpu.roll(v, CR - 1, 0))
    down = (flow - pltpu.roll(flow, 1, 0)) + leak_s[...] * v
    return total_a + down[:, 0:128], total_b + down[:, 128:256]


def fields_body(src_ref, x_ref, d_ref, ee_s, es_s, leak_s, poc_ref, q_ref, r_ref):
    for k in range(K):
        image = operate(d_ref[k], None, ee_s, es_s, leak_s)
        part = operate(x_ref[k], None, ee_s, es_s, leak_s)
        patch = src_ref[k]
        for half in range(2):
            at = slice(128 * half, 128 * half + 128)
            q_ref[k, :, at] = image[half]
            r_ref[k, :, at] = jnp.where(poc_ref[half] == patch, SOURCE_AMPS, 0.0) - part[half]


def products_body(
    d_ref, q_ref, r_ref,
    own_first_ref, own_second_ref, cols_ref, far_second_ref, cols_second_ref, far_first_ref, cols_first_ref,
    gram_ref, nf_ref, sf_ref, cf_ref,
    q_s, r_s,
):
    even = jnp.bitwise_and(lax.axis_index("row"), 1) == 0
    first = (own_first_ref[...], far_first_ref[...])
    second = (own_second_ref[...], far_second_ref[...])
    for out, before, after in ((nf_ref, second, first), (sf_ref, first, second)):
        own = jnp.where(even, before[0], after[0])
        far = jnp.where(even, before[1], after[1])
        edge = jnp.where(far[32:33, :] > 0, 0.5 * (own[32:33, :] + far[32:33, :]), 0.0)
        out[...] = edge * (own[0:32, :] - far[0:32, :])
    lane = iota((CR, 128), 1)
    even = jnp.bitwise_and(lax.axis_index("col"), 1) == 0
    next_cols = jnp.where(even, cols_first_ref[...], cols_second_ref[...])
    last_cols = jnp.where(even, cols_second_ref[...], cols_first_ref[...])
    far = jnp.where((lane & 1) == 0, pltpu.roll(next_cols, 127, 1), pltpu.roll(last_cols, 1, 1))
    own = cols_ref[...]
    edge = jnp.where(far > 0, 0.5 * (own + far), 0.0)
    edge = jnp.where((lane & 1) == 0, edge[:, 64:65], edge[:, 65:66])
    cf_ref[...] = jnp.where(lane < 64, edge * (own - far), 0.0)

    for n, at, row, flows in ((0, 0, 0, nf_ref), (1, CR - 8, 7, sf_ref)):
        q_s[n] = q_ref[:, at : at + 8, :]
        r_s[n] = r_ref[:, at : at + 8, :]
        for k in range(K):
            q_s[n, k, row : row + 1, :] += flows[k + 16 : k + 17, :]
            r_s[n, k, row : row + 1, :] -= flows[k : k + 1, :]
    side = iota((K, 8, 128), 2)

    def complete(inner, flows, base):
        turned = jnp.concatenate(
            [turn_columns(flows, base + k).reshape(1, 8, 128) for k in range(K)], axis=0
        )
        if base == 0:
            turned = -turned
        return jnp.concatenate(
            [
                inner[:, :, 0:128] + jnp.where(side == 0, turned, 0.0),
                inner[:, :, 128:256] + jnp.where(side == 127, turned, 0.0),
            ],
            axis=2,
        ).reshape(128, CC)

    acc = jnp.zeros((256, 256), F32)
    for b in range(CR // 8):
        rows = slice(8 * b, 8 * b + 8)
        dh, dl = split(d_ref[:, rows, :].reshape(128, CC))
        image = q_s[0] if b == 0 else (q_s[1] if b == CR // 8 - 1 else q_ref[:, rows, :])
        part = r_s[0] if b == 0 else (r_s[1] if b == CR // 8 - 1 else r_ref[:, rows, :])
        flows = cf_ref[rows, :]
        qh, ql = split(complete(image, flows, 16))
        rh, rl = split(complete(part, flows, 0))
        lh = stack2(dh, qh)
        ll = stack2(dl, ql)
        gh = stack2(qh, rh)
        gl = stack2(ql, rl)
        left = jnp.concatenate([lh, lh, ll], axis=1)
        acc = acc + dot(left, jnp.concatenate([gh, gl, gh], axis=1), 1, 1)
    i = iota((256, 256), 0)
    j = iota((256, 256), 1)
    kept = jnp.where((i & 7) == (j & 7), acc, 0.0)
    fold_lanes = jnp.where((iota((256, 128), 0) >> 3) == iota((256, 128), 1), 1.0, 0.0)
    small = dot_full(kept.reshape(32, 8, 256).sum(axis=1), fold_lanes)
    packed = small[0:8]
    for q in range(1, 4):
        packed = packed + pltpu.roll(small[8 * q : 8 * q + 8], 32 * q, 1)
    for o in range(DEVICES):
        gram_ref[8 * o : 8 * o + 8, :] = packed


def mixer(mix):
    high, low = split(mix)
    return stack2(jnp.concatenate([high, high], axis=1), jnp.concatenate([low, jnp.zeros_like(low)], axis=1))


def mixed(mix, d):
    both = dot(mix, stack2(*split(d)))
    return both[0:128] + both[128:256]


def part(system, p):
    lane = iota((16, 128), 1)
    return jnp.where(lane < 16, pltpu.roll(system, 128 - 16 * p, 1), 0.0)


def padded(coef):
    return stack2(coef, jnp.zeros((112, 128), F32))


def widen(coef):
    i = iota((128, 128), 0)
    j = iota((128, 128), 1)
    repeat_rows = jnp.where((i >> 3) == j, 1.0, 0.0)
    repeat_lanes = jnp.where(i == (j >> 3), 1.0, 0.0)
    wide = dot_full(dot_full(repeat_rows, padded(coef), 1, 1), repeat_lanes)
    return jnp.where((i & 7) == (j & 7), wide, 0.0)


def iterate_body(
    gram_ref, x_ref, d_ref, ee_s, es_s, slot_ref, ids_ref, nf_ref, sf_ref, cf_ref,
    out_ref, msg_ref, system_ref, nn_ref, sn_ref, cn_ref,
    xn_ref, cur_s, turn_s, sem,
):
    packed = gram_ref[...].reshape(DEVICES, 8, 128).sum(axis=0)
    small = jnp.concatenate(
        [packed] + [pltpu.roll(packed, 128 - 32 * q, 1) for q in range(1, 4)], axis=0
    )
    lane = iota((16, 128), 1)
    row = iota((16, 128), 0)
    system = jnp.where(lane < 32, small[0:16], pltpu.roll(small[16:32], 32, 1))
    system = jnp.where(lane < 64, system, 0.0)
    for j in range(K):
        column = jnp.broadcast_to(system[:, j : j + 1], (16, 128))
        pivot = system[j : j + 1, :] / column[j : j + 1, :]
        system = jnp.where(row == j, pivot, system - column * pivot)

    system_ref[...] = system
    alpha = part(system, 1)
    i = iota((128, 128), 0)
    j = iota((128, 128), 1)
    mix = mixer(widen(alpha))
    for b in range(CR // 8):
        rows = slice(8 * b, 8 * b + 8)
        step = mixed(mix, d_ref[:, rows, :].reshape(128, CC))
        xn_ref[:, rows, :] = x_ref[:, rows, :] + step.reshape(16, 8, CC)
    leave = pltpu.make_async_copy(xn_ref, out_ref, sem)
    leave.start()
    base = jnp.concatenate(
        [jnp.where(row == lane, 1.0, 0.0), alpha, jnp.zeros((96, 128), F32)], axis=0
    )
    pair_rows = jnp.where((i >> 1) == j, 1.0, 0.0)
    pair_lanes = jnp.where(i == (j >> 1), 1.0, 0.0)
    pairs = dot_full(dot_full(pair_rows, base), pair_lanes)
    cn = dot_full(cf_ref[...], jnp.where((i & 1) == (j & 1), pairs, 0.0))
    cn_ref[...] = cn
    turn_s[...] = jnp.abs(cn).T
    turned = base.T[0:16, 0:32]
    nn_ref[...] = dot_full(turned, nf_ref[...])
    sn_ref[...] = dot_full(turned, sf_ref[...])

    def field_step(k):
        v = xn_ref[k]
        flow = jnp.abs(ee_s[...] * (v - pltpu.roll(v, CC - 1, 1)))
        total = flow + pltpu.roll(flow, 1, 1)
        flow = jnp.abs(es_s[...] * (v - pltpu.roll(v, CR - 1, 0)))
        cur_s[k] = total + (flow + pltpu.roll(flow, 1, 0))
        cur_s[k, 0:1, :] += jnp.abs(nn_ref[k : k + 1, :])
        cur_s[k, CR - 1 : CR, :] += jnp.abs(sn_ref[k : k + 1, :])

    for k in range(K):
        field_step(k)
    take = iota((32, 256), 0)
    given = iota((32, 256), 1) & 127
    rows_of = one_hot(((given >> 3) == (take & 15)) & (((given >> 2) & 1) == (take >> 4)))
    strips = []
    for b in range(CR // 8):
        high, low = split(cur_s[:, 8 * b : 8 * b + 8, :].reshape(128, CC))
        both = dot(rows_of, stack2(high, low))
        strips += [both[0:16], both[16:32]]
    cell = iota((CC, CC), 0)
    spot = iota((CC, CC), 1)
    blocks = jnp.zeros((128, CC), F32)
    for q in range(4):
        high, low = split(jnp.concatenate([strips[4 * i + q] for i in range(8)], axis=0))
        spread = one_hot(spot == q * 64 + (cell >> 2))
        blocks = blocks + (dot(high, spread) + dot(low, spread))
    outer = jnp.concatenate(
        [turn_s[pl.ds(1, 16, stride=2), :], turn_s[pl.ds(0, 16, stride=2), :]], axis=1
    )
    band = (iota((K, CC), 1) & 127) >> 4
    outer = jnp.concatenate([jnp.where(band == i, outer, 0.0) for i in range(8)], axis=0)
    target = ((cell >> 2) & 3) * 64 + jnp.where(cell < 128, 0, 63)
    rim = dot(stack2(*split(outer)), one_hot(spot == target))
    blocks = 0.5 * (blocks + (rim[0:128] + rim[128:256]))
    owner = iota((128, CC), 0)
    stacked = jnp.zeros((256, 128), F32)
    for b in range(8):
        inner = blocks[16 * b : 16 * b + 16]
        slot = slot_ref[b : b + 1, :]
        entry = jnp.broadcast_to(slot >> 7, (16, CC))
        spread = jnp.concatenate([jnp.where(entry == e, inner, 0.0) for e in range(SLOTS)], axis=0)
        high, low = split(spread)
        place = one_hot(owner == (slot & 127))
        stacked = stacked + (dot(high, place, 1, 1) + dot(low, place, 1, 1))
    msg_ref[pl.ds(0, DEVICES, stride=3), :] = stacked[0:128].T
    msg_ref[pl.ds(1, DEVICES, stride=3), :] = stacked[128:256].T
    msg_ref[pl.ds(2, DEVICES, stride=3), :] = ids_ref[...]
    leave.wait()


def direction_body(
    src_ref, xn_ref, d_ref, ee_s, es_s, leak_s, poc_ref, system_ref, nn_ref, sn_ref, cn_ref,
    do_ref, db_s,
):
    system = system_ref[...]
    beta = dot_full(part(system, 2), padded(part(system, 1))) - part(system, 3)
    mix = mixer(widen(beta))
    for b in range(CR // 8):
        rows = slice(8 * b, 8 * b + 8)
        step = mixed(mix, d_ref[:, rows, :].reshape(128, CC))
        db_s[:, rows, :] = step.reshape(16, 8, CC)

    def field_step(k):
        total = operate(xn_ref[k], turn_columns(cn_ref[...], k), ee_s, es_s, leak_s)
        patch = src_ref[k]
        for half in range(2):
            at = slice(128 * half, 128 * half + 128)
            source = jnp.where(poc_ref[half] == patch, SOURCE_AMPS, 0.0)
            do_ref[k, :, at] = (source - total[half]) + db_s[k, :, at]
        do_ref[k, 0:1, :] -= nn_ref[k : k + 1, :]
        do_ref[k, CR - 1 : CR, :] -= sn_ref[k : k + 1, :]

    for k in range(K):
        field_step(k)


def owner_body(msg_ref, out_ref, ids_s):
    me = lax.axis_index("row") * lax.axis_size("col") + lax.axis_index("col")
    values = stack2(
        msg_ref[pl.ds(0, DEVICES, stride=3), :].T, msg_ref[pl.ds(1, DEVICES, stride=3), :].T
    )
    ids_s[...] = msg_ref[pl.ds(2, DEVICES, stride=3), :].T
    ids = ids_s[pl.ds(pl.multiple_of(jnp.bitwise_and(me, 7) * 16, 16), 16), :]
    patch = iota((128, 256), 0)
    total = jnp.zeros((64, 128), F32)
    for e in range(0, SLOTS, 2):
        pair = jnp.concatenate(
            [values[16 * e : 16 * e + 16], values[16 * e + 16 : 16 * e + 32]], axis=1
        )
        at = jnp.concatenate([ids[e : e + 1], ids[e + 1 : e + 2]], axis=1).astype(jnp.int32)
        group = jnp.broadcast_to(at >> 7, (16, 256))
        spread = jnp.concatenate([jnp.where(group == g, pair, 0.0) for g in range(4)], axis=0)
        high, low = split(spread)
        place = one_hot(patch == (at & 127))
        total = total + (dot(high, place, 1, 1) + dot(low, place, 1, 1))
    for g in range(4):
        out_ref[:, 128 * g : 128 * g + 128] = total[16 * g : 16 * g + 16]


def neighbours(value, axis, which):
    count = lax.axis_size(axis)
    starts = range(which, count - 1, 2)
    return lax.ppermute(value, axis, [(i, i + 1) for i in starts] + [(i + 1, i) for i in starts])


def on_device(iterate, direction, conductance, ground, local_patch, tile_patches, sources):
    vmem = pl.BlockSpec(memory_space=pltpu.VMEM)
    smem = pl.BlockSpec(memory_space=pltpu.SMEM)
    hbm = pl.BlockSpec(memory_space=pltpu.HBM)
    field = pltpu.VMEM((K, CR, CC), F32)
    plane = pltpu.VMEM((CR, CC), F32)

    first, second, columns, x_held, d_held, patch_of_cell, slots, ids, ee, es, leak = call(
        front_body,
        (
            pltpu.VMEM((40, CC), F32),
            pltpu.VMEM((40, CC), F32),
            pltpu.VMEM((CR, 128), F32),
            field,
            field,
            pltpu.VMEM((2, CR, 128), jnp.int32),
            pltpu.VMEM((8, CC), jnp.int32),
            pltpu.VMEM((DEVICES, 128), F32),
            plane,
            plane,
            plane,
        ),
        scratch=[
            plane,
            pltpu.VMEM((CR, CC), jnp.int32),
            pltpu.VMEM((CR, CC), jnp.int32),
            pltpu.VMEM((1, 1, 2048), jnp.int32),
            pltpu.VMEM((2, CR, 128), jnp.int32),
            pltpu.SemaphoreType.DMA((12,)),
        ],
        specs=[hbm] * 6,
        places=(vmem,) * 11,
        moved=8_000_000,
    )(*[pltpu.with_memory_space_constraint(a, pltpu.HBM) for a in (iterate, direction, conductance, ground, local_patch, tile_patches)])
    far_second = neighbours(second, "row", 1)
    cols_second = neighbours(columns, "col", 1)
    far_first = neighbours(first, "row", 0)
    cols_first = neighbours(columns, "col", 0)

    image, part = call(
        fields_body,
        (pltpu.VMEM((K, CR, CC), F32), pltpu.VMEM((K, CR, CC), F32)),
        specs=[smem] + [vmem] * 6,
        places=(vmem, vmem),
        moved=12_000_000,
    )(sources, x_held, d_held, ee, es, leak, patch_of_cell)

    gram, nf, sf, cf = call(
        products_body,
        (f32(8 * DEVICES, 128), f32(32, CC), f32(32, CC), f32(CR, 128)),
        scratch=[pltpu.VMEM((2, K, 8, CC), F32), pltpu.VMEM((2, K, 8, CC), F32)],
        specs=[vmem] * 10,
        moved=20_000_000,
    )(
        d_held, image, part,
        first, second, columns, far_second, cols_second, far_first, cols_first,
    )
    gram = lax.all_to_all(gram, AXES, 0, 0, tiled=True)

    new_iterate, message, system, nn, sn, cn = call(
        iterate_body,
        (f32(K, CR, CC), f32(DEVICES * 3, 128), f32(16, 128), f32(16, CC), f32(16, CC), f32(CR, 128)),
        scratch=[
            field,
            field,
            pltpu.VMEM((128, 128), F32),
            pltpu.SemaphoreType.DMA(()),
        ],
        specs=[vmem] * 10,
        places=(hbm,) + (vmem,) * 5,
        moved=20_000_000,
    )(gram, x_held, d_held, ee, es, slots, ids, nf, sf, cf)
    received = lax.all_to_all(message.reshape(DEVICES, 1, 384), AXES, 0, 0, tiled=True)
    new_direction = call(
        direction_body,
        f32(K, CR, CC),
        scratch=[field],
        specs=[smem] + [vmem] * 10,
        moved=20_000_000,
    )(sources, new_iterate, direction, ee, es, leak, patch_of_cell, system, nn, sn, cn)
    migration = call(
        owner_body,
        f32(K, PATCH_DEV),
        scratch=[pltpu.VMEM((128, 128), F32)],
        specs=[vmem],
        moved=1_000_000,
    )(received.reshape(DEVICES * 3, 128))
    return new_iterate, new_direction, migration


def solution(mesh):
    in_specs = (
        P(None, "row", "col"),
        P(None, "row", "col"),
        P("row", "col"),
        P("row", "col"),
        P("row", "col"),
        P("row", "col", None),
        P(),
    )
    out_specs = (P(None, "row", "col"), P(None, "row", "col"), P(None, ("row", "col")))
    return jax.shard_map(
        on_device, mesh=mesh, in_specs=in_specs, out_specs=out_specs, check_vma=False
    )
```
